32 devices in a mesh: pool: 8 (over y, x, core), fft: 4 (over z).
Axes of the slice: x: 2, y: 2, z: 4, core: 2. Of those that a mesh axis runs over, the one named last changes fastest.
Arguments:
- orbitals: bfloat16 [2, 8, 64, 8192], P(None, 'pool', None, 'fft'), may hold values from -12 to 12
- box_index: int32 [8192], P('fft'), may hold values from 0 to 262143, as said below
- partner_pool: int32 [8], replicated, may hold values from 0 to 7, each once
- potential: float32 [64, 64, 128], replicated, may hold values from -9 to 9
Outputs:
- response: bfloat16 [2, 8, 64, 8192], P(None, 'pool', None, 'fft')
- coupling: float32 [2, 8, 64, 64], P(None, 'pool')
The draws below stay inside these ranges and needn't reach their ends.
Inputs may be any that keep to these rules, and one draw needn't show every extreme that they name: `box_index`: entries are distinct. The 2048 entries of index d of fft lie on exactly 64 columns x * 64 + y of the box (a column is the 64 points of one x and y), and no column holds entries of two indices of fft. `partner_pool`: A permutation of the k-points.
All inputs are finite; a program needn't handle non-finite values.
Results may differ from the reference program's by a relative error of at most 0.02.
Values may be sent and summed in bfloat16 or wider, within the bound.
No kernel may reach another device: no remote copies, remote signals or barrier semaphores. Data moves between devices by JAX's collectives and lax.ppermute only.
A program may use at most 192 MiB of HBM per device.

```python
import jax
import jax.numpy as jnp
from jax import lax

NB = 64
BOX = 64
NPW_DEV = 2048
K = 8
NPW = 8192
STICK_DEV = 64


def centred(values):
    return (values + BOX // 2) % BOX - BOX // 2


def draw_box_index(key, part):
    devices = NPW // NPW_DEV
    total = STICK_DEV * devices
    plane = BOX * BOX
    base = jax.random.fold_in(key, 11)
    columns = jnp.arange(plane, dtype=jnp.int32)
    col_x = centred(columns // BOX)
    col_y = centred(columns % BOX)
    radial = col_x * col_x + col_y * col_y
    along = col_x + col_y
    across = col_x - col_y
    sheared = along * along + 64 * across * across
    col_tie = jax.random.permutation(jax.random.fold_in(base, 1), plane).astype(jnp.int32)
    order = jnp.argsort(sheared * plane + col_tie, stable=True).astype(jnp.int32)
    sticks = order[:total]
    ranks = jnp.arange(total, dtype=jnp.int32)
    rounds = ranks // devices
    places = ranks % devices
    owner = jnp.where(rounds % 2 == 0, places, devices - 1 - places)
    grouped = sticks[jnp.argsort(owner * total + ranks, stable=True)].reshape(devices, STICK_DEV)
    depth = jnp.arange(BOX, dtype=jnp.int32)
    depth_g = centred(depth)
    cell_count = STICK_DEV * BOX
    ceiling = 3 * (BOX // 2) * (BOX // 2) + 1

    def shard(slot, mine):
        rad = radial[mine][:, None] + (depth_g * depth_g)[None, :]
        cells = mine[:, None] * BOX + depth[None, :]
        off_centre = jnp.where(depth_g != 0, 1, 0).astype(jnp.int32)[None, :]
        cell_tie = jax.random.permutation(jax.random.fold_in(base, 2 * slot + 2), cell_count).astype(jnp.int32)
        score = (off_centre * ceiling + rad).reshape(-1) * cell_count + cell_tie
        picked = jnp.argsort(score, stable=True)[:NPW_DEV]
        chosen = cells.reshape(-1)[picked]
        return jax.random.permutation(jax.random.fold_in(base, 2 * slot + 3), chosen)
    slots = jnp.arange(devices, dtype=jnp.int32)
    return jax.vmap(shard)(slots, grouped).reshape(-1).astype(jnp.int32)


def shard_levels(stream_key, dims, cuts, smallest, high):
    factor_of, own = 1.0, jax.random.fold_in(stream_key, 6)
    for dim, blocks in cuts:
        heights = jnp.exp(jax.random.uniform(jax.random.fold_in(own, dim), (blocks,), jnp.float32, smallest / len(cuts), high / len(cuts)))
        factor_of = factor_of * jnp.repeat(heights, dims[dim] // blocks).reshape([-1 if axis == dim else 1 for axis in range(len(dims))])
    return factor_of


def bell_draw(rng, dims, width, bound, split=(), held_as=jnp.bfloat16):
    values = jax.random.normal(rng, dims, jnp.float32) * width
    if len(split) > 0:
        values = shard_levels(rng, dims, split, -0.22, 0.18) * values
    return jnp.clip(values, min=-bound, max=bound).astype(held_as)


def setup_inputs(seed: int = 0) -> dict:
    seeds = jax.random.split(jax.random.key(seed), 5)
    return {
        "orbitals": bell_draw(seeds[0], (2, K, NB, NPW), 2.0, 12.0, ((1, 8), (3, 4))),
        "box_index": draw_box_index(jax.random.fold_in(seeds[4], 71), 0),
        "partner_pool": jax.random.permutation(seeds[2], K).astype(jnp.int32),
        "potential": bell_draw(seeds[3], (BOX, BOX, 2 * BOX), 1.5, 9.0, (), jnp.float32),
    }


def tables(side, signum):
    points = jnp.arange(side, dtype=jnp.int32)
    products = points[:, None] * points[None, :] % side
    angles = 2.0 * jnp.pi / side * products.astype(jnp.float32)
    scaling = 1.0 / jnp.sqrt(jnp.float32(side))
    cosine = jnp.cos(angles) * scaling
    sines = jnp.sin(angles) * scaling
    rows_real = jnp.stack([cosine, -signum * sines], axis=1)
    rows_imag = jnp.stack([signum * sines, cosine], axis=1)
    return jnp.stack([rows_real, rows_imag], axis=0).astype(jnp.bfloat16)

def transform(grid_rows, weights, axis_name):
    bands, parts, span, flat = grid_rows.shape
    side = weights.shape[1]
    lifted = grid_rows.astype(jnp.float32)
    table = weights.astype(jnp.float32)
    high = lax.Precision.HIGHEST
    if axis_name == 'first':
        result = jnp.einsum('tasb,nsbq->ntaq', table, lifted, precision=high)
    elif axis_name == 'second':
        view = lifted.reshape(bands, parts, span, side, side)
        result = jnp.einsum('tasb,nsxbz->ntxaz', table, view, precision=high).reshape(bands, parts, span, flat)
    else:
        view = lifted.reshape(bands, parts, span, side, side)
        result = jnp.einsum('tasb,nsxyb->ntxya', table, view, precision=high).reshape(bands, parts, span, flat)
    return result.astype(jnp.bfloat16)

def modulate(grid_rows, potential):
    side = potential.shape[0]
    field = potential.reshape(side, side, 2, side)
    field = jnp.transpose(field, (2, 3, 1, 0)).reshape(2, side, side * side)
    lifted = grid_rows.astype(jnp.float32)
    real_part = field[0][None] * lifted[:, 0] - field[1][None] * lifted[:, 1]
    imag_part = field[0][None] * lifted[:, 1] + field[1][None] * lifted[:, 0]
    return jnp.stack([real_part, imag_part], axis=1).astype(jnp.bfloat16)

def reference(orbitals, box_index, partner_pool, potential):
    inverse_w = tables(BOX, 1.0)
    forward_w = tables(BOX, -1.0)

    def respond(coeffs):
        rows = jnp.moveaxis(coeffs, 1, 0)
        grid = jnp.zeros((NB, 2, BOX * BOX * BOX), jnp.bfloat16).at[:, :, box_index].set(rows)
        grid = grid.reshape(NB, 2, BOX, BOX * BOX)
        grid = transform(grid, inverse_w, 'third')
        grid = transform(grid, inverse_w, 'second')
        grid = transform(grid, inverse_w, 'first')
        grid = modulate(grid, potential)
        grid = transform(grid, forward_w, 'first')
        grid = transform(grid, forward_w, 'second')
        grid = transform(grid, forward_w, 'third')
        picked = grid.reshape(NB, 2, BOX * BOX * BOX)[:, :, box_index]
        return jnp.moveaxis(picked, 0, 1)
    stacked = lax.map(respond, jnp.moveaxis(orbitals, 1, 0))
    response = jnp.moveaxis(stacked, 0, 1)
    partner = jnp.take(orbitals, partner_pool, axis=1).astype(jnp.float32)
    lifted = response.astype(jnp.float32)
    rotated = jnp.stack([lifted[1], -lifted[0]])
    high = lax.Precision.HIGHEST
    real_part = jnp.einsum('skmp,sknp->kmn', partner, lifted, precision=high)
    imag_part = jnp.einsum('skmp,sknp->kmn', partner, rotated, precision=high)
    coupling = jnp.stack([real_part, imag_part]) / jnp.sqrt(jnp.float32(NPW))
    return (response, coupling)
```

```python
import functools

import jax
import jax.numpy as jnp
import ml_dtypes
import numpy as np
from jax import lax
from jax.experimental import pallas as pl
from jax.experimental.pallas import tpu as pltpu
from jax.sharding import PartitionSpec as P

STICK_DEV = 64
LANES = 128
BF16 = jnp.bfloat16
F32 = jnp.float32
VMEM_LIMIT = 48 * 1024 * 1024


def cos_sin(side):
    points = np.arange(side)
    angles = (2.0 * np.pi / side) * (points[:, None] * points[None, :] % side)
    scaling = 1.0 / np.sqrt(side)
    cosine = (np.cos(angles) * scaling).astype(ml_dtypes.bfloat16)
    sine = (np.sin(angles) * scaling).astype(ml_dtypes.bfloat16)
    return cosine, sine


def dot(a, b):
    return jnp.dot(a, b, preferred_element_type=F32)


def dot_nt(a, b):
    return lax.dot_general(a, b, (((1,), (1,)), ((), ())), preferred_element_type=F32)


def one_hot(row, count):
    places = lax.broadcasted_iota(jnp.int32, (count, row.shape[1]), 0)
    return jnp.where(places == row, 1.0, 0.0).astype(BF16)


def triangles(side):
    rows = lax.broadcasted_iota(jnp.int32, (side, side), 0)
    cols = lax.broadcasted_iota(jnp.int32, (side, side), 1)
    upper = jnp.where(rows < cols, 1.0, 0.0).astype(BF16)
    lower = jnp.where(rows > cols, 1.0, 0.0).astype(BF16)
    return upper, lower, jnp.ones((side, side), BF16)


def prefix(occupied, tri):
    upper, lower, ones = tri
    in_rows = dot(occupied, ones).astype(BF16)
    return dot(occupied, upper) + dot(lower, in_rows)


def locate(idx, side):
    bits = side.bit_length() - 1
    tri = triangles(side)
    xh = one_hot(idx >> (2 * bits), side)
    yh = one_hot((idx >> bits) & (side - 1), side)
    zh = one_hot(idx & (side - 1), side)
    columns = jnp.minimum(dot_nt(xh, yh), 1.0).astype(BF16)
    slots = prefix(columns, tri).astype(BF16)
    slot = jnp.sum(xh.astype(F32) * dot(slots, yh), axis=0, keepdims=True)
    ch = one_hot(slot.astype(jnp.int32), STICK_DEV)
    cells = dot_nt(zh, ch)
    ranks = prefix(cells.astype(BF16), tri)
    high = jnp.floor(ranks * (1.0 / side))
    low = ranks - high * side
    looked = dot(high.astype(BF16), ch) * side + dot(low.astype(BF16), ch)
    rank = jnp.sum(zh.astype(F32) * looked, axis=0, keepdims=True)
    return xh, yh, zh, ch, slot, cells, ranks, rank.astype(jnp.int32)


def sort_kernel(side, groups, idx_ref, x_ref, out_ref, rank_ref):
    rank = locate(idx_ref[...], side)[-1]
    rank_ref[...] = rank
    waves = rank.shape[1]
    rows = x_ref.shape[0]
    bands = rows // 2
    share = bands // groups
    low = one_hot(rank & 255, 256)
    for part in range(waves // 256):
        mask = jnp.where((rank >> 8) == part, 1.0, 0.0).astype(BF16)
        piece = dot_nt(x_ref[...] * mask, low)
        for q in range(groups):
            re = piece[q * share : (q + 1) * share]
            im = piece[bands + q * share : bands + (q + 1) * share]
            both = jnp.concatenate([re, im], axis=0).astype(BF16)
            out_ref[q, :, part * 256 : (part + 1) * 256] = both


def prep_kernel(
    side, chunks, idx_ref, pot_ref, cs_ref, cyr_ref, syr_ref,
    tab_ref, field_ref, spot_ref, col_ref, dep_ref,
):
    groups = idx_ref.shape[0]
    waves = idx_ref.shape[1]
    tiles = waves // LANES
    half = side // 2
    for d in range(groups):
        xh, yh, zh, ch, slot, cells, ranks, rank = locate(idx_ref[d : d + 1, :], side)
        at_x = jnp.minimum(dot_nt(ch, xh), 1.0).astype(BF16)
        at_y = jnp.minimum(dot_nt(ch, yh), 1.0).astype(BF16)
        both = dot(at_x, cs_ref[...])
        cx, sx = both[:, :LANES], both[:, LANES:]
        rows = slice(d * STICK_DEV, (d + 1) * STICK_DEV)
        for k in range(chunks):
            cy = dot(at_y, cyr_ref[:, k * LANES : (k + 1) * LANES])
            sy = dot(at_y, syr_ref[:, k * LANES : (k + 1) * LANES])
            base = 2 * k * LANES
            tab_ref[rows, base : base + LANES] = (cy * cx - sy * sx).astype(BF16)
            tab_ref[rows, base + LANES : base + 2 * LANES] = (cy * sx + sy * cx).astype(BF16)
        spot = ranks.astype(jnp.int32)
        spot_ref[d] = jnp.where(cells > 0.5, spot, spot - 4096)
        low = one_hot(rank & (LANES - 1), LANES)
        high = one_hot(rank >> 7, tiles)
        col = dot_nt(high * slot.astype(BF16), low).astype(jnp.int32)
        depth = jnp.sum(
            zh.astype(F32) * lax.broadcasted_iota(jnp.int32, zh.shape, 0).astype(F32),
            axis=0, keepdims=True,
        )
        dep = dot_nt(high * depth.astype(BF16), low).astype(jnp.int32)
        col_ref[d * tiles : (d + 1) * tiles, :] = col + (d % 2) * STICK_DEV
        dep_ref[d * tiles : (d + 1) * tiles, :] = dep
    lane = lax.broadcasted_iota(jnp.int32, (side, LANES), 1)
    first = lane < side
    flipped = (lane & side) + ((side - (lane & (side - 1))) & (side - 1))

    def pair(row_a, row_b):
        p = jnp.where(first, row_a, pltpu.roll(row_b, side, 1))
        q = jnp.where(first, pltpu.roll(row_a, side, 1), row_b)
        return p, q

    def plane(y):
        return pot_ref[pl.ds(y, side, stride=side), :]

    def mirror(y):
        if y == 0 or y >= half:
            return jnp.zeros((side, LANES), F32)
        return jnp.take_along_axis(plane(side - y), flipped, axis=1)

    zero = jnp.zeros((side, LANES), F32)
    for k in range(chunks):
        ya, yb = 2 * k, 2 * k + 1
        p, q = pair(plane(ya), plane(yb) if yb <= half else zero)
        field_ref[0, :, k * LANES : (k + 1) * LANES] = p
        field_ref[1, :, k * LANES : (k + 1) * LANES] = q
        p, q = pair(mirror(ya), mirror(yb))
        field_ref[2, :, k * LANES : (k + 1) * LANES] = p
        field_ref[3, :, k * LANES : (k + 1) * LANES] = q


def box_kernel(
    side, chunks, team, x_ref, tab_ref, field_ref, spot_ref, col_ref, dep_ref, start_s, dep_s,
    wz_ref, out_ref, xf, grid, t_scr, l_scr,
):
    groups, rows, waves = x_ref.shape
    bands = rows // 2
    tiles = waves // LANES
    blocks = rows // 8
    span = 2 * side
    xf[...] = x_ref[...].astype(F32)
    upper_half = lax.broadcasted_iota(jnp.int32, (1, LANES), 1) >= STICK_DEV

    def expand(z, carry):
        for dp in range(groups // 2):
            spot = jnp.concatenate(
                [spot_ref[2 * dp, pl.ds(z, 1), :], spot_ref[2 * dp + 1, pl.ds(z, 1), :]], axis=1
            )
            at = jnp.broadcast_to(spot & (LANES - 1), (8, LANES))
            tile = spot >> 7
            sources = []
            for dd in range(2):
                d = 2 * dp + dd
                t0 = (start_s[d, z, 0] & 4095) >> 7
                mine = upper_half if dd else jnp.logical_not(upper_half)
                for step in range(2):
                    chosen = jnp.broadcast_to(mine & (tile == t0 + step), (8, LANES))
                    where = jnp.minimum(t0 + step, tiles - 1)
                    sources.append((d, pl.multiple_of(where * LANES, LANES), chosen))
            for block in range(blocks):
                value = jnp.zeros((8, LANES), F32)
                for d, begin, chosen in sources:
                    source = xf[d, block * 8 : (block + 1) * 8, pl.ds(begin, LANES)]
                    value = jnp.where(chosen, jnp.take_along_axis(source, at, axis=1), value)
                grid[dp, pl.ds(block * 8 * side + z, 8, stride=side), :] = value
        return carry

    lax.fori_loop(0, side, expand, 0)

    def depth_in(b, carry):
        both = jnp.concatenate(
            [
                jnp.concatenate(
                    [grid[n, pl.ds(b * side, side), :], grid[n, pl.ds((bands + b) * side, side), :]],
                    axis=0,
                )
                for n in range(groups // 2)
            ],
            axis=1,
        ).astype(BF16)
        t_scr[pl.ds(b * span, span), :] = dot(wz_ref[0], both).astype(BF16)
        return carry

    lax.fori_loop(0, bands, depth_in, 0)

    def planes(g, carry):
        rows_g = pl.ds(g * team * span, team * span)
        sticks = t_scr[rows_g, :]
        for k in range(chunks):
            here = slice(k * LANES, (k + 1) * LANES)
            wide = slice(2 * k * LANES, 2 * (k + 1) * LANES)
            ab = dot(sticks, tab_ref[:, wide])
            p, q = field_ref[0, :, here], field_ref[1, :, here]
            p2, q2 = field_ref[2, :, here], field_ref[3, :, here]
            for b in range(team):
                u, x = ab[b * span : b * span + side, :LANES], ab[b * span : b * span + side, LANES:]
                w, v = ab[b * span + side : (b + 1) * span, :LANES], ab[b * span + side : (b + 1) * span, LANES:]
                pr, pi, mr, mi = u - v, w + x, u + v, w - x
                ar, ai = p * pr - q * pi, p * pi + q * pr
                br, bi = p2 * mr - q2 * mi, p2 * mi + q2 * mr
                even = jnp.concatenate([ar + br, ai + bi], axis=0).astype(BF16)
                odd = jnp.concatenate([ai - bi, br - ar], axis=0).astype(BF16)
                l_scr[b * span : (b + 1) * span, wide] = jnp.concatenate([even, odd], axis=1)
        back = dot_nt(l_scr[...], tab_ref[...]).astype(BF16)
        for b in range(team):
            done = dot(wz_ref[1], back[b * span : (b + 1) * span])
            for n in range(groups // 2):
                here = slice(n * LANES, (n + 1) * LANES)
                grid[n, pl.ds((g * team + b) * side, side), :] = done[:side, here]
                grid[n, pl.ds((bands + g * team + b) * side, side), :] = done[side:, here]
        return carry

    lax.fori_loop(0, bands // team, planes, 0)

    for d in range(groups):

        def collect(t, carry, d=d):
            row = d * tiles + t
            at = jnp.broadcast_to(col_ref[pl.ds(row, 1), :], (8, LANES))
            depth = jnp.broadcast_to(dep_ref[pl.ds(row, 1), :], (8, LANES))

            def level(z, values):
                mask = depth == z
                new = []
                for block in range(blocks):
                    source = grid[d // 2, pl.ds(block * 8 * side + z, 8, stride=side), :]
                    new.append(jnp.where(mask, jnp.take_along_axis(source, at, axis=1), values[block]))
                return tuple(new)

            values = lax.fori_loop(
                dep_s[row, 0], dep_s[row, LANES - 1] + 1, level,
                tuple(jnp.zeros((8, LANES), F32) for _ in range(blocks)),
            )
            out_ref[d, :, pl.ds(pl.multiple_of(t * LANES, LANES), LANES)] = jnp.concatenate(
                values, axis=0
            ).astype(BF16)
            return carry

        lax.fori_loop(0, tiles, collect, 0)


def finish_kernel(target_ref, y_ref, rank_ref, partner_ref, out_ref, g_ref):
    rank = rank_ref[...]
    waves = rank.shape[1]
    groups, rows, _ = y_ref.shape
    share = rows // 2
    low = one_hot(rank & 255, 256)
    total = None
    for part in range(waves // 256):
        pieces = [y_ref[q, :, part * 256 : (part + 1) * 256].astype(F32) for q in range(groups)]
        piece = jnp.concatenate(
            [piece[:share] for piece in pieces] + [piece[share:] for piece in pieces], axis=0
        ).astype(BF16)
        value = dot(piece, low)
        value = jnp.where((rank >> 8) == part, value, 0.0)
        total = value if total is None else total + value
    response = total.astype(BF16)
    out_ref[...] = response
    products = dot_nt(partner_ref[0], response)
    half = products.shape[0] // 2
    g_ref[0] = products[:half, :half] + products[half:, half:]
    g_ref[1] = products[:half, half:] - products[half:, :half]


def whole(memory=pltpu.VMEM):
    return pl.BlockSpec(memory_space=memory)


def params():
    return pltpu.CompilerParams(vmem_limit_bytes=VMEM_LIMIT)


def shards(orbitals, box_index, partner_pool, potential):
    fft_count = lax.axis_size("fft")
    side = potential.shape[0]
    bands = orbitals.shape[2]
    waves = orbitals.shape[3]
    share = bands // fft_count
    columns = STICK_DEV * fft_count
    chunks = (side // 2 + 1 + 1) // 2
    tiles = waves // LANES
    coeffs = orbitals.reshape(2 * bands, waves)

    cosine, sine = cos_sin(side)
    cs = jnp.asarray(np.concatenate([cosine, cosine, sine, sine], axis=1))
    half_points = (np.arange(2 * chunks * side) // side) % side
    cyr = jnp.asarray(cosine[:, half_points])
    syr = jnp.asarray(sine[:, half_points])
    inward = np.block([[cosine, -sine], [sine, cosine]])
    outward = np.block([[cosine, sine], [-sine, cosine]])
    wz = jnp.asarray(np.stack([inward, outward]))

    gathered = lax.all_gather(coeffs, "pool", axis=0)
    all_index = lax.all_gather(box_index, "fft", axis=0)

    ordered, rank = pl.pallas_call(
        functools.partial(sort_kernel, side, fft_count),
        out_shape=(
            jax.ShapeDtypeStruct((fft_count, 2 * share, waves), BF16),
            jax.ShapeDtypeStruct((1, waves), jnp.int32),
        ),
        in_specs=[whole(), whole()],
        out_specs=(whole(), whole()),
        compiler_params=params(),
        name="sort_waves",
    )(box_index.reshape(1, waves), coeffs)
    moved = lax.all_to_all(ordered, "fft", split_axis=0, concat_axis=0, tiled=True)

    tab, field, spot, col, dep = pl.pallas_call(
        functools.partial(prep_kernel, side, chunks),
        out_shape=(
            jax.ShapeDtypeStruct((columns, 2 * chunks * LANES), BF16),
            jax.ShapeDtypeStruct((4, side, chunks * LANES), F32),
            jax.ShapeDtypeStruct((fft_count, side, STICK_DEV), jnp.int32),
            jax.ShapeDtypeStruct((fft_count * tiles, LANES), jnp.int32),
            jax.ShapeDtypeStruct((fft_count * tiles, LANES), jnp.int32),
        ),
        in_specs=[whole()] * 5,
        out_specs=(whole(),) * 5,
        compiler_params=params(),
        cost_estimate=pl.CostEstimate(flops=10**9, bytes_accessed=10**7, transcendentals=0),
        name="prepare",
    )(all_index, potential.reshape(side * side, 2 * side), cs, cyr, syr)

    team = min(4, share)
    back = pl.pallas_call(
        functools.partial(box_kernel, side, chunks, team),
        out_shape=jax.ShapeDtypeStruct((fft_count, 2 * share, waves), BF16),
        in_specs=[whole()] * 6 + [whole(pltpu.SMEM)] * 2 + [whole()],
        out_specs=whole(),
        scratch_shapes=[
            pltpu.VMEM((fft_count, 2 * share, waves), F32),
            pltpu.VMEM((columns // LANES, 2 * share * side, LANES), F32),
            pltpu.VMEM((2 * share * side, columns), BF16),
            pltpu.VMEM((team * 2 * side, 2 * chunks * LANES), BF16),
        ],
        compiler_params=params(),
        cost_estimate=pl.CostEstimate(flops=10**10, bytes_accessed=10**7, transcendentals=0),
        name="box_work",
    )(moved, tab, field, spot, col, dep, spot[:, :, :1], dep, wz)
    returned = lax.all_to_all(back, "fft", split_axis=0, concat_axis=0, tiled=True)

    target = partner_pool[lax.axis_index("pool")].reshape(1)
    response, sums = pl.pallas_call(
        finish_kernel,
        grid_spec=pltpu.PrefetchScalarGridSpec(
            num_scalar_prefetch=1,
            grid=(1,),
            in_specs=[
                pl.BlockSpec((fft_count, 2 * share, waves), lambda i, t: (0, 0, 0)),
                pl.BlockSpec((1, waves), lambda i, t: (0, 0)),
                pl.BlockSpec((1, 2 * bands, waves), lambda i, t: (t[0], 0, 0)),
            ],
            out_specs=[
                pl.BlockSpec((2 * bands, waves), lambda i, t: (0, 0)),
                pl.BlockSpec((2, bands, bands), lambda i, t: (0, 0, 0)),
            ],
        ),
        out_shape=(
            jax.ShapeDtypeStruct((2 * bands, waves), BF16),
            jax.ShapeDtypeStruct((2, bands, bands), F32),
        ),
        compiler_params=params(),
        name="finish",
    )(target, returned, rank, gathered)
    summed = lax.psum(sums.astype(BF16), "fft").astype(F32)
    coupling = (summed / jnp.sqrt(jnp.float32(waves * fft_count)))[:, None]
    return response.reshape(2, 1, bands, waves), coupling


def solution(mesh):
    placed = (P(None, "pool", None, "fft"), P("fft"), P(), P())
    return jax.shard_map(
        shards,
        mesh=mesh,
        in_specs=placed,
        out_specs=(P(None, "pool", None, "fft"), P(None, "pool", None, None)),
        check_vma=False,
    )
```

```python
import functools

import jax
import jax.numpy as jnp
import ml_dtypes
import numpy as np
from jax import lax
from jax.experimental import pallas as pl
from jax.experimental.pallas import tpu as pltpu
from jax.sharding import PartitionSpec as P

STICK_DEV = 64
LANES = 128
UNROLL = 4
BF16 = jnp.bfloat16
F32 = jnp.float32
VMEM_LIMIT = 48 * 1024 * 1024


def cos_sin(side):
    points = np.arange(side)
    angles = (2.0 * np.pi / side) * (points[:, None] * points[None, :] % side)
    scaling = 1.0 / np.sqrt(side)
    cosine = (np.cos(angles) * scaling).astype(ml_dtypes.bfloat16)
    sine = (np.sin(angles) * scaling).astype(ml_dtypes.bfloat16)
    return cosine, sine


def dot(a, b):
    return jnp.dot(a, b, preferred_element_type=F32)


def dot_nt(a, b):
    return lax.dot_general(a, b, (((1,), (1,)), ((), ())), preferred_element_type=F32)


def one_hot(row, count):
    places = lax.broadcasted_iota(jnp.int32, (count, row.shape[1]), 0)
    return jnp.where(places == row, 1.0, 0.0).astype(BF16)


def triangles(side):
    rows = lax.broadcasted_iota(jnp.int32, (side, side), 0)
    cols = lax.broadcasted_iota(jnp.int32, (side, side), 1)
    upper = jnp.where(rows < cols, 1.0, 0.0).astype(BF16)
    lower = jnp.where(rows > cols, 1.0, 0.0).astype(BF16)
    return upper, lower, jnp.ones((side, side), BF16)


def prefix(occupied, tri):
    upper, lower, ones = tri
    in_rows = dot(occupied, ones).astype(BF16)
    return dot(occupied, upper) + dot(lower, in_rows)


def locate(idx, side):
    bits = side.bit_length() - 1
    tri = triangles(side)
    xh = one_hot(idx >> (2 * bits), side)
    yh = one_hot((idx >> bits) & (side - 1), side)
    zh = one_hot(idx & (side - 1), side)
    columns = jnp.minimum(dot_nt(xh, yh), 1.0).astype(BF16)
    slots = prefix(columns, tri).astype(BF16)
    slot = jnp.sum(xh.astype(F32) * dot(slots, yh), axis=0, keepdims=True)
    ch = one_hot(slot.astype(jnp.int32), STICK_DEV)
    cells = dot_nt(zh, ch)
    ranks = prefix(cells.astype(BF16), tri)
    high = jnp.floor(ranks * (1.0 / side))
    low = ranks - high * side
    looked = dot(high.astype(BF16), ch) * side + dot(low.astype(BF16), ch)
    rank = jnp.sum(zh.astype(F32) * looked, axis=0, keepdims=True)
    return xh, yh, ch, cells, ranks, rank.astype(jnp.int32)


def sort_kernel(side, groups, idx_ref, x_ref, out_ref, rank_ref):
    rank = locate(idx_ref[...], side)[-1]
    rank_ref[...] = rank
    waves = rank.shape[1]
    rows = x_ref.shape[0]
    bands = rows // 2
    share = bands // groups
    low = one_hot(rank & 255, 256)
    for part in range(waves // 256):
        mask = jnp.where((rank >> 8) == part, 1.0, 0.0).astype(BF16)
        piece = dot_nt(x_ref[...] * mask, low)
        for q in range(groups):
            re = piece[q * share : (q + 1) * share]
            im = piece[bands + q * share : bands + (q + 1) * share]
            both = jnp.concatenate([re, im], axis=0).astype(BF16)
            out_ref[q, :, part * 256 : (part + 1) * 256] = both


def prep_kernel(
    side, chunks, groups, me_ref, *refs,
):
    idx_refs, refs = refs[:groups], refs[groups:]
    pot_ref, cs_ref, cyr_ref, syr_ref, tab_ref, field_ref, spot_ref, start_ref = refs
    half = side // 2
    me = me_ref[0]
    for shift in range(groups):
        d = lax.rem(me + groups - shift, groups)
        xh, yh, ch, cells, ranks = locate(idx_refs[shift][...], side)[:5]
        at_x = jnp.minimum(dot_nt(ch, xh), 1.0).astype(BF16)
        at_y = jnp.minimum(dot_nt(ch, yh), 1.0).astype(BF16)
        both = dot(at_x, cs_ref[...])
        cx, sx = both[:, :LANES], both[:, LANES:]
        rows = pl.ds(pl.multiple_of(d * STICK_DEV, STICK_DEV), STICK_DEV)
        for k in range(chunks):
            cy = dot(at_y, cyr_ref[:, k * LANES : (k + 1) * LANES])
            sy = dot(at_y, syr_ref[:, k * LANES : (k + 1) * LANES])
            base = 2 * k * LANES
            tab_ref[rows, base : base + LANES] = (cy * cx - sy * sx).astype(BF16)
            tab_ref[rows, base + LANES : base + 2 * LANES] = (cy * sx + sy * cx).astype(BF16)
        block = float(STICK_DEV)
        begins = jnp.floor(ranks[:, :1] * (1.0 / block))
        spot = jnp.where(cells > 0.5, ranks - begins * block, -1.0)
        spot_ref[d] = jnp.concatenate([spot, spot], axis=1)
        level = dot_nt(jnp.ones((8, STICK_DEV), BF16), cells.astype(BF16))
        before = dot(level.astype(BF16), triangles(side)[0])
        start_ref[pl.ds(d, 1), :] = (before[:1] * (1.0 / block)).astype(jnp.int32)
    lane = lax.broadcasted_iota(jnp.int32, (side, LANES), 1)
    first = lane < side
    flipped = (lane & side) + ((side - (lane & (side - 1))) & (side - 1))

    def pair(row_a, row_b):
        p = jnp.where(first, row_a, pltpu.roll(row_b, side, 1))
        q = jnp.where(first, pltpu.roll(row_a, side, 1), row_b)
        return p, q

    def plane(y):
        return pot_ref[pl.ds(y, side, stride=side), :]

    def mirror(y):
        if y == 0 or y >= half:
            return jnp.zeros((side, LANES), F32)
        return jnp.take_along_axis(plane(side - y), flipped, axis=1)

    zero = jnp.zeros((side, LANES), F32)
    for k in range(chunks):
        ya, yb = 2 * k, 2 * k + 1
        p, q = pair(plane(ya), plane(yb) if yb <= half else zero)
        field_ref[0, :, k * LANES : (k + 1) * LANES] = p
        field_ref[1, :, k * LANES : (k + 1) * LANES] = q
        p, q = pair(mirror(ya), mirror(yb))
        field_ref[2, :, k * LANES : (k + 1) * LANES] = p
        field_ref[3, :, k * LANES : (k + 1) * LANES] = q


def box_kernel(
    side, chunks, team, x_ref, tab_ref, field_ref, spot_ref, start_s, wz_ref,
    out_ref, xf, grid, t_scr, l_scr, acc,
):
    groups, rows, waves = x_ref.shape
    bands = rows // 2
    blocks = rows // 8
    span = 2 * side
    xf[0] = x_ref[...]
    for d in range(groups):
        wide_x = x_ref[d].astype(F32)
        xf[1, d] = jnp.concatenate([wide_x[:, STICK_DEV:], wide_x[:, :STICK_DEV]], axis=1).astype(BF16)
        acc[0, d] = jnp.zeros((rows, waves), F32)
        acc[1, d] = jnp.zeros((rows, waves), F32)
    left = lax.broadcasted_iota(jnp.int32, (1, LANES), 1) < STICK_DEV
    places = lax.broadcasted_iota(jnp.int32, (LANES, LANES), 0).astype(F32).astype(BF16)
    one, none = jnp.ones((LANES, LANES), BF16), jnp.zeros((LANES, LANES), BF16)

    def picks(z, dp):
        row_a = jnp.where(left, spot_ref[2 * dp, pl.ds(z, 1), :], -1.0).astype(BF16)
        row_b = jnp.where(left, -1.0, spot_ref[2 * dp + 1, pl.ds(z, 1), :]).astype(BF16)
        return jnp.concatenate(
            [jnp.where(places == row_a, one, none), jnp.where(places == row_b, one, none)], axis=0
        )

    def window(z, d):
        begin = start_s[d, z]
        return begin & 1, pl.ds(pl.multiple_of((begin >> 1) * LANES, LANES), LANES)

    def expand(z):
        for dp in range(groups // 2):
            pieces = []
            for d in (2 * dp, 2 * dp + 1):
                odd, lanes = window(z, d)
                pieces.append(xf[odd, d, :, lanes])
            value = dot(jnp.concatenate(pieces, axis=1), picks(z, dp))
            for block in range(blocks):
                rows_z = pl.ds(block * 8 * side + z, 8, stride=side)
                grid[dp, rows_z, :] = value[block * 8 : (block + 1) * 8]

    def collect(z):
        for dp in range(groups // 2):
            source = jnp.concatenate(
                [grid[dp, pl.ds(block * 8 * side + z, 8, stride=side), :] for block in range(blocks)],
                axis=0,
            ).astype(BF16)
            value = dot_nt(source, picks(z, dp))
            for dd in range(2):
                d = 2 * dp + dd
                odd, lanes = window(z, d)
                acc[odd, d, :, lanes] += value[:, dd * LANES : (dd + 1) * LANES]

    def levels(step):
        def body(i, carry):
            for j in range(UNROLL):
                step(i * UNROLL + j)
            return carry

        lax.fori_loop(0, side // UNROLL, body, 0)

    levels(expand)

    def depth_in(b, carry):
        both = jnp.concatenate(
            [
                jnp.concatenate(
                    [grid[n, pl.ds(b * side, side), :], grid[n, pl.ds((bands + b) * side, side), :]],
                    axis=0,
                )
                for n in range(groups // 2)
            ],
            axis=1,
        ).astype(BF16)
        t_scr[pl.ds(b * span, span), :] = dot(wz_ref[0], both).astype(BF16)
        return carry

    lax.fori_loop(0, bands, depth_in, 0)

    def planes(g, carry):
        rows_g = pl.ds(g * team * span, team * span)
        sticks = t_scr[rows_g, :]
        for k in range(chunks):
            here = slice(k * LANES, (k + 1) * LANES)
            wide = slice(2 * k * LANES, 2 * (k + 1) * LANES)
            ab = dot(sticks, tab_ref[:, wide])
            p, q = field_ref[0, :, here], field_ref[1, :, here]
            p2, q2 = field_ref[2, :, here], field_ref[3, :, here]
            for b in range(team):
                u, x = ab[b * span : b * span + side, :LANES], ab[b * span : b * span + side, LANES:]
                w, v = ab[b * span + side : (b + 1) * span, :LANES], ab[b * span + side : (b + 1) * span, LANES:]
                pr, pi, mr, mi = u - v, w + x, u + v, w - x
                ar, ai = p * pr - q * pi, p * pi + q * pr
                br, bi = p2 * mr - q2 * mi, p2 * mi + q2 * mr
                even = jnp.concatenate([ar + br, ai + bi], axis=0).astype(BF16)
                odd = jnp.concatenate([ai - bi, br - ar], axis=0).astype(BF16)
                l_scr[b * span : (b + 1) * span, wide] = jnp.concatenate([even, odd], axis=1)
        back = dot_nt(l_scr[...], tab_ref[...]).astype(BF16)
        for b in range(team):
            done = dot(wz_ref[1], back[b * span : (b + 1) * span])
            for n in range(groups // 2):
                here = slice(n * LANES, (n + 1) * LANES)
                grid[n, pl.ds((g * team + b) * side, side), :] = done[:side, here]
                grid[n, pl.ds((bands + g * team + b) * side, side), :] = done[side:, here]
        return carry

    lax.fori_loop(0, bands // team, planes, 0)

    levels(collect)
    for d in range(groups):
        late = acc[1, d]
        late = jnp.concatenate([late[:, waves - STICK_DEV :], late[:, : waves - STICK_DEV]], axis=1)
        out_ref[d] = (acc[0, d] + late).astype(BF16)


def finish_kernel(target_ref, y_ref, rank_ref, all_ref, out_ref, g_ref, partner, sem):
    fetch = pltpu.make_async_copy(all_ref.at[target_ref[0]], partner, sem)
    fetch.start()
    rank = rank_ref[...]
    waves = rank.shape[1]
    groups, rows, _ = y_ref.shape
    share = rows // 2
    low = one_hot(rank & 255, 256)
    total = None
    for part in range(waves // 256):
        pieces = [y_ref[q, :, part * 256 : (part + 1) * 256].astype(F32) for q in range(groups)]
        piece = jnp.concatenate(
            [piece[:share] for piece in pieces] + [piece[share:] for piece in pieces], axis=0
        ).astype(BF16)
        value = dot(piece, low)
        value = jnp.where((rank >> 8) == part, value, 0.0)
        total = value if total is None else total + value
    response = total.astype(BF16)
    out_ref[...] = response
    fetch.wait()
    products = dot_nt(partner[...], response)
    half = products.shape[0] // 2
    g_ref[0] = (products[:half, :half] + products[half:, half:]).astype(BF16)
    g_ref[1] = (products[:half, half:] - products[half:, :half]).astype(BF16)


def whole(memory=pltpu.VMEM):
    return pl.BlockSpec(memory_space=memory)


def params():
    return pltpu.CompilerParams(vmem_limit_bytes=VMEM_LIMIT)


def shards(orbitals, box_index, partner_pool, potential):
    fft_count = lax.axis_size("fft")
    side = potential.shape[0]
    bands = orbitals.shape[2]
    waves = orbitals.shape[3]
    share = bands // fft_count
    columns = STICK_DEV * fft_count
    chunks = (side // 2 + 1 + 1) // 2
    tiles = waves // LANES
    coeffs = orbitals.reshape(2 * bands, waves)

    cosine, sine = cos_sin(side)
    cs = jnp.asarray(np.concatenate([cosine, cosine, sine, sine], axis=1))
    half_points = (np.arange(2 * chunks * side) // side) % side
    cyr = jnp.asarray(cosine[:, half_points])
    syr = jnp.asarray(sine[:, half_points])
    inward = np.block([[cosine, -sine], [sine, cosine]])
    outward = np.block([[cosine, sine], [-sine, cosine]])
    wz = jnp.asarray(np.stack([inward, outward]))

    me = lax.axis_index("fft")
    shifts = [[(i, (i + s) % fft_count) for i in range(fft_count)] for s in range(1, fft_count)]
    own_index = box_index.reshape(1, waves)
    indices = [own_index] + [lax.ppermute(own_index, "fft", shift) for shift in shifts]
    gathered = lax.all_gather(coeffs, "pool", axis=0)

    ordered, rank = pl.pallas_call(
        functools.partial(sort_kernel, side, fft_count),
        out_shape=(
            jax.ShapeDtypeStruct((fft_count, 2 * share, waves), BF16),
            jax.ShapeDtypeStruct((1, waves), jnp.int32),
        ),
        in_specs=[whole(), whole()],
        out_specs=(whole(), whole()),
        compiler_params=params(),
        name="sort_waves",
    )(own_index, coeffs)
    moved = lax.all_to_all(ordered, "fft", split_axis=0, concat_axis=0, tiled=True)

    tab, field, spot, start = pl.pallas_call(
        functools.partial(prep_kernel, side, chunks, fft_count),
        out_shape=(
            jax.ShapeDtypeStruct((columns, 2 * chunks * LANES), BF16),
            jax.ShapeDtypeStruct((4, side, chunks * LANES), F32),
            jax.ShapeDtypeStruct((fft_count, side, 2 * STICK_DEV), F32),
            jax.ShapeDtypeStruct((fft_count, side), jnp.int32),
        ),
        in_specs=[whole(pltpu.SMEM)] + [whole()] * (fft_count + 4),
        out_specs=(whole(),) * 4,
        compiler_params=params(),
        cost_estimate=pl.CostEstimate(flops=10**9, bytes_accessed=10**7, transcendentals=0),
        name="prepare",
    )(me.reshape(1), *indices, potential.reshape(side * side, 2 * side), cs, cyr, syr)

    team = min(4, share)
    back = pl.pallas_call(
        functools.partial(box_kernel, side, chunks, team),
        out_shape=jax.ShapeDtypeStruct((fft_count, 2 * share, waves), BF16),
        in_specs=[whole()] * 4 + [whole(pltpu.SMEM), whole()],
        out_specs=whole(),
        scratch_shapes=[
            pltpu.VMEM((2, fft_count, 2 * share, waves), BF16),
            pltpu.VMEM((columns // LANES, 2 * share * side, LANES), F32),
            pltpu.VMEM((2 * share * side, columns), BF16),
            pltpu.VMEM((team * 2 * side, 2 * chunks * LANES), BF16),
            pltpu.VMEM((2, fft_count, 2 * share, waves), F32),
        ],
        compiler_params=params(),
        cost_estimate=pl.CostEstimate(flops=10**10, bytes_accessed=10**7, transcendentals=0),
        name="box_work",
    )(moved, tab, field, spot, start, wz)
    returned = lax.all_to_all(back, "fft", split_axis=0, concat_axis=0, tiled=True)

    target = partner_pool[lax.axis_index("pool")].reshape(1)
    response, sums = pl.pallas_call(
        finish_kernel,
        out_shape=(
            jax.ShapeDtypeStruct((2 * bands, waves), BF16),
            jax.ShapeDtypeStruct((2, bands, bands), BF16),
        ),
        in_specs=[whole(pltpu.SMEM), whole(), whole(), whole(pltpu.HBM)],
        out_specs=(whole(), whole()),
        scratch_shapes=[pltpu.VMEM((2 * bands, waves), BF16), pltpu.SemaphoreType.DMA],
        compiler_params=params(),
        name="finish",
    )(target, returned, rank, gathered)
    shares = [sums] + [lax.ppermute(sums, "fft", shift) for shift in shifts]
    summed = None
    for d in range(fft_count):
        offset = lax.rem(me + fft_count - d, fft_count)
        term = shares[0]
        for s in range(1, fft_count):
            term = jnp.where(offset == s, shares[s], term)
        term = term.astype(F32)
        summed = term if summed is None else summed + term
    coupling = (summed / jnp.sqrt(jnp.float32(waves * fft_count)))[:, None]
    return response.reshape(2, 1, bands, waves), coupling


def solution(mesh):
    placed = (P(None, "pool", None, "fft"), P("fft"), P(), P())
    return jax.shard_map(
        shards,
        mesh=mesh,
        in_specs=placed,
        out_specs=(P(None, "pool", None, "fft"), P(None, "pool", None, None)),
        check_vma=False,
    )
```

```python
import functools

import jax
import jax.numpy as jnp
import ml_dtypes
import numpy as np
from jax import lax
from jax.experimental import pallas as pl
from jax.experimental.pallas import tpu as pltpu
from jax.sharding import PartitionSpec as P

STICK_DEV = 64
LANES = 128
UNROLL = 4
BF16 = jnp.bfloat16
F32 = jnp.float32
VMEM_LIMIT = 36 * 1024 * 1024


def cos_sin(side):
    points = np.arange(side)
    angles = (2.0 * np.pi / side) * (points[:, None] * points[None, :] % side)
    scaling = 1.0 / np.sqrt(side)
    cosine = (np.cos(angles) * scaling).astype(ml_dtypes.bfloat16)
    sine = (np.sin(angles) * scaling).astype(ml_dtypes.bfloat16)
    return cosine, sine


def dot(a, b):
    return jnp.dot(a, b, preferred_element_type=F32)


def dot_nt(a, b):
    return lax.dot_general(a, b, (((1,), (1,)), ((), ())), preferred_element_type=F32)


def one_hot(row, count):
    places = lax.broadcasted_iota(jnp.int32, (count, row.shape[1]), 0)
    return jnp.where(places == row, 1.0, 0.0).astype(BF16)


def triangles(side):
    rows = lax.broadcasted_iota(jnp.int32, (side, side), 0)
    cols = lax.broadcasted_iota(jnp.int32, (side, side), 1)
    upper = jnp.where(rows < cols, 1.0, 0.0).astype(BF16)
    lower = jnp.where(rows > cols, 1.0, 0.0).astype(BF16)
    return upper, lower, jnp.ones((side, side), BF16)


def prefix(occupied, tri):
    upper, lower, ones = tri
    in_rows = dot(occupied, ones).astype(BF16)
    return dot(occupied, upper) + dot(lower, in_rows)


def locate(idx, side):
    bits = side.bit_length() - 1
    tri = triangles(side)
    xh = one_hot(idx >> (2 * bits), side)
    yh = one_hot((idx >> bits) & (side - 1), side)
    zh = one_hot(idx & (side - 1), side)
    columns = jnp.minimum(dot_nt(xh, yh), 1.0).astype(BF16)
    slots = prefix(columns, tri).astype(BF16)
    slot = jnp.sum(xh.astype(F32) * dot(slots, yh), axis=0, keepdims=True)
    ch = one_hot(slot.astype(jnp.int32), STICK_DEV)
    cells = dot_nt(zh, ch)
    ranks = prefix(cells.astype(BF16), tri)
    high = jnp.floor(ranks * (1.0 / side))
    low = ranks - high * side
    looked = dot(high.astype(BF16), ch) * side + dot(low.astype(BF16), ch)
    rank = jnp.sum(zh.astype(F32) * looked, axis=0, keepdims=True)
    return xh, yh, ch, cells, ranks, rank.astype(jnp.int32)


def sort_block(x_ref, rank, low, part):
    mask = jnp.where((rank >> 8) == part, 1.0, 0.0).astype(BF16)
    return dot_nt(x_ref[...] * mask, low)


def sort_kernel(side, groups, idx_ref, x_hbm, out_ref, rank_ref, x_ref, sem):
    fetch = pltpu.make_async_copy(x_hbm, x_ref, sem)
    fetch.start()
    xh, yh, ch, cells, ranks, rank = locate(idx_ref[...], side)
    rank_ref[...] = rank
    waves = rank.shape[1]
    bands = x_ref.shape[0] // 2
    share = bands // groups
    rows = 2 * share
    lane = lax.broadcasted_iota(jnp.int32, (STICK_DEV, side), 1).astype(F32)
    cells = jnp.concatenate([cells[i : i + rows] for i in range(0, side, rows)], axis=1)
    slot = lax.broadcasted_iota(jnp.int32, (rows, LANES), 1) // rows
    place = jnp.zeros((rows, LANES), F32)
    count = 0
    for hot in (xh, yh):
        at = jnp.minimum(dot_nt(ch, hot), 1.0)
        value = jnp.sum(at * lane, axis=1, keepdims=True)
        for i in range(0, STICK_DEV, rows):
            place = jnp.where(slot == count, value[i : i + rows], place)
            count += 1
    extra = jnp.concatenate([cells, place], axis=1).astype(BF16)
    low = one_hot(rank & 255, 256)
    fetch.wait()
    for q in range(groups):
        out_ref[q, :, waves:] = extra
    for part in range(waves // 256):
        piece = sort_block(x_ref, rank, low, part)
        for q in range(groups):
            re = piece[q * share : (q + 1) * share]
            im = piece[bands + q * share : bands + (q + 1) * share]
            both = jnp.concatenate([re, im], axis=0).astype(BF16)
            out_ref[q, :, part * 256 : (part + 1) * 256] = both


def field_kernel(side, chunks, pot_ref, field_ref):
    half = side // 2
    lane = lax.broadcasted_iota(jnp.int32, (side, LANES), 1)
    first = lane < side
    flipped = (lane & side) + ((side - (lane & (side - 1))) & (side - 1))

    def pair(row_a, row_b):
        p = jnp.where(first, row_a, pltpu.roll(row_b, side, 1))
        q = jnp.where(first, pltpu.roll(row_a, side, 1), row_b)
        return p, q

    def plane(y):
        return pot_ref[pl.ds(y, side, stride=side), :]

    def mirror(y):
        if y == 0 or y >= half:
            return jnp.zeros((side, LANES), F32)
        return jnp.take_along_axis(plane(side - y), flipped, axis=1)

    zero = jnp.zeros((side, LANES), F32)
    for k in range(chunks):
        ya, yb = 2 * k, 2 * k + 1
        here = slice(k * LANES, (k + 1) * LANES)
        field_ref[0, :, here], field_ref[1, :, here] = pair(
            plane(ya), plane(yb) if yb <= half else zero
        )
        field_ref[2, :, here], field_ref[3, :, here] = pair(mirror(ya), mirror(yb))


def select_kernel(order_ref, in_ref, out_ref, sems):
    copies = []
    for i in range(out_ref.shape[0]):
        copy = pltpu.make_async_copy(in_ref.at[order_ref[i]], out_ref.at[i], sems.at[i])
        copy.start()
        copies.append(copy)
    for copy in copies:
        copy.wait()


def box_kernel(
    side, chunks, team, waves, x_ref, field_ref, cs_ref, cyr_ref, syr_ref, wz_ref,
    out_ref, xf, grid, t_scr, l_scr, acc, tab_ref, spot_ref, start_v, start_s, sem,
):
    groups, rows, _ = x_ref.shape
    bands = rows // 2
    blocks = rows // 8
    span = 2 * side
    tri = triangles(side)
    parts = side // rows
    cells_end = waves + parts * STICK_DEV
    lane_f = lax.broadcasted_iota(jnp.int32, (STICK_DEV, side), 1).astype(F32)
    at_x, at_y = [], []
    for d in range(groups):
        cells = jnp.concatenate(
            [x_ref[d, :, waves + i * STICK_DEV : waves + (i + 1) * STICK_DEV].astype(F32) for i in range(parts)],
            axis=0,
        )
        place = x_ref[d, :, cells_end : cells_end + LANES].astype(F32)
        for which, hots in enumerate((at_x, at_y)):
            value = jnp.concatenate(
                [place[:, i * rows : i * rows + 1] for i in range(which * parts, (which + 1) * parts)],
                axis=0,
            )
            hots.append(jnp.where(lane_f == value, 1.0, 0.0))
        ranks = prefix(cells.astype(BF16), tri)
        begins = jnp.floor(ranks[:, :1] * (1.0 / STICK_DEV))
        spot = jnp.where(cells > 0.5, ranks - begins * STICK_DEV, -1.0)
        spot_ref[d] = jnp.concatenate([spot, spot], axis=1)
        level = dot_nt(jnp.ones((8, STICK_DEV), BF16), cells.astype(BF16))
        before = dot(level.astype(BF16), tri[0])
        start_v[d : d + 1, :side] = (before[:1] * (1.0 / STICK_DEV)).astype(jnp.int32)
    to_scalars = pltpu.make_async_copy(start_v, start_s, sem)
    to_scalars.start()
    at_x = jnp.concatenate(at_x, axis=0).astype(BF16)
    at_y = jnp.concatenate(at_y, axis=0).astype(BF16)
    both = dot(at_x, cs_ref[...])
    cx, sx = both[:, :LANES], both[:, LANES:]
    for k in range(chunks):
        cy = dot(at_y, cyr_ref[:, k * LANES : (k + 1) * LANES])
        sy = dot(at_y, syr_ref[:, k * LANES : (k + 1) * LANES])
        base = 2 * k * LANES
        tab_ref[:, base : base + LANES] = (cy * cx - sy * sx).astype(BF16)
        tab_ref[:, base + LANES : base + 2 * LANES] = (cy * sx + sy * cx).astype(BF16)
    to_scalars.wait()

    xf[0] = x_ref[:, :, :waves]
    for d in range(groups):
        wide_x = x_ref[d, :, :waves].astype(F32)
        xf[1, d] = jnp.concatenate([wide_x[:, STICK_DEV:], wide_x[:, :STICK_DEV]], axis=1).astype(BF16)
        acc[0, d] = jnp.zeros((rows, waves), F32)
        acc[1, d] = jnp.zeros((rows, waves), F32)
    left = lax.broadcasted_iota(jnp.int32, (1, LANES), 1) < STICK_DEV
    places = lax.broadcasted_iota(jnp.int32, (LANES, LANES), 0).astype(F32).astype(BF16)
    one, none = jnp.ones((LANES, LANES), BF16), jnp.zeros((LANES, LANES), BF16)

    def picks(z, dp):
        row_a = jnp.where(left, spot_ref[2 * dp, pl.ds(z, 1), :], -1.0).astype(BF16)
        row_b = jnp.where(left, -1.0, spot_ref[2 * dp + 1, pl.ds(z, 1), :]).astype(BF16)
        return jnp.concatenate(
            [jnp.where(places == row_a, one, none), jnp.where(places == row_b, one, none)], axis=0
        )

    def window(z, d):
        begin = start_s[d, z]
        return begin & 1, pl.ds(pl.multiple_of((begin >> 1) * LANES, LANES), LANES)

    def expand(z):
        for dp in range(groups // 2):
            pieces = []
            for d in (2 * dp, 2 * dp + 1):
                odd, lanes = window(z, d)
                pieces.append(xf[odd, d, :, lanes])
            value = dot(jnp.concatenate(pieces, axis=1), picks(z, dp))
            for block in range(blocks):
                rows_z = pl.ds(block * 8 * side + z, 8, stride=side)
                grid[dp, rows_z, :] = value[block * 8 : (block + 1) * 8]

    def collect(z):
        for dp in range(groups // 2):
            source = jnp.concatenate(
                [grid[dp, pl.ds(block * 8 * side + z, 8, stride=side), :] for block in range(blocks)],
                axis=0,
            ).astype(BF16)
            value = dot_nt(source, picks(z, dp))
            for dd in range(2):
                d = 2 * dp + dd
                odd, lanes = window(z, d)
                acc[odd, d, :, lanes] += value[:, dd * LANES : (dd + 1) * LANES]

    def levels(step):
        def body(i, carry):
            for j in range(UNROLL):
                step(i * UNROLL + j)
            return carry

        lax.fori_loop(0, side // UNROLL, body, 0)

    levels(expand)

    def depth_in(b, carry):
        both = jnp.concatenate(
            [
                jnp.concatenate(
                    [grid[n, pl.ds(b * side, side), :], grid[n, pl.ds((bands + b) * side, side), :]],
                    axis=0,
                )
                for n in range(groups // 2)
            ],
            axis=1,
        ).astype(BF16)
        t_scr[pl.ds(b * span, span), :] = dot(wz_ref[0], both).astype(BF16)
        return carry

    lax.fori_loop(0, bands, depth_in, 0)

    def planes(g, carry):
        rows_g = pl.ds(g * team * span, team * span)
        sticks = t_scr[rows_g, :]
        for k in range(chunks):
            here = slice(k * LANES, (k + 1) * LANES)
            wide = slice(2 * k * LANES, 2 * (k + 1) * LANES)
            ab = dot(sticks, tab_ref[:, wide])
            p, q = field_ref[0, :, here], field_ref[1, :, here]
            p2, q2 = field_ref[2, :, here], field_ref[3, :, here]
            for b in range(team):
                u, x = ab[b * span : b * span + side, :LANES], ab[b * span : b * span + side, LANES:]
                w, v = ab[b * span + side : (b + 1) * span, :LANES], ab[b * span + side : (b + 1) * span, LANES:]
                pr, pi, mr, mi = u - v, w + x, u + v, w - x
                ar, ai = p * pr - q * pi, p * pi + q * pr
                br, bi = p2 * mr - q2 * mi, p2 * mi + q2 * mr
                even = jnp.concatenate([ar + br, ai + bi], axis=0).astype(BF16)
                odd = jnp.concatenate([ai - bi, br - ar], axis=0).astype(BF16)
                l_scr[b * span : (b + 1) * span, wide] = jnp.concatenate([even, odd], axis=1)
        back = dot_nt(l_scr[...], tab_ref[...]).astype(BF16)
        for b in range(team):
            done = dot(wz_ref[1], back[b * span : (b + 1) * span])
            for n in range(groups // 2):
                here = slice(n * LANES, (n + 1) * LANES)
                grid[n, pl.ds((g * team + b) * side, side), :] = done[:side, here]
                grid[n, pl.ds((bands + g * team + b) * side, side), :] = done[side:, here]
        return carry

    lax.fori_loop(0, bands // team, planes, 0)

    levels(collect)
    for d in range(groups):
        late = acc[1, d]
        late = jnp.concatenate([late[:, waves - STICK_DEV :], late[:, : waves - STICK_DEV]], axis=1)
        out_ref[d] = (acc[0, d] + late).astype(BF16)


def partner_kernel(x_ref, rank_ref, out_ref):
    rank = rank_ref[...]
    low = one_hot(rank & 255, 256)
    for part in range(rank.shape[1] // 256):
        out_ref[:, part * 256 : (part + 1) * 256] = sort_block(x_ref, rank, low, part).astype(BF16)


def by_part(blocks):
    share = blocks[0].shape[0] // 2
    return jnp.concatenate(
        [block[:share] for block in blocks] + [block[share:] for block in blocks], axis=0
    ).astype(BF16)


def couple_kernel(y_ref, partner_ref, g_ref):
    response = by_part([y_ref[q].astype(F32) for q in range(y_ref.shape[0])])
    products = dot_nt(partner_ref[...], response)
    half = products.shape[0] // 2
    g_ref[0] = (products[:half, :half] + products[half:, half:]).astype(BF16)
    g_ref[1] = (products[:half, half:] - products[half:, :half]).astype(BF16)


def unsort_kernel(y_ref, rank_ref, out_ref):
    rank = rank_ref[...]
    low = one_hot(rank & 255, 256)
    total = None
    for part in range(rank.shape[1] // 256):
        here = slice(part * 256, (part + 1) * 256)
        piece = by_part([y_ref[q, :, here].astype(F32) for q in range(y_ref.shape[0])])
        value = jnp.where((rank >> 8) == part, dot(piece, low), 0.0)
        total = value if total is None else total + value
    out_ref[...] = total.astype(BF16)


def whole(memory=pltpu.VMEM):
    return pl.BlockSpec(memory_space=memory)


def params():
    return pltpu.CompilerParams(vmem_limit_bytes=VMEM_LIMIT)


def shards(orbitals, box_index, partner_pool, potential):
    fft_count = lax.axis_size("fft")
    side = potential.shape[0]
    bands = orbitals.shape[2]
    waves = orbitals.shape[3]
    share = bands // fft_count
    columns = STICK_DEV * fft_count
    chunks = (side // 2 + 1 + 1) // 2
    coeffs = orbitals.reshape(2 * bands, waves)

    cosine, sine = cos_sin(side)
    cs = jnp.asarray(np.concatenate([cosine, cosine, sine, sine], axis=1))
    half_points = (np.arange(2 * chunks * side) // side) % side
    cyr = jnp.asarray(cosine[:, half_points])
    syr = jnp.asarray(sine[:, half_points])
    inward = np.block([[cosine, -sine], [sine, cosine]])
    outward = np.block([[cosine, sine], [-sine, cosine]])
    wz = jnp.asarray(np.stack([inward, outward]))

    me = lax.axis_index("fft")
    shifts = [[(i, (i + s) % fft_count) for i in range(fft_count)] for s in range(1, fft_count)]
    pool_count = lax.axis_size("pool")
    rows = 2 * share
    packed = waves + side * STICK_DEV // rows + LANES

    ordered, rank = pl.pallas_call(
        functools.partial(sort_kernel, side, fft_count),
        out_shape=(
            jax.ShapeDtypeStruct((fft_count, rows, packed), BF16),
            jax.ShapeDtypeStruct((1, waves), jnp.int32),
        ),
        in_specs=[whole(), whole(pltpu.HBM)],
        out_specs=(whole(), whole()),
        scratch_shapes=[pltpu.VMEM((2 * bands, waves), BF16), pltpu.SemaphoreType.DMA],
        compiler_params=params(),
        name="sort_waves",
    )(box_index.reshape(1, waves), coeffs)
    moved = lax.all_to_all(ordered, "fft", split_axis=0, concat_axis=0, tiled=True)

    spread = lax.all_to_all(
        coeffs.reshape(pool_count, 2 * bands // pool_count, waves), "pool", 0, 0, tiled=True
    )
    chosen = pl.pallas_call(
        select_kernel,
        out_shape=jax.ShapeDtypeStruct(spread.shape, BF16),
        in_specs=[whole(pltpu.SMEM), whole(pl.ANY)],
        out_specs=whole(pl.ANY),
        scratch_shapes=[pltpu.SemaphoreType.DMA((pool_count,))],
        compiler_params=params(),
        name="select_partner",
    )(partner_pool, spread)
    partner = lax.all_to_all(chosen, "pool", 0, 0, tiled=True).reshape(2 * bands, waves)

    field = pl.pallas_call(
        functools.partial(field_kernel, side, chunks),
        out_shape=jax.ShapeDtypeStruct((4, side, chunks * LANES), F32),
        in_specs=[whole()],
        out_specs=whole(),
        compiler_params=params(),
        cost_estimate=pl.CostEstimate(flops=10**9, bytes_accessed=10**7, transcendentals=0),
        name="field_pairs",
    )(potential.reshape(side * side, 2 * side))

    team = min(4, share)
    back = pl.pallas_call(
        functools.partial(box_kernel, side, chunks, team, waves),
        out_shape=jax.ShapeDtypeStruct((fft_count, rows, waves), BF16),
        in_specs=[whole()] * 6,
        out_specs=whole(),
        scratch_shapes=[
            pltpu.VMEM((2, fft_count, rows, waves), BF16),
            pltpu.VMEM((columns // LANES, rows * side, LANES), F32),
            pltpu.VMEM((rows * side, columns), BF16),
            pltpu.VMEM((team * 2 * side, 2 * chunks * LANES), BF16),
            pltpu.VMEM((2, fft_count, rows, waves), F32),
            pltpu.VMEM((columns, 2 * chunks * LANES), BF16),
            pltpu.VMEM((fft_count, side, 2 * STICK_DEV), F32),
            pltpu.VMEM((fft_count, LANES), jnp.int32),
            pltpu.SMEM((fft_count, LANES), jnp.int32),
            pltpu.SemaphoreType.DMA,
        ],
        compiler_params=params(),
        cost_estimate=pl.CostEstimate(flops=10**10, bytes_accessed=10**7, transcendentals=0),
        name="box_work",
    )(moved, field, cs, cyr, syr, wz)
    returned = lax.all_to_all(back, "fft", split_axis=0, concat_axis=0, tiled=True)

    ordered_partner = pl.pallas_call(
        partner_kernel,
        out_shape=jax.ShapeDtypeStruct((2 * bands, waves), BF16),
        in_specs=[whole(), whole()],
        out_specs=whole(),
        compiler_params=params(),
        cost_estimate=pl.CostEstimate(flops=10**9, bytes_accessed=10**7, transcendentals=0),
        name="sort_partner",
    )(partner, rank)
    sums = pl.pallas_call(
        couple_kernel,
        out_shape=jax.ShapeDtypeStruct((2, bands, bands), BF16),
        in_specs=[whole(), whole()],
        out_specs=whole(),
        compiler_params=params(),
        name="couple",
    )(returned, ordered_partner)
    shares = [sums] + [lax.ppermute(sums, "fft", shift) for shift in shifts]
    response = pl.pallas_call(
        unsort_kernel,
        out_shape=jax.ShapeDtypeStruct((2 * bands, waves), BF16),
        in_specs=[whole(), whole()],
        out_specs=whole(),
        compiler_params=params(),
        cost_estimate=pl.CostEstimate(flops=10**9, bytes_accessed=10**7, transcendentals=0),
        name="unsort",
    )(returned, rank)
    summed = None
    for d in range(fft_count):
        offset = lax.rem(me + fft_count - d, fft_count)
        term = shares[0]
        for s in range(1, fft_count):
            term = jnp.where(offset == s, shares[s], term)
        term = term.astype(F32)
        summed = term if summed is None else summed + term
    coupling = (summed / jnp.sqrt(jnp.float32(waves * fft_count)))[:, None]
    return response.reshape(2, 1, bands, waves), coupling


def solution(mesh):
    placed = (P(None, "pool", None, "fft"), P("fft"), P(), P())
    return jax.shard_map(
        shards,
        mesh=mesh,
        in_specs=placed,
        out_specs=(P(None, "pool", None, "fft"), P(None, "pool", None, None)),
        check_vma=False,
    )
```

```python
import functools

import jax
import jax.numpy as jnp
import ml_dtypes
import numpy as np
from jax import lax
from jax.experimental import pallas as pl
from jax.experimental.pallas import tpu as pltpu
from jax.sharding import PartitionSpec as P

STICK_DEV = 64
LANES = 128
UNROLL = 4
BF16 = jnp.bfloat16
F32 = jnp.float32
VMEM_LIMIT = 24 * 1024 * 1024
SORT_LIMIT = 60 * 1024 * 1024


def cos_sin(side):
    points = np.arange(side)
    angles = (2.0 * np.pi / side) * (points[:, None] * points[None, :] % side)
    scaling = 1.0 / np.sqrt(side)
    cosine = (np.cos(angles) * scaling).astype(ml_dtypes.bfloat16)
    sine = (np.sin(angles) * scaling).astype(ml_dtypes.bfloat16)
    return cosine, sine


def dot(a, b):
    return jnp.dot(a, b, preferred_element_type=F32)


def dot_nt(a, b):
    return lax.dot_general(a, b, (((1,), (1,)), ((), ())), preferred_element_type=F32)


def one_hot(row, count):
    places = lax.broadcasted_iota(jnp.int32, (count, row.shape[1]), 0)
    return jnp.where(places == row, 1.0, 0.0).astype(BF16)


def triangles(side):
    rows = lax.broadcasted_iota(jnp.int32, (side, side), 0)
    cols = lax.broadcasted_iota(jnp.int32, (side, side), 1)
    upper = jnp.where(rows < cols, 1.0, 0.0).astype(BF16)
    lower = jnp.where(rows > cols, 1.0, 0.0).astype(BF16)
    return upper, lower, jnp.ones((side, side), BF16)


def prefix(occupied, tri):
    upper, lower, ones = tri
    in_rows = dot(occupied, ones).astype(BF16)
    return dot(occupied, upper) + dot(lower, in_rows)


def locate(idx, side):
    bits = side.bit_length() - 1
    tri = triangles(side)
    xh = one_hot(idx >> (2 * bits), side)
    yh = one_hot((idx >> bits) & (side - 1), side)
    zh = one_hot(idx & (side - 1), side)
    columns = jnp.minimum(dot_nt(xh, yh), 1.0).astype(BF16)
    slots = prefix(columns, tri).astype(BF16)
    slot = jnp.sum(xh.astype(F32) * dot(slots, yh), axis=0, keepdims=True)
    ch = one_hot(slot.astype(jnp.int32), STICK_DEV)
    cells = dot_nt(zh, ch)
    ranks = prefix(cells.astype(BF16), tri)
    high = jnp.floor(ranks * (1.0 / side))
    low = ranks - high * side
    looked = dot(high.astype(BF16), ch) * side + dot(low.astype(BF16), ch)
    rank = jnp.sum(zh.astype(F32) * looked, axis=0, keepdims=True)
    return xh, yh, ch, cells, ranks, rank.astype(jnp.int32)


def sort_kernel(side, groups, me_ref, idx_ref, x_hbm, *refs):
    outs, (all_ref, rank_ref, x_ref, wide, pieces, sem) = refs[:groups], refs[groups:]
    fetch = pltpu.make_async_copy(x_hbm, x_ref, sem)
    fetch.start()
    xh, yh, ch, cells, ranks, rank = locate(idx_ref[...], side)
    rank_ref[...] = rank
    waves = rank.shape[1]
    both = x_ref.shape[0]
    bands = both // 2
    share = bands // groups
    rows = 2 * share
    lane = lax.broadcasted_iota(jnp.int32, (STICK_DEV, side), 1).astype(F32)
    cells = jnp.concatenate([cells[i : i + rows] for i in range(0, side, rows)], axis=1)
    slot = lax.broadcasted_iota(jnp.int32, (rows, LANES), 1) // rows
    place = jnp.zeros((rows, LANES), F32)
    count = 0
    for hot in (xh, yh):
        at = jnp.minimum(dot_nt(ch, hot), 1.0)
        value = jnp.sum(at * lane, axis=1, keepdims=True)
        for i in range(0, STICK_DEV, rows):
            place = jnp.where(slot == count, value[i : i + rows], place)
            count += 1
    extra = jnp.concatenate([cells, place], axis=1).astype(BF16)
    low = one_hot(rank & 255, 256)
    for out in outs:
        out[:, waves:] = extra
    fetch.wait()
    parts = waves // 256
    for part in range(parts):
        mask = jnp.where((rank >> 8) == part, 1.0, 0.0).astype(BF16)
        wide[part * both : (part + 1) * both] = x_ref[...] * mask
    pieces[...] = dot_nt(wide[...], low)
    for part in range(parts):
        here = slice(part * 256, (part + 1) * 256)
        all_ref[:, here] = pieces[part * both : (part + 1) * both].astype(BF16)
        for shift, out in enumerate(outs):
            q = lax.rem(me_ref[0] + shift, groups)
            begin = pl.multiple_of(part * both + q * share, 8)
            re = pieces[pl.ds(begin, share)]
            im = pieces[pl.ds(begin + bands, share)]
            out[:, here] = jnp.concatenate([re, im], axis=0).astype(BF16)


def field_kernel(side, chunks, pot_ref, cs_ref, field_ref, cyr_ref, syr_ref):
    half = side // 2
    left = lax.broadcasted_iota(jnp.int32, (side, LANES), 1) < side
    for ref, begin in ((cyr_ref, 0), (syr_ref, LANES)):
        table = cs_ref[:, begin : begin + side].astype(F32)
        for k in range(chunks):
            ya, yb = (2 * k) % side, (2 * k + 1) % side
            ref[:, k * LANES : (k + 1) * LANES] = jnp.where(
                left, table[:, ya : ya + 1], table[:, yb : yb + 1]
            ).astype(BF16)
    lane = lax.broadcasted_iota(jnp.int32, (side, LANES), 1)
    first = lane < side
    flipped = (lane & side) + ((side - (lane & (side - 1))) & (side - 1))

    def pair(row_a, row_b):
        p = jnp.where(first, row_a, pltpu.roll(row_b, side, 1))
        q = jnp.where(first, pltpu.roll(row_a, side, 1), row_b)
        return p, q

    def plane(y):
        return pot_ref[pl.ds(y, side, stride=side), :]

    def mirror(y):
        if y == 0 or y >= half:
            return jnp.zeros((side, LANES), F32)
        return jnp.take_along_axis(plane(side - y), flipped, axis=1)

    zero = jnp.zeros((side, LANES), F32)
    for k in range(chunks):
        ya, yb = 2 * k, 2 * k + 1
        here = slice(k * LANES, (k + 1) * LANES)
        field_ref[0, :, here], field_ref[1, :, here] = pair(
            plane(ya), plane(yb) if yb <= half else zero
        )
        field_ref[2, :, here], field_ref[3, :, here] = pair(mirror(ya), mirror(yb))


def select_kernel(order_ref, in_ref, out_ref, sems):
    copies = []
    for i in range(out_ref.shape[0]):
        copy = pltpu.make_async_copy(in_ref.at[order_ref[i]], out_ref.at[i], sems.at[i])
        copy.start()
        copies.append(copy)
    for copy in copies:
        copy.wait()


def box_kernel(
    side, chunks, team, waves, groups, *refs,
):
    x_refs, refs = refs[:groups], refs[groups:]
    (field_ref, cs_ref, cyr_ref, syr_ref, wz_ref), refs = refs[:5], refs[5:]
    out_refs, refs = refs[:groups], refs[groups:]
    xf, grid, t_scr, l_scr, acc, tab_ref, spot_ref, start_v, start_s, sem = refs
    rows = x_refs[0].shape[0]
    bands = rows // 2
    blocks = rows // 8
    span = 2 * side
    tri = triangles(side)
    parts = side // rows
    cells_end = waves + parts * STICK_DEV
    lane_f = lax.broadcasted_iota(jnp.int32, (STICK_DEV, side), 1).astype(F32)
    at_x, at_y = [], []
    for d in range(groups):
        cells = jnp.concatenate(
            [x_refs[d][:, waves + i * STICK_DEV : waves + (i + 1) * STICK_DEV].astype(F32) for i in range(parts)],
            axis=0,
        )
        place = x_refs[d][:, cells_end : cells_end + LANES].astype(F32)
        for which, hots in enumerate((at_x, at_y)):
            value = jnp.concatenate(
                [place[:, i * rows : i * rows + 1] for i in range(which * parts, (which + 1) * parts)],
                axis=0,
            )
            hots.append(jnp.where(lane_f == value, 1.0, 0.0))
        ranks = prefix(cells.astype(BF16), tri)
        begins = jnp.floor(ranks[:, :1] * (1.0 / STICK_DEV))
        spot = jnp.where(cells > 0.5, ranks - begins * STICK_DEV, -1.0)
        spot_ref[d] = jnp.concatenate([spot, spot], axis=1)
        level = dot_nt(jnp.ones((8, STICK_DEV), BF16), cells.astype(BF16))
        before = dot(level.astype(BF16), tri[0])
        start_v[d : d + 1, :side] = (before[:1] * (1.0 / STICK_DEV)).astype(jnp.int32)
    to_scalars = pltpu.make_async_copy(start_v, start_s, sem)
    to_scalars.start()
    at_x = jnp.concatenate(at_x, axis=0).astype(BF16)
    at_y = jnp.concatenate(at_y, axis=0).astype(BF16)
    both = dot(at_x, cs_ref[...])
    cx, sx = both[:, :LANES], both[:, LANES:]
    for k in range(chunks):
        cy = dot(at_y, cyr_ref[:, k * LANES : (k + 1) * LANES])
        sy = dot(at_y, syr_ref[:, k * LANES : (k + 1) * LANES])
        base = 2 * k * LANES
        tab_ref[:, base : base + LANES] = (cy * cx - sy * sx).astype(BF16)
        tab_ref[:, base + LANES : base + 2 * LANES] = (cy * sx + sy * cx).astype(BF16)
    to_scalars.wait()

    for d in range(groups):
        xf[0, d] = x_refs[d][:, :waves]
        wide_x = x_refs[d][:, :waves].astype(F32)
        xf[1, d] = jnp.concatenate([wide_x[:, STICK_DEV:], wide_x[:, :STICK_DEV]], axis=1).astype(BF16)
        acc[0, d] = jnp.zeros((rows, waves), F32)
        acc[1, d] = jnp.zeros((rows, waves), F32)
    left = lax.broadcasted_iota(jnp.int32, (1, LANES), 1) < STICK_DEV
    places = lax.broadcasted_iota(jnp.int32, (LANES, LANES), 0).astype(F32).astype(BF16)
    one, none = jnp.ones((LANES, LANES), BF16), jnp.zeros((LANES, LANES), BF16)

    def picks(z, dp):
        row_a = jnp.where(left, spot_ref[2 * dp, pl.ds(z, 1), :], -1.0).astype(BF16)
        row_b = jnp.where(left, -1.0, spot_ref[2 * dp + 1, pl.ds(z, 1), :]).astype(BF16)
        return jnp.concatenate(
            [jnp.where(places == row_a, one, none), jnp.where(places == row_b, one, none)], axis=0
        )

    def window(z, d):
        begin = start_s[d, z]
        return begin & 1, pl.ds(pl.multiple_of((begin >> 1) * LANES, LANES), LANES)

    def expand(z):
        for dp in range(groups // 2):
            pieces = []
            for d in (2 * dp, 2 * dp + 1):
                odd, lanes = window(z, d)
                pieces.append(xf[odd, d, :, lanes])
            value = dot(jnp.concatenate(pieces, axis=1), picks(z, dp))
            for block in range(blocks):
                rows_z = pl.ds(block * 8 * side + z, 8, stride=side)
                grid[dp, rows_z, :] = value[block * 8 : (block + 1) * 8]

    def collect(z):
        for dp in range(groups // 2):
            source = jnp.concatenate(
                [grid[dp, pl.ds(block * 8 * side + z, 8, stride=side), :] for block in range(blocks)],
                axis=0,
            ).astype(BF16)
            value = dot_nt(source, picks(z, dp))
            for dd in range(2):
                d = 2 * dp + dd
                odd, lanes = window(z, d)
                acc[odd, d, :, lanes] += value[:, dd * LANES : (dd + 1) * LANES]

    def levels(step):
        def body(i, carry):
            for j in range(UNROLL):
                step(i * UNROLL + j)
            return carry

        lax.fori_loop(0, side // UNROLL, body, 0)

    levels(expand)

    def depth_in(b, carry):
        both = jnp.concatenate(
            [
                jnp.concatenate(
                    [grid[n, pl.ds(b * side, side), :], grid[n, pl.ds((bands + b) * side, side), :]],
                    axis=0,
                )
                for n in range(groups // 2)
            ],
            axis=1,
        ).astype(BF16)
        t_scr[pl.ds(b * span, span), :] = dot(wz_ref[0], both).astype(BF16)
        return carry

    lax.fori_loop(0, bands, depth_in, 0)

    def planes(g, carry):
        rows_g = pl.ds(g * team * span, team * span)
        sticks = t_scr[rows_g, :]
        for k in range(chunks):
            here = slice(k * LANES, (k + 1) * LANES)
            wide = slice(2 * k * LANES, 2 * (k + 1) * LANES)
            ab = dot(sticks, tab_ref[:, wide])
            p, q = field_ref[0, :, here], field_ref[1, :, here]
            p2, q2 = field_ref[2, :, here], field_ref[3, :, here]
            for b in range(team):
                u, x = ab[b * span : b * span + side, :LANES], ab[b * span : b * span + side, LANES:]
                w, v = ab[b * span + side : (b + 1) * span, :LANES], ab[b * span + side : (b + 1) * span, LANES:]
                pr, pi, mr, mi = u - v, w + x, u + v, w - x
                ar, ai = p * pr - q * pi, p * pi + q * pr
                br, bi = p2 * mr - q2 * mi, p2 * mi + q2 * mr
                even = jnp.concatenate([ar + br, ai + bi], axis=0).astype(BF16)
                odd = jnp.concatenate([ai - bi, br - ar], axis=0).astype(BF16)
                l_scr[b * span : (b + 1) * span, wide] = jnp.concatenate([even, odd], axis=1)
        back = dot_nt(l_scr[...], tab_ref[...]).astype(BF16)
        for b in range(team):
            done = dot(wz_ref[1], back[b * span : (b + 1) * span])
            for n in range(groups // 2):
                here = slice(n * LANES, (n + 1) * LANES)
                grid[n, pl.ds((g * team + b) * side, side), :] = done[:side, here]
                grid[n, pl.ds((bands + g * team + b) * side, side), :] = done[side:, here]
        return carry

    lax.fori_loop(0, bands // team, planes, 0)

    levels(collect)
    for d in range(groups):
        late = acc[1, d]
        late = jnp.concatenate([late[:, waves - STICK_DEV :], late[:, : waves - STICK_DEV]], axis=1)
        out_refs[d][...] = (acc[0, d] + late).astype(BF16)


def couple_kernel(groups, me_ref, *refs):
    y_refs, (partner_ref, sorted_ref, g_ref, rows_scr) = refs[:groups], refs[groups:]
    share = y_refs[0].shape[0] // 2
    half = groups * share
    for shift, y_ref in enumerate(y_refs):
        begin = pl.multiple_of(lax.rem(me_ref[0] + shift, groups) * share, 8)
        value = y_ref[...].astype(F32)
        rows_scr[pl.ds(begin, share)] = value[:share]
        rows_scr[pl.ds(begin + half, share)] = value[share:]
    response = rows_scr[...].astype(BF16)
    sorted_ref[...] = response
    products = dot_nt(partner_ref[...], response)
    g_ref[0] = (products[:half, :half] + products[half:, half:]).astype(BF16)
    g_ref[1] = (products[:half, half:] - products[half:, :half]).astype(BF16)


def unsort_kernel(y_ref, rank_ref, out_ref):
    both, waves = y_ref.shape
    parts = waves // 256
    stacked = jnp.concatenate([y_ref[:, i * 256 : (i + 1) * 256] for i in range(parts)], axis=0)
    for tile in range(parts):
        here = slice(tile * 256, (tile + 1) * 256)
        rank = rank_ref[:, here]
        values = dot(stacked, one_hot(rank & 255, 256))
        total = None
        for part in range(parts):
            value = jnp.where((rank >> 8) == part, values[part * both : (part + 1) * both], 0.0)
            total = value if total is None else total + value
        out_ref[:, here] = total.astype(BF16)


def whole(memory=pltpu.VMEM):
    return pl.BlockSpec(memory_space=memory)


def params(limit=VMEM_LIMIT):
    return pltpu.CompilerParams(vmem_limit_bytes=limit)


def shards(orbitals, box_index, partner_pool, potential):
    fft_count = lax.axis_size("fft")
    side = potential.shape[0]
    bands = orbitals.shape[2]
    waves = orbitals.shape[3]
    share = bands // fft_count
    columns = STICK_DEV * fft_count
    chunks = (side // 2 + 1 + 1) // 2
    coeffs = orbitals.reshape(2 * bands, waves)

    cosine, sine = cos_sin(side)
    cs = jnp.asarray(np.concatenate([cosine, cosine, sine, sine], axis=1))
    inward = np.block([[cosine, -sine], [sine, cosine]])
    outward = np.block([[cosine, sine], [-sine, cosine]])
    wz = jnp.asarray(np.stack([inward, outward]))

    me = lax.axis_index("fft")
    me_row = me.reshape(1)
    onward = [[(i, (i + s) % fft_count) for i in range(fft_count)] for s in range(fft_count)]
    home = [[(j, i) for i, j in pairs] for pairs in onward]
    pool_count = lax.axis_size("pool")
    rows = 2 * share
    packed = waves + side * STICK_DEV // rows + LANES
    scalars, blocks = whole(pltpu.SMEM), [whole()] * fft_count

    *ordered, ordered_all, rank = pl.pallas_call(
        functools.partial(sort_kernel, side, fft_count),
        out_shape=[jax.ShapeDtypeStruct((rows, packed), BF16)] * fft_count
        + [
            jax.ShapeDtypeStruct((2 * bands, waves), BF16),
            jax.ShapeDtypeStruct((1, waves), jnp.int32),
        ],
        in_specs=[scalars, whole(), whole(pltpu.HBM)],
        out_specs=blocks + [whole(), whole()],
        scratch_shapes=[
            pltpu.VMEM((2 * bands, waves), BF16),
            pltpu.VMEM((waves // 256 * 2 * bands, waves), BF16),
            pltpu.VMEM((waves // 256 * 2 * bands, 256), F32),
            pltpu.SemaphoreType.DMA,
        ],
        compiler_params=params(SORT_LIMIT),
        name="sort_waves",
    )(me_row, box_index.reshape(1, waves), coeffs)
    moved = [ordered[0]] + [lax.ppermute(ordered[s], "fft", onward[s]) for s in range(1, fft_count)]

    spread = lax.all_to_all(
        ordered_all.reshape(pool_count, 2 * bands // pool_count, waves), "pool", 0, 0, tiled=True
    )
    chosen = pl.pallas_call(
        select_kernel,
        out_shape=jax.ShapeDtypeStruct(spread.shape, BF16),
        in_specs=[scalars, whole(pl.ANY)],
        out_specs=whole(pl.ANY),
        scratch_shapes=[pltpu.SemaphoreType.DMA((pool_count,))],
        compiler_params=params(),
        name="select_partner",
    )(partner_pool, spread)
    partner = lax.all_to_all(chosen, "pool", 0, 0, tiled=True).reshape(2 * bands, waves)

    field, cyr, syr = pl.pallas_call(
        functools.partial(field_kernel, side, chunks),
        out_shape=(
            jax.ShapeDtypeStruct((4, side, chunks * LANES), F32),
            jax.ShapeDtypeStruct((side, chunks * LANES), BF16),
            jax.ShapeDtypeStruct((side, chunks * LANES), BF16),
        ),
        in_specs=[whole(), whole()],
        out_specs=(whole(),) * 3,
        compiler_params=params(),
        cost_estimate=pl.CostEstimate(flops=10**9, bytes_accessed=10**7, transcendentals=0),
        name="field_pairs",
    )(potential.reshape(side * side, 2 * side), cs)

    team = min(4, share)
    back = pl.pallas_call(
        functools.partial(box_kernel, side, chunks, team, waves, fft_count),
        out_shape=[jax.ShapeDtypeStruct((rows, waves), BF16)] * fft_count,
        in_specs=blocks + [whole()] * 5,
        out_specs=blocks,
        scratch_shapes=[
            pltpu.VMEM((2, fft_count, rows, waves), BF16),
            pltpu.VMEM((columns // LANES, rows * side, LANES), F32),
            pltpu.VMEM((rows * side, columns), BF16),
            pltpu.VMEM((team * 2 * side, 2 * chunks * LANES), BF16),
            pltpu.VMEM((2, fft_count, rows, waves), F32),
            pltpu.VMEM((columns, 2 * chunks * LANES), BF16),
            pltpu.VMEM((fft_count, side, 2 * STICK_DEV), F32),
            pltpu.VMEM((fft_count, LANES), jnp.int32),
            pltpu.SMEM((fft_count, LANES), jnp.int32),
            pltpu.SemaphoreType.DMA,
        ],
        compiler_params=params(),
        cost_estimate=pl.CostEstimate(flops=10**10, bytes_accessed=10**7, transcendentals=0),
        name="box_work",
    )(*moved, field, cs, cyr, syr, wz)
    returned = [back[0]] + [lax.ppermute(back[s], "fft", home[s]) for s in range(1, fft_count)]

    sorted_response, sums = pl.pallas_call(
        functools.partial(couple_kernel, fft_count),
        out_shape=(
            jax.ShapeDtypeStruct((2 * bands, waves), BF16),
            jax.ShapeDtypeStruct((2, bands, bands), BF16),
        ),
        in_specs=[scalars] + blocks + [whole()],
        out_specs=(whole(), whole()),
        scratch_shapes=[pltpu.VMEM((2 * bands, waves), F32)],
        compiler_params=params(),
        name="couple",
    )(me_row, *returned, partner)
    shares = [sums] + [lax.ppermute(sums, "fft", onward[s]) for s in range(1, fft_count)]
    response = pl.pallas_call(
        unsort_kernel,
        out_shape=jax.ShapeDtypeStruct((2 * bands, waves), BF16),
        in_specs=[whole(), whole()],
        out_specs=whole(),
        compiler_params=params(),
        cost_estimate=pl.CostEstimate(flops=10**9, bytes_accessed=10**7, transcendentals=0),
        name="unsort",
    )(sorted_response, rank)
    summed = None
    for d in range(fft_count):
        offset = lax.rem(me + fft_count - d, fft_count)
        term = shares[0]
        for s in range(1, fft_count):
            term = jnp.where(offset == s, shares[s], term)
        term = term.astype(F32)
        summed = term if summed is None else summed + term
    coupling = (summed / jnp.sqrt(jnp.float32(waves * fft_count)))[:, None]
    return response.reshape(2, 1, bands, waves), coupling


def solution(mesh):
    placed = (P(None, "pool", None, "fft"), P("fft"), P(), P())
    return jax.shard_map(
        shards,
        mesh=mesh,
        in_specs=placed,
        out_specs=(P(None, "pool", None, "fft"), P(None, "pool", None, None)),
        check_vma=False,
    )
```

```python
import functools

import jax
import jax.numpy as jnp
import ml_dtypes
import numpy as np
from jax import lax
from jax.experimental import pallas as pl
from jax.experimental.pallas import tpu as pltpu
from jax.sharding import PartitionSpec as P

STICK_DEV = 64
LANES = 128
UNROLL = 16
BF16 = jnp.bfloat16
F32 = jnp.float32
VMEM_LIMIT = 24 * 1024 * 1024
SORT_LIMIT = 60 * 1024 * 1024
ARRANGE_COST = 10**11


def cos_sin(side):
    points = np.arange(side)
    angles = (2.0 * np.pi / side) * (points[:, None] * points[None, :] % side)
    scaling = 1.0 / np.sqrt(side)
    cosine = (np.cos(angles) * scaling).astype(ml_dtypes.bfloat16)
    sine = (np.sin(angles) * scaling).astype(ml_dtypes.bfloat16)
    return cosine, sine


def dot(a, b):
    return jnp.dot(a, b, preferred_element_type=F32)


def dot_nt(a, b):
    return lax.dot_general(a, b, (((1,), (1,)), ((), ())), preferred_element_type=F32)


def one_hot(row, count):
    places = lax.broadcasted_iota(jnp.int32, (count, row.shape[1]), 0)
    return jnp.where(places == row, 1.0, 0.0).astype(BF16)


def triangles(side):
    rows = lax.broadcasted_iota(jnp.int32, (side, side), 0)
    cols = lax.broadcasted_iota(jnp.int32, (side, side), 1)
    upper = jnp.where(rows < cols, 1.0, 0.0).astype(BF16)
    lower = jnp.where(rows > cols, 1.0, 0.0).astype(BF16)
    return upper, lower, jnp.ones((side, side), BF16)


def prefix(occupied, tri):
    upper, lower, ones = tri
    in_rows = dot(occupied, ones).astype(BF16)
    return dot(occupied, upper) + dot(lower, in_rows)


def locate(idx, side):
    bits = side.bit_length() - 1
    tri = triangles(side)
    xh = one_hot(idx >> (2 * bits), side)
    yh = one_hot((idx >> bits) & (side - 1), side)
    zh = one_hot(idx & (side - 1), side)
    columns = jnp.minimum(dot_nt(xh, yh), 1.0).astype(BF16)
    slots = prefix(columns, tri).astype(BF16)
    slot = jnp.sum(xh.astype(F32) * dot(slots, yh), axis=0, keepdims=True)
    ch = one_hot(slot.astype(jnp.int32), STICK_DEV)
    cells = dot_nt(zh, ch)
    ranks = prefix(cells.astype(BF16), tri)
    high = jnp.floor(ranks * (1.0 / side))
    low = ranks - high * side
    looked = dot(high.astype(BF16), ch) * side + dot(low.astype(BF16), ch)
    rank = jnp.sum(zh.astype(F32) * looked, axis=0, keepdims=True)
    return xh, yh, ch, cells, ranks, rank.astype(jnp.int32)


def sort_kernel(side, groups, me_ref, idx_ref, x_hbm, *refs):
    outs, (all_ref, rank_ref, x_ref, wide, pieces, sem) = refs[:groups], refs[groups:]
    fetch = pltpu.make_async_copy(x_hbm, x_ref, sem)
    fetch.start()
    xh, yh, ch, cells, ranks, rank = locate(idx_ref[...], side)
    rank_ref[...] = rank
    waves = rank.shape[1]
    both = x_ref.shape[0]
    bands = both // 2
    share = bands // groups
    rows = 2 * share
    lane = lax.broadcasted_iota(jnp.int32, (STICK_DEV, side), 1).astype(F32)
    cells = jnp.concatenate([cells[i : i + rows] for i in range(0, side, rows)], axis=1)
    slot = lax.broadcasted_iota(jnp.int32, (rows, LANES), 1) // rows
    place = jnp.zeros((rows, LANES), F32)
    count = 0
    for hot in (xh, yh):
        at = jnp.minimum(dot_nt(ch, hot), 1.0)
        value = jnp.sum(at * lane, axis=1, keepdims=True)
        for i in range(0, STICK_DEV, rows):
            place = jnp.where(slot == count, value[i : i + rows], place)
            count += 1
    extra = jnp.concatenate([cells, place], axis=1).astype(BF16)
    low = one_hot(rank & 255, 256)
    for out in outs:
        out[:, waves:] = extra
    fetch.wait()
    parts = waves // 256
    for part in range(parts):
        mask = jnp.where((rank >> 8) == part, 1.0, 0.0).astype(BF16)
        wide[part * both : (part + 1) * both] = x_ref[...] * mask
    pieces[...] = dot_nt(wide[...], low)
    for part in range(parts):
        here = slice(part * 256, (part + 1) * 256)
        all_ref[:, here] = pieces[part * both : (part + 1) * both].astype(BF16)
        for shift, out in enumerate(outs):
            q = me_ref[0] ^ shift
            begin = pl.multiple_of(part * both + q * share, 8)
            re = pieces[pl.ds(begin, share)]
            im = pieces[pl.ds(begin + bands, share)]
            out[:, here] = jnp.concatenate([re, im], axis=0).astype(BF16)


def field_kernel(side, chunks, pot_ref, cs_ref, waves_ref, field_ref, cyr_ref, syr_ref, copy_ref):
    copy_ref[...] = waves_ref[...]
    half = side // 2
    left = lax.broadcasted_iota(jnp.int32, (side, LANES), 1) < side
    for ref, begin in ((cyr_ref, 0), (syr_ref, LANES)):
        table = cs_ref[:, begin : begin + side].astype(F32)
        for k in range(chunks):
            ya, yb = (2 * k) % side, (2 * k + 1) % side
            ref[:, k * LANES : (k + 1) * LANES] = jnp.where(
                left, table[:, ya : ya + 1], table[:, yb : yb + 1]
            ).astype(BF16)
    lane = lax.broadcasted_iota(jnp.int32, (side, LANES), 1)
    first = lane < side
    flipped = (lane & side) + ((side - (lane & (side - 1))) & (side - 1))

    def pair(row_a, row_b):
        p = jnp.where(first, row_a, pltpu.roll(row_b, side, 1))
        q = jnp.where(first, pltpu.roll(row_a, side, 1), row_b)
        return p, q

    def plane(y):
        return pot_ref[pl.ds(y, side, stride=side), :]

    def mirror(y):
        if y == 0 or y >= half:
            return jnp.zeros((side, LANES), F32)
        return jnp.take_along_axis(plane(side - y), flipped, axis=1)

    zero = jnp.zeros((side, LANES), F32)
    for k in range(chunks):
        ya, yb = 2 * k, 2 * k + 1
        here = slice(k * LANES, (k + 1) * LANES)
        field_ref[0, :, here], field_ref[1, :, here] = pair(
            plane(ya), plane(yb) if yb <= half else zero
        )
        field_ref[2, :, here], field_ref[3, :, here] = pair(mirror(ya), mirror(yb))


def select_kernel(order_ref, in_ref, out_ref, sems):
    copies = []
    for i in range(out_ref.shape[0]):
        copy = pltpu.make_async_copy(in_ref.at[order_ref[i]], out_ref.at[i], sems.at[i])
        copy.start()
        copies.append(copy)
    for copy in copies:
        copy.wait()


def box_kernel(
    side, chunks, team, waves, groups, *refs,
):
    x_refs, refs = refs[:groups], refs[groups:]
    (field_ref, cs_ref, cyr_ref, syr_ref, wz_ref), refs = refs[:5], refs[5:]
    out_refs, refs = refs[:groups], refs[groups:]
    xf, grid, t_scr, l_scr, acc, tab_ref, spot_ref, start_v, start_s, sem = refs
    rows = x_refs[0].shape[0]
    bands = rows // 2
    blocks = rows // 8
    span = 2 * side
    tri = triangles(side)
    parts = side // rows
    cells_end = waves + parts * STICK_DEV
    lane_f = lax.broadcasted_iota(jnp.int32, (STICK_DEV, side), 1).astype(F32)
    at_x, at_y = [], []
    for d in range(groups):
        cells = jnp.concatenate(
            [x_refs[d][:, waves + i * STICK_DEV : waves + (i + 1) * STICK_DEV].astype(F32) for i in range(parts)],
            axis=0,
        )
        place = x_refs[d][:, cells_end : cells_end + LANES].astype(F32)
        for which, hots in enumerate((at_x, at_y)):
            value = jnp.concatenate(
                [place[:, i * rows : i * rows + 1] for i in range(which * parts, (which + 1) * parts)],
                axis=0,
            )
            hots.append(jnp.where(lane_f == value, 1.0, 0.0))
        ranks = prefix(cells.astype(BF16), tri)
        begins = jnp.floor(ranks[:, :1] * (1.0 / STICK_DEV))
        spot = jnp.where(cells > 0.5, ranks - begins * STICK_DEV, -1.0)
        spot_ref[d] = jnp.concatenate([spot, spot], axis=1)
        level = dot_nt(jnp.ones((8, STICK_DEV), BF16), cells.astype(BF16))
        before = dot(level.astype(BF16), tri[0])
        start_v[d : d + 1, :side] = (before[:1] * (1.0 / STICK_DEV)).astype(jnp.int32)
    to_scalars = pltpu.make_async_copy(start_v, start_s, sem)
    to_scalars.start()
    at_x = jnp.concatenate(at_x, axis=0).astype(BF16)
    at_y = jnp.concatenate(at_y, axis=0).astype(BF16)
    both = dot(at_x, cs_ref[...])
    cx, sx = both[:, :LANES], both[:, LANES:]
    for k in range(chunks):
        cy = dot(at_y, cyr_ref[:, k * LANES : (k + 1) * LANES])
        sy = dot(at_y, syr_ref[:, k * LANES : (k + 1) * LANES])
        base = 2 * k * LANES
        tab_ref[:, base : base + LANES] = (cy * cx - sy * sx).astype(BF16)
        tab_ref[:, base + LANES : base + 2 * LANES] = (cy * sx + sy * cx).astype(BF16)
    to_scalars.wait()

    for d in range(groups):
        xf[0, d] = x_refs[d][:, :waves]
        wide_x = x_refs[d][:, :waves].astype(F32)
        xf[1, d] = jnp.concatenate([wide_x[:, STICK_DEV:], wide_x[:, :STICK_DEV]], axis=1).astype(BF16)
        acc[0, d] = jnp.zeros((rows, waves), F32)
        acc[1, d] = jnp.zeros((rows, waves), F32)
    left = lax.broadcasted_iota(jnp.int32, (1, LANES), 1) < STICK_DEV
    places = lax.broadcasted_iota(jnp.int32, (LANES, LANES), 0).astype(F32).astype(BF16)
    one, none = jnp.ones((LANES, LANES), BF16), jnp.zeros((LANES, LANES), BF16)

    def picks(z, dp):
        row_a = jnp.where(left, spot_ref[2 * dp, pl.ds(z, 1), :], -1.0).astype(BF16)
        row_b = jnp.where(left, -1.0, spot_ref[2 * dp + 1, pl.ds(z, 1), :]).astype(BF16)
        return jnp.concatenate(
            [jnp.where(places == row_a, one, none), jnp.where(places == row_b, one, none)], axis=0
        )

    def window(z, d):
        begin = start_s[d, z]
        return begin & 1, pl.ds(pl.multiple_of((begin >> 1) * LANES, LANES), LANES)

    def expand(z):
        for dp in range(groups // 2):
            pieces = []
            for d in (2 * dp, 2 * dp + 1):
                odd, lanes = window(z, d)
                pieces.append(xf[odd, d, :, lanes])
            value = dot(jnp.concatenate(pieces, axis=1), picks(z, dp))
            for block in range(blocks):
                rows_z = pl.ds(block * 8 * side + z, 8, stride=side)
                grid[dp, rows_z, :] = value[block * 8 : (block + 1) * 8]

    def collect(z):
        for dp in range(groups // 2):
            source = jnp.concatenate(
                [grid[dp, pl.ds(block * 8 * side + z, 8, stride=side), :] for block in range(blocks)],
                axis=0,
            ).astype(BF16)
            value = dot_nt(source, picks(z, dp))
            for dd in range(2):
                d = 2 * dp + dd
                odd, lanes = window(z, d)
                acc[odd, d, :, lanes] += value[:, dd * LANES : (dd + 1) * LANES]

    def levels(step):
        def body(i, carry):
            for j in range(UNROLL):
                step(i * UNROLL + j)
            return carry

        lax.fori_loop(0, side // UNROLL, body, 0)

    levels(expand)

    def depth_in(b, carry):
        both = jnp.concatenate(
            [
                jnp.concatenate(
                    [grid[n, pl.ds(b * side, side), :], grid[n, pl.ds((bands + b) * side, side), :]],
                    axis=0,
                )
                for n in range(groups // 2)
            ],
            axis=1,
        ).astype(BF16)
        t_scr[pl.ds(b * span, span), :] = dot(wz_ref[0], both).astype(BF16)
        return carry

    lax.fori_loop(0, bands, depth_in, 0)

    def planes(g, carry):
        rows_g = pl.ds(g * team * span, team * span)
        sticks = t_scr[rows_g, :]
        for k in range(chunks):
            here = slice(k * LANES, (k + 1) * LANES)
            wide = slice(2 * k * LANES, 2 * (k + 1) * LANES)
            ab = dot(sticks, tab_ref[:, wide])
            p, q = field_ref[0, :, here], field_ref[1, :, here]
            p2, q2 = field_ref[2, :, here], field_ref[3, :, here]
            for b in range(team):
                u, x = ab[b * span : b * span + side, :LANES], ab[b * span : b * span + side, LANES:]
                w, v = ab[b * span + side : (b + 1) * span, :LANES], ab[b * span + side : (b + 1) * span, LANES:]
                pr, pi, mr, mi = u - v, w + x, u + v, w - x
                ar, ai = p * pr - q * pi, p * pi + q * pr
                br, bi = p2 * mr - q2 * mi, p2 * mi + q2 * mr
                even = jnp.concatenate([ar + br, ai + bi], axis=0).astype(BF16)
                odd = jnp.concatenate([ai - bi, br - ar], axis=0).astype(BF16)
                l_scr[b * span : (b + 1) * span, wide] = jnp.concatenate([even, odd], axis=1)
        back = dot_nt(l_scr[...], tab_ref[...]).astype(BF16)
        for b in range(team):
            done = dot(wz_ref[1], back[b * span : (b + 1) * span])
            for n in range(groups // 2):
                here = slice(n * LANES, (n + 1) * LANES)
                grid[n, pl.ds((g * team + b) * side, side), :] = done[:side, here]
                grid[n, pl.ds((bands + g * team + b) * side, side), :] = done[side:, here]
        return carry

    lax.fori_loop(0, bands // team, planes, 0)

    levels(collect)
    for d in range(groups):
        late = acc[1, d]
        late = jnp.concatenate([late[:, waves - STICK_DEV :], late[:, : waves - STICK_DEV]], axis=1)
        out_refs[d][...] = (acc[0, d] + late).astype(BF16)


def arrange_kernel(groups, me_ref, *refs):
    y_refs, (sorted_ref, rows_scr) = refs[:groups], refs[groups:]
    share = y_refs[0].shape[0] // 2
    half = groups * share
    for shift, y_ref in enumerate(y_refs):
        begin = pl.multiple_of((me_ref[0] ^ shift) * share, 8)
        value = y_ref[...].astype(F32)
        rows_scr[pl.ds(begin, share)] = value[:share]
        rows_scr[pl.ds(begin + half, share)] = value[share:]
    sorted_ref[...] = rows_scr[...].astype(BF16)


def couple_kernel(partner_ref, sorted_ref, g_ref):
    products = dot_nt(partner_ref[...], sorted_ref[...])
    half = products.shape[0] // 2
    g_ref[0] = (products[:half, :half] + products[half:, half:]).astype(BF16)
    g_ref[1] = (products[:half, half:] - products[half:, :half]).astype(BF16)


def unsort_kernel(y_ref, rank_ref, out_ref):
    both, waves = y_ref.shape
    parts = waves // 256
    stacked = jnp.concatenate([y_ref[:, i * 256 : (i + 1) * 256] for i in range(parts)], axis=0)
    for tile in range(parts):
        here = slice(tile * 256, (tile + 1) * 256)
        rank = rank_ref[:, here]
        values = dot(stacked, one_hot(rank & 255, 256))
        total = None
        for part in range(parts):
            value = jnp.where((rank >> 8) == part, values[part * both : (part + 1) * both], 0.0)
            total = value if total is None else total + value
        out_ref[:, here] = total.astype(BF16)


def whole(memory=pltpu.VMEM):
    return pl.BlockSpec(memory_space=memory)


def params(limit=VMEM_LIMIT):
    return pltpu.CompilerParams(vmem_limit_bytes=limit)


def shards(orbitals, box_index, partner_pool, potential):
    fft_count = lax.axis_size("fft")
    side = potential.shape[0]
    bands = orbitals.shape[2]
    waves = orbitals.shape[3]
    share = bands // fft_count
    columns = STICK_DEV * fft_count
    chunks = (side // 2 + 1 + 1) // 2
    coeffs = orbitals.reshape(2 * bands, waves)

    cosine, sine = cos_sin(side)
    cs = jnp.asarray(np.concatenate([cosine, cosine, sine, sine], axis=1))
    inward = np.block([[cosine, -sine], [sine, cosine]])
    outward = np.block([[cosine, sine], [-sine, cosine]])
    wz = jnp.asarray(np.stack([inward, outward]))

    me = lax.axis_index("fft")
    me_row = me.reshape(1)
    pairs = [[(i, i ^ s) for i in range(fft_count)] for s in range(fft_count)]
    pool_count = lax.axis_size("pool")
    rows = 2 * share
    packed = waves + side * STICK_DEV // rows + LANES
    scalars, blocks = whole(pltpu.SMEM), [whole()] * fft_count

    *ordered, ordered_all, rank = pl.pallas_call(
        functools.partial(sort_kernel, side, fft_count),
        out_shape=[jax.ShapeDtypeStruct((rows, packed), BF16)] * fft_count
        + [
            jax.ShapeDtypeStruct((2 * bands, waves), BF16),
            jax.ShapeDtypeStruct((1, waves), jnp.int32),
        ],
        in_specs=[scalars, whole(), whole(pltpu.HBM)],
        out_specs=blocks + [whole(), whole()],
        scratch_shapes=[
            pltpu.VMEM((2 * bands, waves), BF16),
            pltpu.VMEM((waves // 256 * 2 * bands, waves), BF16),
            pltpu.VMEM((waves // 256 * 2 * bands, 256), F32),
            pltpu.SemaphoreType.DMA,
        ],
        compiler_params=params(SORT_LIMIT),
        name="sort_waves",
    )(me_row, box_index.reshape(1, waves), coeffs)
    moved = [ordered[0]] + [lax.ppermute(ordered[s], "fft", pairs[s]) for s in range(1, fft_count)]

    field, cyr, syr, passed = pl.pallas_call(
        functools.partial(field_kernel, side, chunks),
        out_shape=(
            jax.ShapeDtypeStruct((4, side, chunks * LANES), F32),
            jax.ShapeDtypeStruct((side, chunks * LANES), BF16),
            jax.ShapeDtypeStruct((side, chunks * LANES), BF16),
            jax.ShapeDtypeStruct((2 * bands, waves), BF16),
        ),
        in_specs=[whole()] * 3,
        out_specs=(whole(),) * 4,
        compiler_params=params(),
        cost_estimate=pl.CostEstimate(flops=10**9, bytes_accessed=10**7, transcendentals=0),
        name="field_pairs",
    )(potential.reshape(side * side, 2 * side), cs, ordered_all)

    team = min(4, share)
    back = pl.pallas_call(
        functools.partial(box_kernel, side, chunks, team, waves, fft_count),
        out_shape=[jax.ShapeDtypeStruct((rows, waves), BF16)] * fft_count,
        in_specs=blocks + [whole()] * 5,
        out_specs=blocks,
        scratch_shapes=[
            pltpu.VMEM((2, fft_count, rows, waves), BF16),
            pltpu.VMEM((columns // LANES, rows * side, LANES), F32),
            pltpu.VMEM((rows * side, columns), BF16),
            pltpu.VMEM((team * 2 * side, 2 * chunks * LANES), BF16),
            pltpu.VMEM((2, fft_count, rows, waves), F32),
            pltpu.VMEM((columns, 2 * chunks * LANES), BF16),
            pltpu.VMEM((fft_count, side, 2 * STICK_DEV), F32),
            pltpu.VMEM((fft_count, LANES), jnp.int32),
            pltpu.SMEM((fft_count, LANES), jnp.int32),
            pltpu.SemaphoreType.DMA,
        ],
        compiler_params=params(),
        cost_estimate=pl.CostEstimate(flops=10**10, bytes_accessed=10**7, transcendentals=0),
        name="box_work",
    )(*moved, field, cs, cyr, syr, wz)
    spread = lax.all_to_all(
        passed.reshape(pool_count, 2 * bands // pool_count, waves), "pool", 0, 0, tiled=True
    )
    chosen = pl.pallas_call(
        select_kernel,
        out_shape=jax.ShapeDtypeStruct(spread.shape, BF16),
        in_specs=[scalars, whole(pl.ANY)],
        out_specs=whole(pl.ANY),
        scratch_shapes=[pltpu.SemaphoreType.DMA((pool_count,))],
        compiler_params=params(),
        name="select_partner",
    )(partner_pool, spread)
    partner = lax.all_to_all(chosen, "pool", 0, 0, tiled=True).reshape(2 * bands, waves)

    returned = [back[0]] + [lax.ppermute(back[s], "fft", pairs[s]) for s in range(1, fft_count)]

    sorted_response = pl.pallas_call(
        functools.partial(arrange_kernel, fft_count),
        out_shape=jax.ShapeDtypeStruct((2 * bands, waves), BF16),
        in_specs=[scalars] + blocks,
        out_specs=whole(),
        scratch_shapes=[pltpu.VMEM((2 * bands, waves), F32)],
        compiler_params=params(),
        cost_estimate=pl.CostEstimate(flops=ARRANGE_COST, bytes_accessed=10**6, transcendentals=0),
        name="arrange",
    )(me_row, *returned)
    sums = pl.pallas_call(
        couple_kernel,
        out_shape=jax.ShapeDtypeStruct((2, bands, bands), BF16),
        in_specs=[whole(), whole()],
        out_specs=whole(),
        compiler_params=params(),
        name="couple",
    )(partner, sorted_response)
    shares = [sums] + [lax.ppermute(sums, "fft", pairs[s]) for s in range(1, fft_count)]
    response = pl.pallas_call(
        unsort_kernel,
        out_shape=jax.ShapeDtypeStruct((2 * bands, waves), BF16),
        in_specs=[whole(), whole()],
        out_specs=whole(),
        compiler_params=params(),
        cost_estimate=pl.CostEstimate(flops=10**9, bytes_accessed=10**7, transcendentals=0),
        name="unsort",
    )(sorted_response, rank)
    summed = None
    for d in range(fft_count):
        offset = me ^ d
        term = shares[0]
        for s in range(1, fft_count):
            term = jnp.where(offset == s, shares[s], term)
        term = term.astype(F32)
        summed = term if summed is None else summed + term
    coupling = (summed / jnp.sqrt(jnp.float32(waves * fft_count)))[:, None]
    return response.reshape(2, 1, bands, waves), coupling


def solution(mesh):
    placed = (P(None, "pool", None, "fft"), P("fft"), P(), P())
    return jax.shard_map(
        shards,
        mesh=mesh,
        in_specs=placed,
        out_specs=(P(None, "pool", None, "fft"), P(None, "pool", None, None)),
        check_vma=False,
    )
```

```python
import functools

import jax
import jax.numpy as jnp
import ml_dtypes
import numpy as np
from jax import lax
from jax.experimental import pallas as pl
from jax.experimental.pallas import tpu as pltpu
from jax.sharding import PartitionSpec as P

STICK_DEV = 64
LANES = 128
UNROLL = 8
CHUNKS = 2
BF16 = jnp.bfloat16
F32 = jnp.float32
VMEM_LIMIT = 24 * 1024 * 1024
SORT_LIMIT = 60 * 1024 * 1024
ARRANGE_COST = 3*10**9
JOIN_COST = 10**7


def cos_sin(side):
    points = np.arange(side)
    angles = (2.0 * np.pi / side) * (points[:, None] * points[None, :] % side)
    scaling = 1.0 / np.sqrt(side)
    cosine = (np.cos(angles) * scaling).astype(ml_dtypes.bfloat16)
    sine = (np.sin(angles) * scaling).astype(ml_dtypes.bfloat16)
    return cosine, sine


def dot(a, b):
    return jnp.dot(a, b, preferred_element_type=F32)


def dot_nt(a, b):
    return lax.dot_general(a, b, (((1,), (1,)), ((), ())), preferred_element_type=F32)


def one_hot(row, count):
    places = lax.broadcasted_iota(jnp.int32, (count, row.shape[1]), 0)
    return jnp.where(places == row, 1.0, 0.0).astype(BF16)


def triangles(side):
    rows = lax.broadcasted_iota(jnp.int32, (side, side), 0)
    cols = lax.broadcasted_iota(jnp.int32, (side, side), 1)
    upper = jnp.where(rows < cols, 1.0, 0.0).astype(BF16)
    lower = jnp.where(rows > cols, 1.0, 0.0).astype(BF16)
    return upper, lower, jnp.ones((side, side), BF16)


def prefix(occupied, tri):
    upper, lower, ones = tri
    in_rows = dot(occupied, ones).astype(BF16)
    return dot(occupied, upper) + dot(lower, in_rows)


def locate(idx, side):
    bits = side.bit_length() - 1
    tri = triangles(side)
    xh = one_hot(idx >> (2 * bits), side)
    yh = one_hot((idx >> bits) & (side - 1), side)
    zh = one_hot(idx & (side - 1), side)
    columns = jnp.minimum(dot_nt(xh, yh), 1.0).astype(BF16)
    slots = prefix(columns, tri).astype(BF16)
    slot = jnp.sum(xh.astype(F32) * dot(slots, yh), axis=0, keepdims=True)
    ch = one_hot(slot.astype(jnp.int32), STICK_DEV)
    cells = dot_nt(zh, ch)
    ranks = prefix(cells.astype(BF16), tri)
    high = jnp.floor(ranks * (1.0 / side))
    low = ranks - high * side
    looked = dot(high.astype(BF16), ch) * side + dot(low.astype(BF16), ch)
    rank = jnp.sum(zh.astype(F32) * looked, axis=0, keepdims=True)
    return xh, yh, ch, slot, cells, rank.astype(jnp.int32)


def sort_kernel(side, groups, me_ref, idx_ref, x_hbm, *refs):
    outs, (all_ref, rank_ref, x_ref, wide, pieces, sem) = refs[: groups * CHUNKS], refs[groups * CHUNKS :]
    fetch = pltpu.make_async_copy(x_hbm, x_ref, sem)
    fetch.start()
    xh, yh, ch, slot_of, cells, rank = locate(idx_ref[...], side)
    rank_ref[...] = rank
    waves = rank.shape[1]
    both = x_ref.shape[0]
    bands = both // 2
    share = bands // groups
    rows = 2 * share // CHUNKS
    lane = lax.broadcasted_iota(jnp.int32, (STICK_DEV, side), 1).astype(F32)
    cells = jnp.concatenate([cells[i : i + rows] for i in range(0, side, rows)], axis=1)
    slot = lax.broadcasted_iota(jnp.int32, (rows, LANES), 1) // rows
    place = jnp.zeros((rows, LANES), F32)
    count = 0
    for hot in (xh, yh):
        at = jnp.minimum(dot_nt(ch, hot), 1.0)
        value = jnp.sum(at * lane, axis=1, keepdims=True)
        for i in range(0, STICK_DEV, rows):
            place = jnp.where(slot == count, value[i : i + rows], place)
            count += 1
    tiles = waves // LANES
    in_tile = one_hot(rank & (LANES - 1), LANES)
    col = dot_nt(one_hot(rank >> 7, tiles) * slot_of.astype(BF16), in_tile)
    col = [col[i : i + rows] for i in range(0, tiles, rows)]
    extra = jnp.concatenate([cells, place] + col, axis=1).astype(BF16)
    low = one_hot(rank & 255, 256)
    for shift in range(groups):
        outs[shift * CHUNKS][:, waves:] = extra
    fetch.wait()
    parts = waves // 256
    for part in range(parts):
        mask = jnp.where((rank >> 8) == part, 1.0, 0.0).astype(BF16)
        wide[part * both : (part + 1) * both] = x_ref[...] * mask
    pieces[...] = dot_nt(wide[...], low)
    half = share // CHUNKS
    for part in range(parts):
        here = slice(part * 256, (part + 1) * 256)
        all_ref[:, here] = pieces[part * both : (part + 1) * both].astype(BF16)
        for shift in range(groups):
            begin = pl.multiple_of(part * both + (me_ref[0] ^ shift) * share, 8)
            re = pieces[pl.ds(begin, share)]
            im = pieces[pl.ds(begin + bands, share)]
            for c in range(CHUNKS):
                mine = slice(c * half, (c + 1) * half)
                outs[shift * CHUNKS + c][:, here] = jnp.concatenate(
                    [re[mine], im[mine]], axis=0
                ).astype(BF16)


def field_kernel(side, chunks, pot_ref, cs_ref, field_ref, cyr_ref, syr_ref):
    half = side // 2
    left = lax.broadcasted_iota(jnp.int32, (side, LANES), 1) < side
    for ref, begin in ((cyr_ref, 0), (syr_ref, LANES)):
        table = cs_ref[:, begin : begin + side].astype(F32)
        for k in range(chunks):
            ya, yb = (2 * k) % side, (2 * k + 1) % side
            ref[:, k * LANES : (k + 1) * LANES] = jnp.where(
                left, table[:, ya : ya + 1], table[:, yb : yb + 1]
            ).astype(BF16)
    lane = lax.broadcasted_iota(jnp.int32, (side, LANES), 1)
    first = lane < side
    flipped = (lane & side) + ((side - (lane & (side - 1))) & (side - 1))

    def pair(row_a, row_b):
        p = jnp.where(first, row_a, pltpu.roll(row_b, side, 1))
        q = jnp.where(first, pltpu.roll(row_a, side, 1), row_b)
        return p, q

    def plane(y):
        return pot_ref[pl.ds(y, side, stride=side), :]

    def mirror(y):
        if y == 0 or y >= half:
            return jnp.zeros((side, LANES), F32)
        return jnp.take_along_axis(plane(side - y), flipped, axis=1)

    zero = jnp.zeros((side, LANES), F32)
    for k in range(chunks):
        ya, yb = 2 * k, 2 * k + 1
        here = slice(k * LANES, (k + 1) * LANES)
        values = pair(plane(ya), plane(yb) if yb <= half else zero) + pair(mirror(ya), mirror(yb))
        for i, value in enumerate(values):
            field_ref[i, :, here] = value.astype(BF16)


def select_kernel(order_ref, in_ref, out_ref, sems):
    copies = []
    for i in range(out_ref.shape[0]):
        copy = pltpu.make_async_copy(in_ref.at[order_ref[i]], out_ref.at[i], sems.at[i])
        copy.start()
        copies.append(copy)
    for copy in copies:
        copy.wait()


def build_tables(side, chunks, waves, x_refs, cs_ref, cyr_ref, syr_ref, tab_ref, spot_ref, col_ref, start_ref):
    rows = x_refs[0].shape[0]
    parts = side // rows
    tiles = waves // LANES
    cells_end = waves + parts * STICK_DEV
    tri = triangles(side)
    lane_f = lax.broadcasted_iota(jnp.int32, (STICK_DEV, side), 1).astype(F32)
    ahead = jnp.where(
        lax.broadcasted_iota(jnp.int32, (side, LANES), 0)
        < lax.broadcasted_iota(jnp.int32, (side, LANES), 1),
        1.0, 0.0,
    ).astype(BF16)
    left = lax.broadcasted_iota(jnp.int32, (tiles, LANES), 1) < STICK_DEV
    at_x, at_y = [], []
    for d, x_ref in enumerate(x_refs):
        cells = jnp.concatenate(
            [x_ref[:, waves + i * STICK_DEV : waves + (i + 1) * STICK_DEV].astype(F32) for i in range(parts)],
            axis=0,
        )
        place = x_ref[:, cells_end : cells_end + LANES].astype(F32)
        for which, hots in enumerate((at_x, at_y)):
            value = jnp.concatenate(
                [place[:, i * rows : i * rows + 1] for i in range(which * parts, (which + 1) * parts)],
                axis=0,
            )
            hots.append(jnp.where(lane_f == value, 1.0, 0.0))
        ranks = prefix(cells.astype(BF16), tri)
        begins = jnp.minimum(jnp.floor(ranks[:, :1] * (1.0 / STICK_DEV)), waves // STICK_DEV - 1.0)
        spot = jnp.where(cells > 0.5, ranks - begins * STICK_DEV, -1.0)
        spot_ref[d] = jnp.concatenate([spot, spot], axis=1)
        level = dot_nt(jnp.ones((8, STICK_DEV), BF16), cells.astype(BF16))
        start_ref[d : d + 1, :] = dot(level.astype(BF16), ahead)[:1].astype(jnp.int32)
        begin = cells_end + LANES
        col = jnp.concatenate(
            [x_ref[:, begin + i * LANES : begin + (i + 1) * LANES].astype(F32) for i in range(tiles // rows)],
            axis=0,
        ) + float((d % 2) * STICK_DEV)
        turned = pltpu.roll(col, STICK_DEV, 1)
        after = jnp.concatenate([turned[1:], turned[:1]], axis=0)
        col_ref[0, d] = col.astype(jnp.int32)
        col_ref[1, d] = jnp.where(left, turned, after).astype(jnp.int32)
    at_x = jnp.concatenate(at_x, axis=0).astype(BF16)
    at_y = jnp.concatenate(at_y, axis=0).astype(BF16)
    both = dot(at_x, cs_ref[...])
    cx, sx = both[:, :LANES], both[:, LANES:]
    for k in range(chunks):
        cy = dot(at_y, cyr_ref[:, k * LANES : (k + 1) * LANES])
        sy = dot(at_y, syr_ref[:, k * LANES : (k + 1) * LANES])
        base = 2 * k * LANES
        tab_ref[:, base : base + LANES] = (cy * cx - sy * sx).astype(BF16)
        tab_ref[:, base + LANES : base + 2 * LANES] = (cy * sx + sy * cx).astype(BF16)


def box_first_kernel(side, chunks, team, waves, groups, *refs):
    x_refs, refs = refs[:groups], refs[groups:]
    (field_ref, cs_ref, cyr_ref, syr_ref, wz_ref), refs = refs[:5], refs[5:]
    out_refs, refs = refs[:groups], refs[groups:]
    (tab_ref, spot_ref, col_ref, start_ref), refs = refs[:4], refs[4:]
    *scratch, start_s, sem = refs
    build_tables(
        side, chunks, waves, x_refs, cs_ref, cyr_ref, syr_ref, tab_ref, spot_ref, col_ref, start_ref
    )
    to_scalars = pltpu.make_async_copy(start_ref, start_s, sem)
    to_scalars.start()
    to_scalars.wait()
    box_work(
        side, chunks, team, waves, x_refs, field_ref, wz_ref, tab_ref, spot_ref, col_ref, start_s,
        out_refs, *scratch,
    )


def box_next_kernel(side, chunks, team, waves, groups, *refs):
    x_refs, refs = refs[:groups], refs[groups:]
    (field_ref, wz_ref, tab_ref, spot_ref, col_ref, start_s), refs = refs[:6], refs[6:]
    out_refs, scratch = refs[:groups], refs[groups:]
    box_work(
        side, chunks, team, waves, x_refs, field_ref, wz_ref, tab_ref, spot_ref, col_ref, start_s,
        out_refs, *scratch,
    )


def box_work(
    side, chunks, team, waves, x_refs, field_ref, wz_ref, tab_ref, spot_ref, col_ref, start_s,
    out_refs, xf, grid, t_scr, l_scr, acc,
):
    groups = len(x_refs)
    rows = x_refs[0].shape[0]
    bands = rows // 2
    blocks = rows // 8
    span = 2 * side
    for d in range(groups):
        value = x_refs[d][:, :waves].astype(F32)
        xf[0, d] = value
        xf[1, d] = jnp.concatenate([value[:, STICK_DEV:], value[:, :STICK_DEV]], axis=1)
        acc[0, d] = jnp.zeros((rows, waves), F32)
        acc[1, d] = jnp.zeros((rows, waves), F32)
    lane = lax.broadcasted_iota(jnp.int32, (8, LANES), 1)
    left = lane < STICK_DEV

    def window(z, d):
        begin = jnp.minimum(start_s[d, z] >> 6, waves // STICK_DEV - 1)
        tile = begin >> 1
        return begin & 1, tile, pl.ds(pl.multiple_of(tile * LANES, LANES), LANES), begin * STICK_DEV

    def expand(z):
        for dp in range(groups // 2):
            spot = jnp.where(
                left,
                jnp.broadcast_to(spot_ref[2 * dp, pl.ds(z, 1), :], (8, LANES)),
                jnp.broadcast_to(spot_ref[2 * dp + 1, pl.ds(z, 1), :], (8, LANES)),
            )
            valid = spot >= 0.0
            at = jnp.maximum(spot, 0.0).astype(jnp.int32)
            odd_a, _, lanes_a, _ = window(z, 2 * dp)
            odd_b, _, lanes_b, _ = window(z, 2 * dp + 1)
            for block in range(blocks):
                part = slice(block * 8, (block + 1) * 8)
                a = jnp.take_along_axis(xf[odd_a, 2 * dp, part, lanes_a], at, axis=1)
                b = jnp.take_along_axis(xf[odd_b, 2 * dp + 1, part, lanes_b], at, axis=1)
                value = jnp.where(valid, jnp.where(left, a, b), 0.0)
                grid[dp, pl.ds(block * 8 * side + z, 8, stride=side), :] = value

    def collect(z):
        for dp in range(groups // 2):
            sources = [
                grid[dp, pl.ds(block * 8 * side + z, 8, stride=side), :] for block in range(blocks)
            ]
            for d in (2 * dp, 2 * dp + 1):
                odd, tile, lanes, base = window(z, d)
                at = jnp.broadcast_to(col_ref[odd, d, pl.ds(tile, 1), :], (8, LANES))
                mask = (lane >= start_s[d, z] - base) & (lane < start_s[d, z + 1] - base)
                for block in range(blocks):
                    part = slice(block * 8, (block + 1) * 8)
                    value = jnp.take_along_axis(sources[block], at, axis=1)
                    acc[odd, d, part, lanes] = jnp.where(mask, value, acc[odd, d, part, lanes])

    def levels(step):
        def body(i, carry):
            for j in range(UNROLL):
                step(i * UNROLL + j)
            return carry

        lax.fori_loop(0, side // UNROLL, body, 0)

    levels(expand)

    def depth_in(b, carry):
        both = jnp.concatenate(
            [
                jnp.concatenate(
                    [grid[n, pl.ds(b * side, side), :], grid[n, pl.ds((bands + b) * side, side), :]],
                    axis=0,
                )
                for n in range(groups // 2)
            ],
            axis=1,
        ).astype(BF16)
        t_scr[pl.ds(b * span, span), :] = dot(wz_ref[0], both).astype(BF16)
        return carry

    lax.fori_loop(0, bands, depth_in, 0)

    def planes(g, carry):
        rows_g = pl.ds(g * team * span, team * span)
        sticks = t_scr[rows_g, :]
        for k in range(chunks):
            here = slice(k * LANES, (k + 1) * LANES)
            wide = slice(2 * k * LANES, 2 * (k + 1) * LANES)
            ab = dot(sticks, tab_ref[:, wide])
            p, q = field_ref[0, :, here], field_ref[1, :, here]
            p2, q2 = field_ref[2, :, here], field_ref[3, :, here]
            for b in range(team):
                u, x = ab[b * span : b * span + side, :LANES], ab[b * span : b * span + side, LANES:]
                w, v = ab[b * span + side : (b + 1) * span, :LANES], ab[b * span + side : (b + 1) * span, LANES:]
                pr, pi, mr, mi = [t.astype(BF16) for t in (u - v, w + x, u + v, w - x)]
                ar, ai = p * pr - q * pi, p * pi + q * pr
                br, bi = p2 * mr - q2 * mi, p2 * mi + q2 * mr
                even = jnp.concatenate([ar + br, ai + bi], axis=0)
                odd = jnp.concatenate([ai - bi, br - ar], axis=0)
                l_scr[b * span : (b + 1) * span, wide] = jnp.concatenate([even, odd], axis=1)
        back = dot_nt(l_scr[...], tab_ref[...]).astype(BF16)
        for b in range(team):
            done = dot(wz_ref[1], back[b * span : (b + 1) * span])
            for n in range(groups // 2):
                here = slice(n * LANES, (n + 1) * LANES)
                grid[n, pl.ds((g * team + b) * side, side), :] = done[:side, here]
                grid[n, pl.ds((bands + g * team + b) * side, side), :] = done[side:, here]
        return carry

    lax.fori_loop(0, bands // team, planes, 0)

    levels(collect)
    for d in range(groups):
        late = acc[1, d]
        late = jnp.concatenate([late[:, waves - STICK_DEV :], late[:, : waves - STICK_DEV]], axis=1)
        out_refs[d][...] = (acc[0, d] + late).astype(BF16)


def arrange_kernel(groups, me_ref, *refs):
    y_refs, (rows_ref,) = refs[:groups], refs[groups:]
    part = y_refs[0].shape[0] // 2
    half = groups * part
    me = me_ref[0]
    for j in range(groups // 2):
        one, other = y_refs[2 * j][...].astype(F32), y_refs[2 * j + 1][...].astype(F32)
        low = jnp.where((me & 1) == 0, one, other)
        high = jnp.where((me & 1) == 0, other, one)
        begin = pl.multiple_of(((me >> 1) ^ j) * (2 * part), 8)
        rows_ref[pl.ds(begin, 2 * part)] = jnp.concatenate([low[:part], high[:part]], axis=0)
        rows_ref[pl.ds(begin + half, 2 * part)] = jnp.concatenate([low[part:], high[part:]], axis=0)


def join_kernel(groups, me_ref, *refs):
    rows_refs, refs = refs[: CHUNKS - 1], refs[CHUNKS - 1 :]
    sorted_ref, rows_scr = refs[groups:]
    arrange_kernel(groups, me_ref, *refs[:groups], rows_scr)
    values = [ref[...] for ref in (*rows_refs, rows_scr)]
    part = values[0].shape[0] // (2 * groups)
    sorted_ref[...] = jnp.concatenate(
        [v[i * part : (i + 1) * part] for i in range(2 * groups) for v in values], axis=0
    ).astype(BF16)


def couple_kernel(partner_ref, sorted_ref, g_ref):
    products = dot_nt(partner_ref[...], sorted_ref[...])
    half = products.shape[0] // 2
    g_ref[0] = (products[:half, :half] + products[half:, half:]).astype(BF16)
    g_ref[1] = (products[:half, half:] - products[half:, :half]).astype(BF16)


def unsort_kernel(y_ref, rank_ref, out_ref):
    both, waves = y_ref.shape
    parts = waves // 256
    stacked = jnp.concatenate([y_ref[:, i * 256 : (i + 1) * 256] for i in range(parts)], axis=0)
    for tile in range(parts):
        here = slice(tile * 256, (tile + 1) * 256)
        rank = rank_ref[:, here]
        values = dot(stacked, one_hot(rank & 255, 256))
        total = None
        for part in range(parts):
            value = jnp.where((rank >> 8) == part, values[part * both : (part + 1) * both], 0.0)
            total = value if total is None else total + value
        out_ref[:, here] = total.astype(BF16)


def whole(memory=pltpu.VMEM):
    return pl.BlockSpec(memory_space=memory)


def params(limit=VMEM_LIMIT):
    return pltpu.CompilerParams(vmem_limit_bytes=limit)


def shards(orbitals, box_index, partner_pool, potential):
    fft_count = lax.axis_size("fft")
    side = potential.shape[0]
    bands = orbitals.shape[2]
    waves = orbitals.shape[3]
    share = bands // fft_count
    columns = STICK_DEV * fft_count
    chunks = (side // 2 + 1 + 1) // 2
    coeffs = orbitals.reshape(2 * bands, waves)

    cosine, sine = cos_sin(side)
    cs = jnp.asarray(np.concatenate([cosine, cosine, sine, sine], axis=1))
    inward = np.block([[cosine, -sine], [sine, cosine]])
    outward = np.block([[cosine, sine], [-sine, cosine]])
    wz = jnp.asarray(np.stack([inward, outward]))

    me = lax.axis_index("fft")
    me_row = me.reshape(1)
    pairs = [[(i, i ^ s) for i in range(fft_count)] for s in range(fft_count)]
    pool_count = lax.axis_size("pool")
    rows = 2 * share // CHUNKS
    tiles = waves // LANES
    packed = waves + side * STICK_DEV // rows + LANES + tiles * LANES // rows
    scalars, blocks = whole(pltpu.SMEM), [whole()] * fft_count

    *ordered, ordered_all, rank = pl.pallas_call(
        functools.partial(sort_kernel, side, fft_count),
        out_shape=[
            jax.ShapeDtypeStruct((rows, waves if c else packed), BF16)
            for _ in range(fft_count)
            for c in range(CHUNKS)
        ]
        + [
            jax.ShapeDtypeStruct((2 * bands, waves), BF16),
            jax.ShapeDtypeStruct((1, waves), jnp.int32),
        ],
        in_specs=[scalars, whole(), whole(pltpu.HBM)],
        out_specs=blocks * CHUNKS + [whole(), whole()],
        scratch_shapes=[
            pltpu.VMEM((2 * bands, waves), BF16),
            pltpu.VMEM((waves // 256 * 2 * bands, waves), BF16),
            pltpu.VMEM((waves // 256 * 2 * bands, 256), F32),
            pltpu.SemaphoreType.DMA,
        ],
        compiler_params=params(SORT_LIMIT),
        name="sort_waves",
    )(me_row, box_index.reshape(1, waves), coeffs)
    moved = [
        [ordered[c]] + [lax.ppermute(ordered[s * CHUNKS + c], "fft", pairs[s]) for s in range(1, fft_count)]
        for c in range(CHUNKS)
    ]

    field, cyr, syr = pl.pallas_call(
        functools.partial(field_kernel, side, chunks),
        out_shape=(
            jax.ShapeDtypeStruct((4, side, chunks * LANES), BF16),
            jax.ShapeDtypeStruct((side, chunks * LANES), BF16),
            jax.ShapeDtypeStruct((side, chunks * LANES), BF16),
        ),
        in_specs=[whole()] * 2,
        out_specs=(whole(),) * 3,
        compiler_params=params(),
        cost_estimate=pl.CostEstimate(flops=10**9, bytes_accessed=10**7, transcendentals=0),
        name="field_pairs",
    )(potential.reshape(side * side, 2 * side), cs)

    team = min(4, rows // 2)
    scratch = [
        pltpu.VMEM((2, fft_count, rows, waves), F32),
        pltpu.VMEM((columns // LANES, rows * side, LANES), F32),
        pltpu.VMEM((rows * side, columns), BF16),
        pltpu.VMEM((team * 2 * side, 2 * chunks * LANES), BF16),
        pltpu.VMEM((2, fft_count, rows, waves), F32),
    ]
    cost = pl.CostEstimate(flops=10**10, bytes_accessed=10**7, transcendentals=0)
    shapes = [jax.ShapeDtypeStruct((rows, waves), BF16)] * fft_count
    *back, tab, spot, col, start = pl.pallas_call(
        functools.partial(box_first_kernel, side, chunks, team, waves, fft_count),
        out_shape=shapes
        + [
            jax.ShapeDtypeStruct((columns, 2 * chunks * LANES), BF16),
            jax.ShapeDtypeStruct((fft_count, side, 2 * STICK_DEV), F32),
            jax.ShapeDtypeStruct((2, fft_count, tiles, LANES), jnp.int32),
            jax.ShapeDtypeStruct((fft_count, LANES), jnp.int32),
        ],
        in_specs=blocks + [whole()] * 5,
        out_specs=blocks + [whole()] * 4,
        scratch_shapes=scratch
        + [pltpu.SMEM((fft_count, LANES), jnp.int32), pltpu.SemaphoreType.DMA],
        compiler_params=params(),
        cost_estimate=cost,
        name="box_first",
    )(*moved[0], field, cs, cyr, syr, wz)
    returned = [[back[0]] + [lax.ppermute(back[s], "fft", pairs[s]) for s in range(1, fft_count)]]
    for c in range(1, CHUNKS):
        back = pl.pallas_call(
            functools.partial(box_next_kernel, side, chunks, team, waves, fft_count),
            out_shape=shapes,
            in_specs=blocks + [whole()] * 5 + [scalars],
            out_specs=blocks,
            scratch_shapes=scratch,
            compiler_params=params(),
            cost_estimate=cost,
            name="box_next",
        )(*moved[c], field, wz, tab, spot, col, start)
        returned.append(
            [back[0]] + [lax.ppermute(back[s], "fft", pairs[s]) for s in range(1, fft_count)]
        )

    spread = lax.all_to_all(
        ordered_all.reshape(pool_count, 2 * bands // pool_count, waves), "pool", 0, 0, tiled=True
    )
    chosen = pl.pallas_call(
        select_kernel,
        out_shape=jax.ShapeDtypeStruct(spread.shape, BF16),
        in_specs=[scalars, whole(pl.ANY)],
        out_specs=whole(pl.ANY),
        scratch_shapes=[pltpu.SemaphoreType.DMA((pool_count,))],
        compiler_params=params(),
        name="select_partner",
    )(partner_pool, spread)
    partner = lax.all_to_all(chosen, "pool", 0, 0, tiled=True).reshape(2 * bands, waves)

    arranged = [
        pl.pallas_call(
            functools.partial(arrange_kernel, fft_count),
            out_shape=jax.ShapeDtypeStruct((rows * fft_count, waves), F32),
            in_specs=[scalars] + blocks,
            out_specs=whole(),
            compiler_params=params(),
            cost_estimate=pl.CostEstimate(
                flops=ARRANGE_COST, bytes_accessed=10**6, transcendentals=0
            ),
            name="arrange",
        )(me_row, *returned[c])
        for c in range(CHUNKS - 1)
    ]
    sorted_response = pl.pallas_call(
        functools.partial(join_kernel, fft_count),
        out_shape=jax.ShapeDtypeStruct((2 * bands, waves), BF16),
        in_specs=[scalars] + [whole()] * (CHUNKS - 1) + blocks,
        out_specs=whole(),
        scratch_shapes=[pltpu.VMEM((rows * fft_count, waves), F32)],
        compiler_params=params(),
        cost_estimate=pl.CostEstimate(flops=JOIN_COST, bytes_accessed=10**6, transcendentals=0),
        name="join",
    )(me_row, *arranged, *returned[-1])
    sums = pl.pallas_call(
        couple_kernel,
        out_shape=jax.ShapeDtypeStruct((2, bands, bands), BF16),
        in_specs=[whole(), whole()],
        out_specs=whole(),
        compiler_params=params(),
        name="couple",
    )(partner, sorted_response)
    shares = [sums] + [lax.ppermute(sums, "fft", pairs[s]) for s in range(1, fft_count)]
    response = pl.pallas_call(
        unsort_kernel,
        out_shape=jax.ShapeDtypeStruct((2 * bands, waves), BF16),
        in_specs=[whole(), whole()],
        out_specs=whole(),
        compiler_params=params(),
        cost_estimate=pl.CostEstimate(flops=10**9, bytes_accessed=10**7, transcendentals=0),
        name="unsort",
    )(sorted_response, rank)
    summed = None
    for d in range(fft_count):
        offset = me ^ d
        term = shares[0]
        for s in range(1, fft_count):
            term = jnp.where(offset == s, shares[s], term)
        term = term.astype(F32)
        summed = term if summed is None else summed + term
    coupling = (summed / jnp.sqrt(jnp.float32(waves * fft_count)))[:, None]
    return response.reshape(2, 1, bands, waves), coupling


def solution(mesh):
    placed = (P(None, "pool", None, "fft"), P("fft"), P(), P())
    return jax.shard_map(
        shards,
        mesh=mesh,
        in_specs=placed,
        out_specs=(P(None, "pool", None, "fft"), P(None, "pool", None, None)),
        check_vma=False,
    )
```

```python
import functools

import jax
import jax.numpy as jnp
import ml_dtypes
import numpy as np
from jax import lax
from jax.experimental import pallas as pl
from jax.experimental.pallas import tpu as pltpu
from jax.sharding import PartitionSpec as P

STICK_DEV = 64
LANES = 128
UNROLL = 8
CHUNKS = 1
BF16 = jnp.bfloat16
F32 = jnp.float32
VMEM_LIMIT = 24 * 1024 * 1024
SORT_LIMIT = 60 * 1024 * 1024
ARRANGE_COST = 3*10**9
JOIN_COST = 10**7


def cos_sin(side):
    points = np.arange(side)
    angles = (2.0 * np.pi / side) * (points[:, None] * points[None, :] % side)
    scaling = 1.0 / np.sqrt(side)
    cosine = (np.cos(angles) * scaling).astype(ml_dtypes.bfloat16)
    sine = (np.sin(angles) * scaling).astype(ml_dtypes.bfloat16)
    return cosine, sine


def dot(a, b):
    return jnp.dot(a, b, preferred_element_type=F32)


def dot_nt(a, b):
    return lax.dot_general(a, b, (((1,), (1,)), ((), ())), preferred_element_type=F32)


def one_hot(row, count):
    places = lax.broadcasted_iota(jnp.int32, (count, row.shape[1]), 0)
    return jnp.where(places == row, 1.0, 0.0).astype(BF16)


def triangles(side):
    rows = lax.broadcasted_iota(jnp.int32, (side, side), 0)
    cols = lax.broadcasted_iota(jnp.int32, (side, side), 1)
    upper = jnp.where(rows < cols, 1.0, 0.0).astype(BF16)
    lower = jnp.where(rows > cols, 1.0, 0.0).astype(BF16)
    return upper, lower, jnp.ones((side, side), BF16)


def prefix(occupied, tri):
    upper, lower, ones = tri
    in_rows = dot(occupied, ones).astype(BF16)
    return dot(occupied, upper) + dot(lower, in_rows)


def locate(idx, side):
    bits = side.bit_length() - 1
    tri = triangles(side)
    xh = one_hot(idx >> (2 * bits), side)
    yh = one_hot((idx >> bits) & (side - 1), side)
    zh = one_hot(idx & (side - 1), side)
    columns = jnp.minimum(dot_nt(xh, yh), 1.0).astype(BF16)
    slots = prefix(columns, tri).astype(BF16)
    slot = jnp.sum(xh.astype(F32) * dot(slots, yh), axis=0, keepdims=True)
    ch = one_hot(slot.astype(jnp.int32), STICK_DEV)
    cells = dot_nt(zh, ch)
    ranks = prefix(cells.astype(BF16), tri)
    high = jnp.floor(ranks * (1.0 / side))
    low = ranks - high * side
    looked = dot(high.astype(BF16), ch) * side + dot(low.astype(BF16), ch)
    rank = jnp.sum(zh.astype(F32) * looked, axis=0, keepdims=True)
    return xh, yh, ch, slot, cells, rank.astype(jnp.int32)


def sort_kernel(side, groups, me_ref, idx_ref, x_hbm, *refs):
    outs, (all_ref, rank_ref, x_ref, wide, pieces, sem) = refs[: groups * CHUNKS], refs[groups * CHUNKS :]
    fetch = pltpu.make_async_copy(x_hbm, x_ref, sem)
    fetch.start()
    xh, yh, ch, slot_of, cells, rank = locate(idx_ref[...], side)
    rank_ref[...] = rank
    waves = rank.shape[1]
    both = x_ref.shape[0]
    bands = both // 2
    share = bands // groups
    rows = 2 * share // CHUNKS
    cells = jnp.concatenate([cells[i : i + rows] for i in range(0, side, rows)], axis=1)
    tiles = waves // LANES
    in_tile = one_hot(rank & (LANES - 1), LANES)
    col = dot_nt(one_hot(rank >> 7, tiles) * slot_of.astype(BF16), in_tile)
    steps = lax.broadcasted_iota(jnp.int32, (8, side), 1).astype(F32).astype(BF16)
    place = [dot_nt(steps, jnp.minimum(dot_nt(ch, hot), 1.0).astype(BF16)) for hot in (xh, yh)]
    lines = [col, jnp.concatenate(place, axis=1)]
    spare = -(tiles + 8) % rows
    if spare:
        lines.append(jnp.zeros((spare, LANES), F32))
    lines = jnp.concatenate(lines, axis=0)
    lines = [lines[i : i + rows] for i in range(0, lines.shape[0], rows)]
    extra = jnp.concatenate([cells] + lines, axis=1).astype(BF16)
    low = one_hot(rank & 255, 256)
    for shift in range(groups):
        outs[shift * CHUNKS][:, waves:] = extra
    fetch.wait()
    parts = waves // 256
    for part in range(parts):
        mask = jnp.where((rank >> 8) == part, 1.0, 0.0).astype(BF16)
        wide[part * both : (part + 1) * both] = x_ref[...] * mask
    pieces[...] = dot_nt(wide[...], low)
    half = share // CHUNKS
    for part in range(parts):
        here = slice(part * 256, (part + 1) * 256)
        all_ref[:, here] = pieces[part * both : (part + 1) * both].astype(BF16)
        for shift in range(groups):
            begin = pl.multiple_of(part * both + (me_ref[0] ^ shift) * share, 8)
            re = pieces[pl.ds(begin, share)]
            im = pieces[pl.ds(begin + bands, share)]
            for c in range(CHUNKS):
                mine = slice(c * half, (c + 1) * half)
                outs[shift * CHUNKS + c][:, here] = jnp.concatenate(
                    [re[mine], im[mine]], axis=0
                ).astype(BF16)


def field_kernel(side, chunks, pot_ref, cs_ref, field_ref, cyr_ref, syr_ref):
    half = side // 2
    left = lax.broadcasted_iota(jnp.int32, (side, LANES), 1) < side
    for ref, begin in ((cyr_ref, 0), (syr_ref, LANES)):
        table = cs_ref[:, begin : begin + side].astype(F32)
        for k in range(chunks):
            ya, yb = (2 * k) % side, (2 * k + 1) % side
            ref[:, k * LANES : (k + 1) * LANES] = jnp.where(
                left, table[:, ya : ya + 1], table[:, yb : yb + 1]
            ).astype(BF16)
    lane = lax.broadcasted_iota(jnp.int32, (side, LANES), 1)
    first = lane < side
    flipped = (lane & side) + ((side - (lane & (side - 1))) & (side - 1))

    def pair(row_a, row_b):
        p = jnp.where(first, row_a, pltpu.roll(row_b, side, 1))
        q = jnp.where(first, pltpu.roll(row_a, side, 1), row_b)
        return p, q

    def plane(y):
        return pot_ref[pl.ds(y, side, stride=side), :]

    def mirror(y):
        if y == 0 or y >= half:
            return jnp.zeros((side, LANES), F32)
        return jnp.take_along_axis(plane(side - y), flipped, axis=1)

    zero = jnp.zeros((side, LANES), F32)
    for k in range(chunks):
        ya, yb = 2 * k, 2 * k + 1
        here = slice(k * LANES, (k + 1) * LANES)
        values = pair(plane(ya), plane(yb) if yb <= half else zero) + pair(mirror(ya), mirror(yb))
        for i, value in enumerate(values):
            field_ref[i, :, here] = value.astype(BF16)


def select_kernel(order_ref, in_ref, out_ref, sems):
    copies = []
    for i in range(out_ref.shape[0]):
        copy = pltpu.make_async_copy(in_ref.at[order_ref[i]], out_ref.at[i], sems.at[i])
        copy.start()
        copies.append(copy)
    for copy in copies:
        copy.wait()


def build_tables(side, chunks, waves, x_refs, cs_ref, cyr_ref, syr_ref, tab_ref, spot_ref, col_ref, start_ref):
    rows = x_refs[0].shape[0]
    parts = side // rows
    tiles = waves // LANES
    cells_end = waves + parts * STICK_DEV
    tri = triangles(side)
    ahead = jnp.where(
        lax.broadcasted_iota(jnp.int32, (side, LANES), 0)
        < lax.broadcasted_iota(jnp.int32, (side, LANES), 1),
        1.0, 0.0,
    ).astype(BF16)
    left = lax.broadcasted_iota(jnp.int32, (tiles, LANES), 1) < STICK_DEV
    at_x, at_y = [], []
    for d, x_ref in enumerate(x_refs):
        cells = jnp.concatenate(
            [x_ref[:, waves + i * STICK_DEV : waves + (i + 1) * STICK_DEV].astype(F32) for i in range(parts)],
            axis=0,
        )
        lines = jnp.concatenate(
            [
                x_ref[:, i : i + LANES].astype(F32)
                for i in range(cells_end, cells_end + -(-(tiles + 8) // rows) * LANES, LANES)
            ],
            axis=0,
        )
        place = lines[tiles : tiles + 1].astype(jnp.int32)
        at_x.append(one_hot(place[:, :side], side).astype(F32).T)
        at_y.append(one_hot(place[:, side:], side).astype(F32).T)
        ranks = prefix(cells.astype(BF16), tri)
        begins = jnp.minimum(jnp.floor(ranks[:, :1] * (1.0 / STICK_DEV)), waves // STICK_DEV - 1.0)
        spot = jnp.where(cells > 0.5, ranks - begins * STICK_DEV, -1.0)
        spot_ref[d] = jnp.concatenate([spot, spot], axis=1)
        level = dot_nt(jnp.ones((8, STICK_DEV), BF16), cells.astype(BF16))
        start_ref[d : d + 1, :] = dot(level.astype(BF16), ahead)[:1].astype(jnp.int32)
        col = lines[:tiles] + float((d % 2) * STICK_DEV)
        turned = pltpu.roll(col, STICK_DEV, 1)
        after = jnp.concatenate([turned[1:], turned[:1]], axis=0)
        col_ref[0, d] = col.astype(jnp.int32)
        col_ref[1, d] = jnp.where(left, turned, after).astype(jnp.int32)
    at_x = jnp.concatenate(at_x, axis=0).astype(BF16)
    at_y = jnp.concatenate(at_y, axis=0).astype(BF16)
    both = dot(at_x, cs_ref[...])
    cx, sx = both[:, :LANES], both[:, LANES:]
    for k in range(chunks):
        cy = dot(at_y, cyr_ref[:, k * LANES : (k + 1) * LANES])
        sy = dot(at_y, syr_ref[:, k * LANES : (k + 1) * LANES])
        base = 2 * k * LANES
        tab_ref[:, base : base + LANES] = (cy * cx - sy * sx).astype(BF16)
        tab_ref[:, base + LANES : base + 2 * LANES] = (cy * sx + sy * cx).astype(BF16)


def box_first_kernel(side, chunks, team, waves, groups, *refs):
    x_refs, refs = refs[:groups], refs[groups:]
    (field_ref, cs_ref, cyr_ref, syr_ref, wz_ref), refs = refs[:5], refs[5:]
    out_refs, refs = refs[:groups], refs[groups:]
    (tab_ref, spot_ref, col_ref, start_ref), refs = refs[:4], refs[4:]
    *scratch, start_s, sem = refs
    build_tables(
        side, chunks, waves, x_refs, cs_ref, cyr_ref, syr_ref, tab_ref, spot_ref, col_ref, start_ref
    )
    to_scalars = pltpu.make_async_copy(start_ref, start_s, sem)
    to_scalars.start()
    to_scalars.wait()
    box_work(
        side, chunks, team, waves, x_refs, field_ref, wz_ref, tab_ref, spot_ref, col_ref, start_s,
        out_refs, *scratch,
    )


def box_next_kernel(side, chunks, team, waves, groups, *refs):
    x_refs, refs = refs[:groups], refs[groups:]
    (field_ref, wz_ref, tab_ref, spot_ref, col_ref, start_s), refs = refs[:6], refs[6:]
    out_refs, scratch = refs[:groups], refs[groups:]
    box_work(
        side, chunks, team, waves, x_refs, field_ref, wz_ref, tab_ref, spot_ref, col_ref, start_s,
        out_refs, *scratch,
    )


def box_work(
    side, chunks, team, waves, x_refs, field_ref, wz_ref, tab_ref, spot_ref, col_ref, start_s,
    out_refs, xf, grid, t_scr, l_scr, acc,
):
    groups = len(x_refs)
    rows = x_refs[0].shape[0]
    bands = rows // 2
    blocks = rows // 8
    span = 2 * side
    for d in range(groups):
        value = x_refs[d][:, :waves].astype(F32)
        xf[0, d] = value
        xf[1, d] = jnp.concatenate([value[:, STICK_DEV:], value[:, :STICK_DEV]], axis=1)
        acc[0, d] = jnp.zeros((rows, waves), F32)
        acc[1, d] = jnp.zeros((rows, waves), F32)
    lane = lax.broadcasted_iota(jnp.int32, (8, LANES), 1)
    left = lane < STICK_DEV

    def window(z, d):
        begin = jnp.minimum(start_s[d, z] >> 6, waves // STICK_DEV - 1)
        tile = begin >> 1
        return begin & 1, tile, pl.ds(pl.multiple_of(tile * LANES, LANES), LANES), begin * STICK_DEV

    def expand(z):
        for dp in range(groups // 2):
            spot = jnp.where(
                left,
                jnp.broadcast_to(spot_ref[2 * dp, pl.ds(z, 1), :], (8, LANES)),
                jnp.broadcast_to(spot_ref[2 * dp + 1, pl.ds(z, 1), :], (8, LANES)),
            )
            valid = spot >= 0.0
            at = jnp.maximum(spot, 0.0).astype(jnp.int32)
            odd_a, _, lanes_a, _ = window(z, 2 * dp)
            odd_b, _, lanes_b, _ = window(z, 2 * dp + 1)
            for block in range(blocks):
                part = slice(block * 8, (block + 1) * 8)
                a = jnp.take_along_axis(xf[odd_a, 2 * dp, part, lanes_a], at, axis=1)
                b = jnp.take_along_axis(xf[odd_b, 2 * dp + 1, part, lanes_b], at, axis=1)
                value = jnp.where(valid, jnp.where(left, a, b), 0.0)
                grid[dp, pl.ds(block * 8 * side + z, 8, stride=side), :] = value

    def collect(z):
        for dp in range(groups // 2):
            sources = [
                grid[dp, pl.ds(block * 8 * side + z, 8, stride=side), :] for block in range(blocks)
            ]
            for d in (2 * dp, 2 * dp + 1):
                odd, tile, lanes, base = window(z, d)
                at = jnp.broadcast_to(col_ref[odd, d, pl.ds(tile, 1), :], (8, LANES))
                mask = (lane >= start_s[d, z] - base) & (lane < start_s[d, z + 1] - base)
                for block in range(blocks):
                    part = slice(block * 8, (block + 1) * 8)
                    value = jnp.take_along_axis(sources[block], at, axis=1)
                    acc[odd, d, part, lanes] = jnp.where(mask, value, acc[odd, d, part, lanes])

    def levels(step):
        def body(i, carry):
            for j in range(UNROLL):
                step(i * UNROLL + j)
            return carry

        lax.fori_loop(0, side // UNROLL, body, 0)

    levels(expand)

    def depth_in(g, carry):
        for b in [g * team + i for i in range(team)]:
            both = jnp.concatenate(
                [
                    jnp.concatenate(
                        [
                            grid[n, pl.ds(b * side, side), :].astype(BF16),
                            grid[n, pl.ds((bands + b) * side, side), :].astype(BF16),
                        ],
                        axis=0,
                    )
                    for n in range(groups // 2)
                ],
                axis=1,
            )
            t_scr[pl.ds(b * span, span), :] = dot(wz_ref[0], both).astype(BF16)
        return carry

    lax.fori_loop(0, bands // team, depth_in, 0)

    def planes(g, carry):
        rows_g = pl.ds(g * team * span, team * span)
        sticks = t_scr[rows_g, :]
        for k in range(chunks):
            here = slice(k * LANES, (k + 1) * LANES)
            wide = slice(2 * k * LANES, 2 * (k + 1) * LANES)
            ab = dot(sticks, tab_ref[:, wide])
            p, q = field_ref[0, :, here], field_ref[1, :, here]
            p2, q2 = field_ref[2, :, here], field_ref[3, :, here]
            for b in range(team):
                u, x = ab[b * span : b * span + side, :LANES], ab[b * span : b * span + side, LANES:]
                w, v = ab[b * span + side : (b + 1) * span, :LANES], ab[b * span + side : (b + 1) * span, LANES:]
                pr, pi, mr, mi = [t.astype(BF16) for t in (u - v, w + x, u + v, w - x)]
                ar, ai = p * pr - q * pi, p * pi + q * pr
                br, bi = p2 * mr - q2 * mi, p2 * mi + q2 * mr
                even = jnp.concatenate([ar + br, ai + bi], axis=0)
                odd = jnp.concatenate([ai - bi, br - ar], axis=0)
                l_scr[b * span : (b + 1) * span, wide] = jnp.concatenate([even, odd], axis=1)
        back = dot_nt(l_scr[...], tab_ref[...]).astype(BF16)
        for b in range(team):
            done = dot(wz_ref[1], back[b * span : (b + 1) * span])
            for n in range(groups // 2):
                here = slice(n * LANES, (n + 1) * LANES)
                grid[n, pl.ds((g * team + b) * side, side), :] = done[:side, here]
                grid[n, pl.ds((bands + g * team + b) * side, side), :] = done[side:, here]
        return carry

    lax.fori_loop(0, bands // team, planes, 0)

    levels(collect)
    for d in range(groups):
        late = acc[1, d]
        late = jnp.concatenate([late[:, waves - STICK_DEV :], late[:, : waves - STICK_DEV]], axis=1)
        out_refs[d][...] = (acc[0, d] + late).astype(BF16)


def arrange_kernel(groups, me_ref, *refs):
    y_refs, (rows_ref,) = refs[:groups], refs[groups:]
    part = y_refs[0].shape[0] // 2
    half = groups * part
    me = me_ref[0]
    for j in range(groups // 2):
        one, other = y_refs[2 * j][...].astype(F32), y_refs[2 * j + 1][...].astype(F32)
        low = jnp.where((me & 1) == 0, one, other)
        high = jnp.where((me & 1) == 0, other, one)
        begin = pl.multiple_of(((me >> 1) ^ j) * (2 * part), 8)
        rows_ref[pl.ds(begin, 2 * part)] = jnp.concatenate([low[:part], high[:part]], axis=0)
        rows_ref[pl.ds(begin + half, 2 * part)] = jnp.concatenate([low[part:], high[part:]], axis=0)


def join_kernel(groups, me_ref, *refs):
    rows_refs, refs = refs[: CHUNKS - 1], refs[CHUNKS - 1 :]
    sorted_ref, rows_scr = refs[groups:]
    arrange_kernel(groups, me_ref, *refs[:groups], rows_scr)
    values = [ref[...] for ref in (*rows_refs, rows_scr)]
    part = values[0].shape[0] // (2 * groups)
    sorted_ref[...] = jnp.concatenate(
        [v[i * part : (i + 1) * part] for i in range(2 * groups) for v in values], axis=0
    ).astype(BF16)


def couple_kernel(partner_ref, sorted_ref, g_ref):
    products = dot_nt(partner_ref[...], sorted_ref[...])
    half = products.shape[0] // 2
    re = products[:half, :half] + products[half:, half:]
    im = products[:half, half:] - products[half:, :half]
    for i in range(g_ref.shape[0]):
        g_ref[i] = jnp.concatenate([re, im], axis=1).astype(BF16)


def unsort_kernel(y_ref, rank_ref, out_ref):
    both, waves = y_ref.shape
    parts = waves // 256
    stacked = jnp.concatenate([y_ref[:, i * 256 : (i + 1) * 256] for i in range(parts)], axis=0)
    for tile in range(parts):
        here = slice(tile * 256, (tile + 1) * 256)
        rank = rank_ref[:, here]
        values = dot(stacked, one_hot(rank & 255, 256))
        total = None
        for part in range(parts):
            value = jnp.where((rank >> 8) == part, values[part * both : (part + 1) * both], 0.0)
            total = value if total is None else total + value
        out_ref[:, here] = total.astype(BF16)


def whole(memory=pltpu.VMEM):
    return pl.BlockSpec(memory_space=memory)


def params(limit=VMEM_LIMIT):
    return pltpu.CompilerParams(vmem_limit_bytes=limit)


def shards(orbitals, box_index, partner_pool, potential):
    fft_count = lax.axis_size("fft")
    side = potential.shape[0]
    bands = orbitals.shape[2]
    waves = orbitals.shape[3]
    share = bands // fft_count
    columns = STICK_DEV * fft_count
    chunks = (side // 2 + 1 + 1) // 2
    coeffs = orbitals.reshape(2 * bands, waves)

    cosine, sine = cos_sin(side)
    cs = jnp.asarray(np.concatenate([cosine, cosine, sine, sine], axis=1))
    inward = np.block([[cosine, -sine], [sine, cosine]])
    outward = np.block([[cosine, sine], [-sine, cosine]])
    wz = jnp.asarray(np.stack([inward, outward]))

    me = lax.axis_index("fft")
    me_row = me.reshape(1)
    pairs = [[(i, i ^ s) for i in range(fft_count)] for s in range(fft_count)]
    pool_count = lax.axis_size("pool")
    rows = 2 * share // CHUNKS
    tiles = waves // LANES
    packed = waves + side * STICK_DEV // rows + -(-(tiles + 8) // rows) * LANES
    scalars, blocks = whole(pltpu.SMEM), [whole()] * fft_count

    *ordered, ordered_all, rank = pl.pallas_call(
        functools.partial(sort_kernel, side, fft_count),
        out_shape=[
            jax.ShapeDtypeStruct((rows, waves if c else packed), BF16)
            for _ in range(fft_count)
            for c in range(CHUNKS)
        ]
        + [
            jax.ShapeDtypeStruct((2 * bands, waves), BF16),
            jax.ShapeDtypeStruct((1, waves), jnp.int32),
        ],
        in_specs=[scalars, whole(), whole(pltpu.HBM)],
        out_specs=blocks * CHUNKS + [whole(), whole()],
        scratch_shapes=[
            pltpu.VMEM((2 * bands, waves), BF16),
            pltpu.VMEM((waves // 256 * 2 * bands, waves), BF16),
            pltpu.VMEM((waves // 256 * 2 * bands, 256), F32),
            pltpu.SemaphoreType.DMA,
        ],
        compiler_params=params(SORT_LIMIT),
        name="sort_waves",
    )(me_row, box_index.reshape(1, waves), coeffs)
    moved = [
        [ordered[c]] + [lax.ppermute(ordered[s * CHUNKS + c], "fft", pairs[s]) for s in range(1, fft_count)]
        for c in range(CHUNKS)
    ]

    field, cyr, syr = pl.pallas_call(
        functools.partial(field_kernel, side, chunks),
        out_shape=(
            jax.ShapeDtypeStruct((4, side, chunks * LANES), BF16),
            jax.ShapeDtypeStruct((side, chunks * LANES), BF16),
            jax.ShapeDtypeStruct((side, chunks * LANES), BF16),
        ),
        in_specs=[whole()] * 2,
        out_specs=(whole(),) * 3,
        compiler_params=params(),
        cost_estimate=pl.CostEstimate(flops=10**9, bytes_accessed=10**7, transcendentals=0),
        name="field_pairs",
    )(potential.reshape(side * side, 2 * side), cs)

    team = min(4, rows // 2)
    scratch = [
        pltpu.VMEM((2, fft_count, rows, waves), F32),
        pltpu.VMEM((columns // LANES, rows * side, LANES), F32),
        pltpu.VMEM((rows * side, columns), BF16),
        pltpu.VMEM((team * 2 * side, 2 * chunks * LANES), BF16),
        pltpu.VMEM((2, fft_count, rows, waves), F32),
    ]
    cost = pl.CostEstimate(flops=10**10, bytes_accessed=10**7, transcendentals=0)
    shapes = [jax.ShapeDtypeStruct((rows, waves), BF16)] * fft_count
    *back, tab, spot, col, start = pl.pallas_call(
        functools.partial(box_first_kernel, side, chunks, team, waves, fft_count),
        out_shape=shapes
        + [
            jax.ShapeDtypeStruct((columns, 2 * chunks * LANES), BF16),
            jax.ShapeDtypeStruct((fft_count, side, 2 * STICK_DEV), F32),
            jax.ShapeDtypeStruct((2, fft_count, tiles, LANES), jnp.int32),
            jax.ShapeDtypeStruct((fft_count, LANES), jnp.int32),
        ],
        in_specs=blocks + [whole()] * 5,
        out_specs=blocks + [whole()] * 4,
        scratch_shapes=scratch
        + [pltpu.SMEM((fft_count, LANES), jnp.int32), pltpu.SemaphoreType.DMA],
        compiler_params=params(),
        cost_estimate=cost,
        name="box_first",
    )(*moved[0], field, cs, cyr, syr, wz)
    returned = [[back[0]] + [lax.ppermute(back[s], "fft", pairs[s]) for s in range(1, fft_count)]]
    for c in range(1, CHUNKS):
        back = pl.pallas_call(
            functools.partial(box_next_kernel, side, chunks, team, waves, fft_count),
            out_shape=shapes,
            in_specs=blocks + [whole()] * 5 + [scalars],
            out_specs=blocks,
            scratch_shapes=scratch,
            compiler_params=params(),
            cost_estimate=cost,
            name="box_next",
        )(*moved[c], field, wz, tab, spot, col, start)
        returned.append(
            [back[0]] + [lax.ppermute(back[s], "fft", pairs[s]) for s in range(1, fft_count)]
        )

    spread = lax.all_to_all(
        ordered_all.reshape(pool_count, 2 * bands // pool_count, waves), "pool", 0, 0, tiled=True
    )
    chosen = pl.pallas_call(
        select_kernel,
        out_shape=jax.ShapeDtypeStruct(spread.shape, BF16),
        in_specs=[scalars, whole(pl.ANY)],
        out_specs=whole(pl.ANY),
        scratch_shapes=[pltpu.SemaphoreType.DMA((pool_count,))],
        compiler_params=params(),
        name="select_partner",
    )(partner_pool, spread)
    partner = lax.all_to_all(chosen, "pool", 0, 0, tiled=True).reshape(2 * bands, waves)

    arranged = [
        pl.pallas_call(
            functools.partial(arrange_kernel, fft_count),
            out_shape=jax.ShapeDtypeStruct((rows * fft_count, waves), F32),
            in_specs=[scalars] + blocks,
            out_specs=whole(),
            compiler_params=params(),
            cost_estimate=pl.CostEstimate(
                flops=ARRANGE_COST, bytes_accessed=10**6, transcendentals=0
            ),
            name="arrange",
        )(me_row, *returned[c])
        for c in range(CHUNKS - 1)
    ]
    sorted_response = pl.pallas_call(
        functools.partial(join_kernel, fft_count),
        out_shape=jax.ShapeDtypeStruct((2 * bands, waves), BF16),
        in_specs=[scalars] + [whole()] * (CHUNKS - 1) + blocks,
        out_specs=whole(),
        scratch_shapes=[pltpu.VMEM((rows * fft_count, waves), F32)],
        compiler_params=params(),
        cost_estimate=pl.CostEstimate(flops=JOIN_COST, bytes_accessed=10**6, transcendentals=0),
        name="join",
    )(me_row, *arranged, *returned[-1])
    sums = pl.pallas_call(
        couple_kernel,
        out_shape=jax.ShapeDtypeStruct((fft_count, bands, 2 * bands), BF16),
        in_specs=[whole(), whole()],
        out_specs=whole(),
        compiler_params=params(),
        name="couple",
    )(partner, sorted_response)
    shares = lax.all_to_all(sums, "fft", 0, 0, tiled=True)
    response = pl.pallas_call(
        unsort_kernel,
        out_shape=jax.ShapeDtypeStruct((2 * bands, waves), BF16),
        in_specs=[whole(), whole()],
        out_specs=whole(),
        compiler_params=params(),
        cost_estimate=pl.CostEstimate(flops=10**9, bytes_accessed=10**7, transcendentals=0),
        name="unsort",
    )(sorted_response, rank)
    summed = jnp.sum(shares.astype(F32), axis=0)
    summed = jnp.stack([summed[:, :bands], summed[:, bands:]])
    coupling = (summed / jnp.sqrt(jnp.float32(waves * fft_count)))[:, None]
    return response.reshape(2, 1, bands, waves), coupling


def solution(mesh):
    placed = (P(None, "pool", None, "fft"), P("fft"), P(), P())
    return jax.shard_map(
        shards,
        mesh=mesh,
        in_specs=placed,
        out_specs=(P(None, "pool", None, "fft"), P(None, "pool", None, None)),
        check_vma=False,
    )
```

```python
import functools

import jax
import jax.numpy as jnp
import ml_dtypes
import numpy as np
from jax import lax
from jax.experimental import pallas as pl
from jax.experimental.pallas import tpu as pltpu
from jax.sharding import PartitionSpec as P

STICK_DEV = 64
LANES = 128
UNROLL = 16
CHUNKS = 1
BF16 = jnp.bfloat16
F32 = jnp.float32
VMEM_LIMIT = 24 * 1024 * 1024
SORT_LIMIT = 60 * 1024 * 1024
ARRANGE_COST = 3*10**9
JOIN_COST = 10**7


def cos_sin(side):
    points = np.arange(side)
    angles = (2.0 * np.pi / side) * (points[:, None] * points[None, :] % side)
    scaling = 1.0 / np.sqrt(side)
    cosine = (np.cos(angles) * scaling).astype(ml_dtypes.bfloat16)
    sine = (np.sin(angles) * scaling).astype(ml_dtypes.bfloat16)
    return cosine, sine


def dot(a, b):
    return jnp.dot(a, b, preferred_element_type=F32)


def dot_nt(a, b):
    return lax.dot_general(a, b, (((1,), (1,)), ((), ())), preferred_element_type=F32)


def one_hot(row, count):
    places = lax.broadcasted_iota(jnp.int32, (count, row.shape[1]), 0)
    return jnp.where(places == row, 1.0, 0.0).astype(BF16)


def triangles(side):
    rows = lax.broadcasted_iota(jnp.int32, (side, side), 0)
    cols = lax.broadcasted_iota(jnp.int32, (side, side), 1)
    upper = jnp.where(rows < cols, 1.0, 0.0).astype(BF16)
    lower = jnp.where(rows > cols, 1.0, 0.0).astype(BF16)
    return upper, lower, jnp.ones((side, side), BF16)


def prefix(occupied, tri):
    upper, lower, ones = tri
    in_rows = dot(occupied, ones).astype(BF16)
    return dot(occupied, upper) + dot(lower, in_rows)


def locate(idx, side):
    bits = side.bit_length() - 1
    tri = triangles(side)
    xh = one_hot(idx >> (2 * bits), side)
    yh = one_hot((idx >> bits) & (side - 1), side)
    zh = one_hot(idx & (side - 1), side)
    columns = jnp.minimum(dot_nt(xh, yh), 1.0).astype(BF16)
    slots = prefix(columns, tri).astype(BF16)
    slot = jnp.sum(xh.astype(F32) * dot(slots, yh), axis=0, keepdims=True)
    ch = one_hot(slot.astype(jnp.int32), STICK_DEV)
    cells = dot_nt(zh, ch)
    ranks = prefix(cells.astype(BF16), tri)
    high = jnp.floor(ranks * (1.0 / side))
    low = ranks - high * side
    looked = dot(high.astype(BF16), ch) * side + dot(low.astype(BF16), ch)
    rank = jnp.sum(zh.astype(F32) * looked, axis=0, keepdims=True)
    return xh, yh, ch, slot, cells, rank.astype(jnp.int32)


def sort_kernel(side, groups, me_ref, idx_ref, x_hbm, *refs):
    outs, (all_ref, rank_ref, x_ref, wide, pieces, sem) = refs[: groups * CHUNKS], refs[groups * CHUNKS :]
    fetch = pltpu.make_async_copy(x_hbm, x_ref, sem)
    fetch.start()
    xh, yh, ch, slot_of, cells, rank = locate(idx_ref[...], side)
    rank_ref[...] = rank
    waves = rank.shape[1]
    both = x_ref.shape[0]
    bands = both // 2
    share = bands // groups
    rows = 2 * share // CHUNKS
    cells = jnp.concatenate([cells[i : i + rows] for i in range(0, side, rows)], axis=1)
    tiles = waves // LANES
    in_tile = one_hot(rank & (LANES - 1), LANES)
    col = dot_nt(one_hot(rank >> 7, tiles) * slot_of.astype(BF16), in_tile)
    steps = lax.broadcasted_iota(jnp.int32, (8, side), 1).astype(F32).astype(BF16)
    place = [dot_nt(steps, jnp.minimum(dot_nt(ch, hot), 1.0).astype(BF16)) for hot in (xh, yh)]
    lines = [col, jnp.concatenate(place, axis=1)]
    spare = -(tiles + 8) % rows
    if spare:
        lines.append(jnp.zeros((spare, LANES), F32))
    lines = jnp.concatenate(lines, axis=0)
    lines = [lines[i : i + rows] for i in range(0, lines.shape[0], rows)]
    extra = jnp.concatenate([cells] + lines, axis=1).astype(BF16)
    low = one_hot(rank & 255, 256)
    for shift in range(groups):
        outs[shift * CHUNKS][:, waves:] = extra
    fetch.wait()
    parts = waves // 256
    step = 2 if parts % 2 == 0 else 1
    half = share // CHUNKS
    for first in range(0, parts, step):
        for part in range(first, first + step):
            mask = jnp.where((rank >> 8) == part, 1.0, 0.0).astype(BF16)
            wide[part * both : (part + 1) * both] = x_ref[...] * mask
        rows_now = slice(first * both, (first + step) * both)
        pieces[rows_now] = dot_nt(wide[rows_now], low)
        for part in range(first, first + step):
            here = slice(part * 256, (part + 1) * 256)
            all_ref[:, here] = pieces[part * both : (part + 1) * both].astype(BF16)
            for shift in range(groups):
                begin = pl.multiple_of(part * both + (me_ref[0] ^ shift) * share, 8)
                re = pieces[pl.ds(begin, share)]
                im = pieces[pl.ds(begin + bands, share)]
                for c in range(CHUNKS):
                    mine = slice(c * half, (c + 1) * half)
                    outs[shift * CHUNKS + c][:, here] = jnp.concatenate(
                        [re[mine], im[mine]], axis=0
                    ).astype(BF16)


def field_kernel(side, chunks, pot_ref, cs_ref, field_ref, cyr_ref, syr_ref):
    half = side // 2
    left = lax.broadcasted_iota(jnp.int32, (side, LANES), 1) < side
    for ref, begin in ((cyr_ref, 0), (syr_ref, LANES)):
        table = cs_ref[:, begin : begin + side].astype(F32)
        for k in range(chunks):
            ya, yb = (2 * k) % side, (2 * k + 1) % side
            ref[:, k * LANES : (k + 1) * LANES] = jnp.where(
                left, table[:, ya : ya + 1], table[:, yb : yb + 1]
            ).astype(BF16)
    lane = lax.broadcasted_iota(jnp.int32, (side, LANES), 1)
    first = lane < side
    flipped = (lane & side) + ((side - (lane & (side - 1))) & (side - 1))

    def pair(row_a, row_b):
        p = jnp.where(first, row_a, pltpu.roll(row_b, side, 1))
        q = jnp.where(first, pltpu.roll(row_a, side, 1), row_b)
        return p, q

    def plane(y):
        return pot_ref[pl.ds(y, side, stride=side), :]

    def mirror(y):
        if y == 0 or y >= half:
            return jnp.zeros((side, LANES), F32)
        return jnp.take_along_axis(plane(side - y), flipped, axis=1)

    zero = jnp.zeros((side, LANES), F32)
    for k in range(chunks):
        ya, yb = 2 * k, 2 * k + 1
        here = slice(k * LANES, (k + 1) * LANES)
        values = pair(plane(ya), plane(yb) if yb <= half else zero) + pair(mirror(ya), mirror(yb))
        for i, value in enumerate(values):
            field_ref[i, :, here] = value.astype(BF16)


def select_kernel(order_ref, in_ref, out_ref, sems):
    copies = []
    for i in range(out_ref.shape[0]):
        copy = pltpu.make_async_copy(in_ref.at[order_ref[i]], out_ref.at[i], sems.at[i])
        copy.start()
        copies.append(copy)
    for copy in copies:
        copy.wait()


def build_tables(side, chunks, waves, x_refs, cs_ref, cyr_ref, syr_ref, tab_ref, spot_ref, col_ref, start_ref):
    rows = x_refs[0].shape[0]
    parts = side // rows
    tiles = waves // LANES
    cells_end = waves + parts * STICK_DEV
    tri = triangles(side)
    ahead = jnp.where(
        lax.broadcasted_iota(jnp.int32, (side, LANES), 0)
        < lax.broadcasted_iota(jnp.int32, (side, LANES), 1),
        1.0, 0.0,
    ).astype(BF16)
    left = lax.broadcasted_iota(jnp.int32, (tiles, LANES), 1) < STICK_DEV
    at_x, at_y = [], []
    for d, x_ref in enumerate(x_refs):
        cells = jnp.concatenate(
            [x_ref[:, waves + i * STICK_DEV : waves + (i + 1) * STICK_DEV].astype(F32) for i in range(parts)],
            axis=0,
        )
        lines = jnp.concatenate(
            [
                x_ref[:, i : i + LANES].astype(F32)
                for i in range(cells_end, cells_end + -(-(tiles + 8) // rows) * LANES, LANES)
            ],
            axis=0,
        )
        place = lines[tiles : tiles + 1].astype(jnp.int32)
        at_x.append(one_hot(place[:, :side], side).astype(F32).T)
        at_y.append(one_hot(place[:, side:], side).astype(F32).T)
        ranks = prefix(cells.astype(BF16), tri)
        begins = jnp.minimum(jnp.floor(ranks[:, :1] * (1.0 / STICK_DEV)), waves // STICK_DEV - 1.0)
        spot = jnp.where(cells > 0.5, ranks - begins * STICK_DEV, -1.0)
        spot_ref[d] = jnp.concatenate([spot, spot], axis=1)
        level = dot_nt(jnp.ones((8, STICK_DEV), BF16), cells.astype(BF16))
        start_ref[d : d + 1, :] = dot(level.astype(BF16), ahead)[:1].astype(jnp.int32)
        col = lines[:tiles] + float((d % 2) * STICK_DEV)
        turned = pltpu.roll(col, STICK_DEV, 1)
        after = jnp.concatenate([turned[1:], turned[:1]], axis=0)
        col_ref[0, d] = col.astype(jnp.int32)
        col_ref[1, d] = jnp.where(left, turned, after).astype(jnp.int32)
    at_x = jnp.concatenate(at_x, axis=0).astype(BF16)
    at_y = jnp.concatenate(at_y, axis=0).astype(BF16)
    both = dot(at_x, cs_ref[...])
    cx, sx = both[:, :LANES], both[:, LANES:]
    for k in range(chunks):
        cy = dot(at_y, cyr_ref[:, k * LANES : (k + 1) * LANES])
        sy = dot(at_y, syr_ref[:, k * LANES : (k + 1) * LANES])
        base = 2 * k * LANES
        tab_ref[:, base : base + LANES] = (cy * cx - sy * sx).astype(BF16)
        tab_ref[:, base + LANES : base + 2 * LANES] = (cy * sx + sy * cx).astype(BF16)


def box_first_kernel(side, chunks, team, waves, groups, *refs):
    x_refs, refs = refs[:groups], refs[groups:]
    (field_ref, cs_ref, cyr_ref, syr_ref, wz_ref), refs = refs[:5], refs[5:]
    out_refs, refs = refs[:groups], refs[groups:]
    (tab_ref, spot_ref, col_ref, start_ref), refs = refs[:4], refs[4:]
    *scratch, start_s, sem = refs
    build_tables(
        side, chunks, waves, x_refs, cs_ref, cyr_ref, syr_ref, tab_ref, spot_ref, col_ref, start_ref
    )
    to_scalars = pltpu.make_async_copy(start_ref, start_s, sem)
    to_scalars.start()
    to_scalars.wait()
    box_work(
        side, chunks, team, waves, x_refs, field_ref, wz_ref, tab_ref, spot_ref, col_ref, start_s,
        out_refs, *scratch,
    )


def box_next_kernel(side, chunks, team, waves, groups, *refs):
    x_refs, refs = refs[:groups], refs[groups:]
    (field_ref, wz_ref, tab_ref, spot_ref, col_ref, start_s), refs = refs[:6], refs[6:]
    out_refs, scratch = refs[:groups], refs[groups:]
    box_work(
        side, chunks, team, waves, x_refs, field_ref, wz_ref, tab_ref, spot_ref, col_ref, start_s,
        out_refs, *scratch,
    )


def box_work(
    side, chunks, team, waves, x_refs, field_ref, wz_ref, tab_ref, spot_ref, col_ref, start_s,
    out_refs, xf, grid, t_scr, l_scr, acc,
):
    groups = len(x_refs)
    rows = x_refs[0].shape[0]
    bands = rows // 2
    blocks = rows // 8
    span = 2 * side
    for d in range(groups):
        value = x_refs[d][:, :waves].astype(F32)
        xf[0, d] = value
        xf[1, d] = jnp.concatenate([value[:, STICK_DEV:], value[:, :STICK_DEV]], axis=1)
        acc[0, d] = jnp.zeros((rows, waves), F32)
        acc[1, d] = jnp.zeros((rows, waves), F32)
    lane = lax.broadcasted_iota(jnp.int32, (8, LANES), 1)
    left = lane < STICK_DEV

    def window(z, d):
        begin = jnp.minimum(start_s[d, z] >> 6, waves // STICK_DEV - 1)
        tile = begin >> 1
        return begin & 1, tile, pl.ds(pl.multiple_of(tile * LANES, LANES), LANES), begin * STICK_DEV

    def expand(z):
        for dp in range(groups // 2):
            spot = jnp.where(
                left,
                jnp.broadcast_to(spot_ref[2 * dp, pl.ds(z, 1), :], (8, LANES)),
                jnp.broadcast_to(spot_ref[2 * dp + 1, pl.ds(z, 1), :], (8, LANES)),
            )
            valid = spot >= 0.0
            at = jnp.maximum(spot, 0.0).astype(jnp.int32)
            odd_a, _, lanes_a, _ = window(z, 2 * dp)
            odd_b, _, lanes_b, _ = window(z, 2 * dp + 1)
            for block in range(blocks):
                part = slice(block * 8, (block + 1) * 8)
                a = jnp.take_along_axis(xf[odd_a, 2 * dp, part, lanes_a], at, axis=1)
                b = jnp.take_along_axis(xf[odd_b, 2 * dp + 1, part, lanes_b], at, axis=1)
                value = jnp.where(valid, jnp.where(left, a, b), 0.0)
                grid[dp, pl.ds(block * 8 * side + z, 8, stride=side), :] = value

    def collect(z):
        for dp in range(groups // 2):
            sources = [
                grid[dp, pl.ds(block * 8 * side + z, 8, stride=side), :] for block in range(blocks)
            ]
            for d in (2 * dp, 2 * dp + 1):
                odd, tile, lanes, base = window(z, d)
                at = jnp.broadcast_to(col_ref[odd, d, pl.ds(tile, 1), :], (8, LANES))
                mask = (lane >= start_s[d, z] - base) & (lane < start_s[d, z + 1] - base)
                for block in range(blocks):
                    part = slice(block * 8, (block + 1) * 8)
                    value = jnp.take_along_axis(sources[block], at, axis=1)
                    acc[odd, d, part, lanes] = jnp.where(mask, value, acc[odd, d, part, lanes])

    def levels(step):
        def body(i, carry):
            for j in range(UNROLL):
                step(i * UNROLL + j)
            return carry

        lax.fori_loop(0, side // UNROLL, body, 0)

    levels(expand)

    def depth_in(g, carry):
        for b in [g * team + i for i in range(team)]:
            both = jnp.concatenate(
                [
                    jnp.concatenate(
                        [
                            grid[n, pl.ds(b * side, side), :].astype(BF16),
                            grid[n, pl.ds((bands + b) * side, side), :].astype(BF16),
                        ],
                        axis=0,
                    )
                    for n in range(groups // 2)
                ],
                axis=1,
            )
            t_scr[pl.ds(b * span, span), :] = dot(wz_ref[0], both).astype(BF16)
        return carry

    lax.fori_loop(0, bands // team, depth_in, 0)

    def planes(g, carry):
        rows_g = pl.ds(g * team * span, team * span)
        sticks = t_scr[rows_g, :]
        for k in range(chunks):
            here = slice(k * LANES, (k + 1) * LANES)
            wide = slice(2 * k * LANES, 2 * (k + 1) * LANES)
            ab = dot(sticks, tab_ref[:, wide])
            p, q = field_ref[0, :, here], field_ref[1, :, here]
            p2, q2 = field_ref[2, :, here], field_ref[3, :, here]
            for b in range(team):
                u, x = ab[b * span : b * span + side, :LANES], ab[b * span : b * span + side, LANES:]
                w, v = ab[b * span + side : (b + 1) * span, :LANES], ab[b * span + side : (b + 1) * span, LANES:]
                pr, pi, mr, mi = [t.astype(BF16) for t in (u - v, w + x, u + v, w - x)]
                ar, ai = p * pr - q * pi, p * pi + q * pr
                br, bi = p2 * mr - q2 * mi, p2 * mi + q2 * mr
                even = jnp.concatenate([ar + br, ai + bi], axis=0)
                odd = jnp.concatenate([ai - bi, br - ar], axis=0)
                l_scr[b * span : (b + 1) * span, wide] = jnp.concatenate([even, odd], axis=1)
        back = dot_nt(l_scr[...], tab_ref[...]).astype(BF16)
        for b in range(team):
            done = dot(wz_ref[1], back[b * span : (b + 1) * span])
            for n in range(groups // 2):
                here = slice(n * LANES, (n + 1) * LANES)
                grid[n, pl.ds((g * team + b) * side, side), :] = done[:side, here]
                grid[n, pl.ds((bands + g * team + b) * side, side), :] = done[side:, here]
        return carry

    lax.fori_loop(0, bands // team, planes, 0)

    levels(collect)
    for d in range(groups):
        late = acc[1, d]
        late = jnp.concatenate([late[:, waves - STICK_DEV :], late[:, : waves - STICK_DEV]], axis=1)
        out_refs[d][...] = (acc[0, d] + late).astype(BF16)


def arrange_kernel(groups, me_ref, *refs):
    y_refs, (rows_ref,) = refs[:groups], refs[groups:]
    part = y_refs[0].shape[0] // 2
    half = groups * part
    me = me_ref[0]
    for j in range(groups // 2):
        one, other = y_refs[2 * j][...].astype(F32), y_refs[2 * j + 1][...].astype(F32)
        low = jnp.where((me & 1) == 0, one, other)
        high = jnp.where((me & 1) == 0, other, one)
        begin = pl.multiple_of(((me >> 1) ^ j) * (2 * part), 8)
        rows_ref[pl.ds(begin, 2 * part)] = jnp.concatenate([low[:part], high[:part]], axis=0)
        rows_ref[pl.ds(begin + half, 2 * part)] = jnp.concatenate([low[part:], high[part:]], axis=0)


def join_kernel(groups, me_ref, *refs):
    rows_refs, refs = refs[: CHUNKS - 1], refs[CHUNKS - 1 :]
    sorted_ref, rows_scr = refs[groups:]
    arrange_kernel(groups, me_ref, *refs[:groups], rows_scr)
    values = [ref[...] for ref in (*rows_refs, rows_scr)]
    part = values[0].shape[0] // (2 * groups)
    sorted_ref[...] = jnp.concatenate(
        [v[i * part : (i + 1) * part] for i in range(2 * groups) for v in values], axis=0
    ).astype(BF16)


def couple_kernel(partner_ref, sorted_ref, g_ref):
    products = dot_nt(partner_ref[...], sorted_ref[...])
    half = products.shape[0] // 2
    g_ref[0] = (products[:half, :half] + products[half:, half:]).astype(BF16)
    g_ref[1] = (products[:half, half:] - products[half:, :half]).astype(BF16)


def unsort_kernel(y_ref, rank_ref, out_ref):
    both, waves = y_ref.shape
    parts = waves // 256
    stacked = jnp.concatenate([y_ref[:, i * 256 : (i + 1) * 256] for i in range(parts)], axis=0)
    for tile in range(parts):
        here = slice(tile * 256, (tile + 1) * 256)
        rank = rank_ref[:, here]
        values = dot(stacked, one_hot(rank & 255, 256))
        total = None
        for part in range(parts):
            value = jnp.where((rank >> 8) == part, values[part * both : (part + 1) * both], 0.0)
            total = value if total is None else total + value
        out_ref[:, here] = total.astype(BF16)


def whole(memory=pltpu.VMEM):
    return pl.BlockSpec(memory_space=memory)


def params(limit=VMEM_LIMIT):
    return pltpu.CompilerParams(vmem_limit_bytes=limit)


def shards(orbitals, box_index, partner_pool, potential):
    fft_count = lax.axis_size("fft")
    side = potential.shape[0]
    bands = orbitals.shape[2]
    waves = orbitals.shape[3]
    share = bands // fft_count
    columns = STICK_DEV * fft_count
    chunks = (side // 2 + 1 + 1) // 2
    coeffs = orbitals.reshape(2 * bands, waves)

    cosine, sine = cos_sin(side)
    cs = jnp.asarray(np.concatenate([cosine, cosine, sine, sine], axis=1))
    inward = np.block([[cosine, -sine], [sine, cosine]])
    outward = np.block([[cosine, sine], [-sine, cosine]])
    wz = jnp.asarray(np.stack([inward, outward]))

    me = lax.axis_index("fft")
    me_row = me.reshape(1)
    pairs = [[(i, i ^ s) for i in range(fft_count)] for s in range(fft_count)]
    pool_count = lax.axis_size("pool")
    rows = 2 * share // CHUNKS
    tiles = waves // LANES
    packed = waves + side * STICK_DEV // rows + -(-(tiles + 8) // rows) * LANES
    scalars, blocks = whole(pltpu.SMEM), [whole()] * fft_count

    *ordered, ordered_all, rank = pl.pallas_call(
        functools.partial(sort_kernel, side, fft_count),
        out_shape=[
            jax.ShapeDtypeStruct((rows, waves if c else packed), BF16)
            for _ in range(fft_count)
            for c in range(CHUNKS)
        ]
        + [
            jax.ShapeDtypeStruct((2 * bands, waves), BF16),
            jax.ShapeDtypeStruct((1, waves), jnp.int32),
        ],
        in_specs=[scalars, whole(), whole(pltpu.HBM)],
        out_specs=blocks * CHUNKS + [whole(), whole()],
        scratch_shapes=[
            pltpu.VMEM((2 * bands, waves), BF16),
            pltpu.VMEM((waves // 256 * 2 * bands, waves), BF16),
            pltpu.VMEM((waves // 256 * 2 * bands, 256), F32),
            pltpu.SemaphoreType.DMA,
        ],
        compiler_params=params(SORT_LIMIT),
        name="sort_waves",
    )(me_row, box_index.reshape(1, waves), coeffs)
    moved = [
        [ordered[c]] + [lax.ppermute(ordered[s * CHUNKS + c], "fft", pairs[s]) for s in range(1, fft_count)]
        for c in range(CHUNKS)
    ]

    field, cyr, syr = pl.pallas_call(
        functools.partial(field_kernel, side, chunks),
        out_shape=(
            jax.ShapeDtypeStruct((4, side, chunks * LANES), BF16),
            jax.ShapeDtypeStruct((side, chunks * LANES), BF16),
            jax.ShapeDtypeStruct((side, chunks * LANES), BF16),
        ),
        in_specs=[whole()] * 2,
        out_specs=(whole(),) * 3,
        compiler_params=params(),
        cost_estimate=pl.CostEstimate(flops=10**9, bytes_accessed=10**7, transcendentals=0),
        name="field_pairs",
    )(potential.reshape(side * side, 2 * side), cs)

    team = min(8, rows // 2)
    scratch = [
        pltpu.VMEM((2, fft_count, rows, waves), F32),
        pltpu.VMEM((columns // LANES, rows * side, LANES), F32),
        pltpu.VMEM((rows * side, columns), BF16),
        pltpu.VMEM((team * 2 * side, 2 * chunks * LANES), BF16),
        pltpu.VMEM((2, fft_count, rows, waves), F32),
    ]
    cost = pl.CostEstimate(flops=10**10, bytes_accessed=10**7, transcendentals=0)
    shapes = [jax.ShapeDtypeStruct((rows, waves), BF16)] * fft_count
    *back, tab, spot, col, start = pl.pallas_call(
        functools.partial(box_first_kernel, side, chunks, team, waves, fft_count),
        out_shape=shapes
        + [
            jax.ShapeDtypeStruct((columns, 2 * chunks * LANES), BF16),
            jax.ShapeDtypeStruct((fft_count, side, 2 * STICK_DEV), F32),
            jax.ShapeDtypeStruct((2, fft_count, tiles, LANES), jnp.int32),
            jax.ShapeDtypeStruct((fft_count, LANES), jnp.int32),
        ],
        in_specs=blocks + [whole()] * 5,
        out_specs=blocks + [whole()] * 4,
        scratch_shapes=scratch
        + [pltpu.SMEM((fft_count, LANES), jnp.int32), pltpu.SemaphoreType.DMA],
        compiler_params=params(),
        cost_estimate=cost,
        name="box_first",
    )(*moved[0], field, cs, cyr, syr, wz)
    returned = [[back[0]] + [lax.ppermute(back[s], "fft", pairs[s]) for s in range(1, fft_count)]]
    for c in range(1, CHUNKS):
        back = pl.pallas_call(
            functools.partial(box_next_kernel, side, chunks, team, waves, fft_count),
            out_shape=shapes,
            in_specs=blocks + [whole()] * 5 + [scalars],
            out_specs=blocks,
            scratch_shapes=scratch,
            compiler_params=params(),
            cost_estimate=cost,
            name="box_next",
        )(*moved[c], field, wz, tab, spot, col, start)
        returned.append(
            [back[0]] + [lax.ppermute(back[s], "fft", pairs[s]) for s in range(1, fft_count)]
        )

    spread = lax.all_to_all(
        ordered_all.reshape(pool_count, 2 * bands // pool_count, waves), "pool", 0, 0, tiled=True
    )
    chosen = pl.pallas_call(
        select_kernel,
        out_shape=jax.ShapeDtypeStruct(spread.shape, BF16),
        in_specs=[scalars, whole(pl.ANY)],
        out_specs=whole(pl.ANY),
        scratch_shapes=[pltpu.SemaphoreType.DMA((pool_count,))],
        compiler_params=params(),
        name="select_partner",
    )(partner_pool, spread)
    partner = lax.all_to_all(chosen, "pool", 0, 0, tiled=True).reshape(2 * bands, waves)

    arranged = [
        pl.pallas_call(
            functools.partial(arrange_kernel, fft_count),
            out_shape=jax.ShapeDtypeStruct((rows * fft_count, waves), F32),
            in_specs=[scalars] + blocks,
            out_specs=whole(),
            compiler_params=params(),
            cost_estimate=pl.CostEstimate(
                flops=ARRANGE_COST, bytes_accessed=10**6, transcendentals=0
            ),
            name="arrange",
        )(me_row, *returned[c])
        for c in range(CHUNKS - 1)
    ]
    sorted_response = pl.pallas_call(
        functools.partial(join_kernel, fft_count),
        out_shape=jax.ShapeDtypeStruct((2 * bands, waves), BF16),
        in_specs=[scalars] + [whole()] * (CHUNKS - 1) + blocks,
        out_specs=whole(),
        scratch_shapes=[pltpu.VMEM((rows * fft_count, waves), F32)],
        compiler_params=params(),
        cost_estimate=pl.CostEstimate(flops=JOIN_COST, bytes_accessed=10**6, transcendentals=0),
        name="join",
    )(me_row, *arranged, *returned[-1])
    sums = pl.pallas_call(
        couple_kernel,
        out_shape=jax.ShapeDtypeStruct((2, bands, bands), BF16),
        in_specs=[whole(), whole()],
        out_specs=whole(),
        compiler_params=params(),
        name="couple",
    )(partner, sorted_response)
    shares = [sums] + [lax.ppermute(sums, "fft", pairs[s]) for s in range(1, fft_count)]
    response = pl.pallas_call(
        unsort_kernel,
        out_shape=jax.ShapeDtypeStruct((2 * bands, waves), BF16),
        in_specs=[whole(), whole()],
        out_specs=whole(),
        compiler_params=params(),
        cost_estimate=pl.CostEstimate(flops=10**9, bytes_accessed=10**7, transcendentals=0),
        name="unsort",
    )(sorted_response, rank)
    summed = None
    for d in range(fft_count):
        offset = me ^ d
        term = shares[0]
        for s in range(1, fft_count):
            term = jnp.where(offset == s, shares[s], term)
        term = term.astype(F32)
        summed = term if summed is None else summed + term
    coupling = (summed / jnp.sqrt(jnp.float32(waves * fft_count)))[:, None]
    return response.reshape(2, 1, bands, waves), coupling


def solution(mesh):
    placed = (P(None, "pool", None, "fft"), P("fft"), P(), P())
    return jax.shard_map(
        shards,
        mesh=mesh,
        in_specs=placed,
        out_specs=(P(None, "pool", None, "fft"), P(None, "pool", None, None)),
        check_vma=False,
    )
```

```python
import functools

import jax
import jax.numpy as jnp
import ml_dtypes
import numpy as np
from jax import lax
from jax.experimental import pallas as pl
from jax.experimental.pallas import tpu as pltpu
from jax.sharding import PartitionSpec as P

STICK_DEV = 64
LANES = 128
UNROLL = 16
CHUNKS = 1
BF16 = jnp.bfloat16
F32 = jnp.float32
VMEM_LIMIT = 24 * 1024 * 1024
SORT_LIMIT = 60 * 1024 * 1024
ARRANGE_COST = 3*10**9
JOIN_COST = 10**11
BOX_COST = 10**10


def cos_sin(side):
    points = np.arange(side)
    angles = (2.0 * np.pi / side) * (points[:, None] * points[None, :] % side)
    scaling = 1.0 / np.sqrt(side)
    cosine = (np.cos(angles) * scaling).astype(ml_dtypes.bfloat16)
    sine = (np.sin(angles) * scaling).astype(ml_dtypes.bfloat16)
    return cosine, sine


def dot(a, b):
    return jnp.dot(a, b, preferred_element_type=F32)


def dot_nt(a, b):
    return lax.dot_general(a, b, (((1,), (1,)), ((), ())), preferred_element_type=F32)


def one_hot(row, count):
    places = lax.broadcasted_iota(jnp.int32, (count, row.shape[1]), 0)
    return jnp.where(places == row, 1.0, 0.0).astype(BF16)


def triangles(side):
    rows = lax.broadcasted_iota(jnp.int32, (side, side), 0)
    cols = lax.broadcasted_iota(jnp.int32, (side, side), 1)
    upper = jnp.where(rows < cols, 1.0, 0.0).astype(BF16)
    lower = jnp.where(rows > cols, 1.0, 0.0).astype(BF16)
    return upper, lower, jnp.ones((side, side), BF16)


def prefix(occupied, tri):
    upper, lower, ones = tri
    in_rows = dot(occupied, ones).astype(BF16)
    return dot(occupied, upper) + dot(lower, in_rows)


def locate(idx, side):
    bits = side.bit_length() - 1
    tri = triangles(side)
    xh = one_hot(idx >> (2 * bits), side)
    yh = one_hot((idx >> bits) & (side - 1), side)
    zh = one_hot(idx & (side - 1), side)
    columns = jnp.minimum(dot_nt(xh, yh), 1.0).astype(BF16)
    slots = prefix(columns, tri).astype(BF16)
    slot = jnp.sum(xh.astype(F32) * dot(slots, yh), axis=0, keepdims=True)
    ch = one_hot(slot.astype(jnp.int32), STICK_DEV)
    cells = dot_nt(zh, ch)
    ranks = prefix(cells.astype(BF16), tri)
    high = jnp.floor(ranks * (1.0 / side))
    low = ranks - high * side
    looked = dot(high.astype(BF16), ch) * side + dot(low.astype(BF16), ch)
    rank = jnp.sum(zh.astype(F32) * looked, axis=0, keepdims=True)
    return xh, yh, ch, slot, cells, rank.astype(jnp.int32)


def sort_kernel(side, groups, me_ref, idx_ref, x_hbm, *refs):
    outs, (re_ref, im_ref, rank_ref, x_ref, wide, pieces, sem) = refs[: groups * CHUNKS], refs[groups * CHUNKS :]
    fetch = pltpu.make_async_copy(x_hbm, x_ref, sem)
    fetch.start()
    xh, yh, ch, slot_of, cells, rank = locate(idx_ref[...], side)
    rank_ref[...] = rank
    waves = rank.shape[1]
    both = x_ref.shape[0]
    bands = both // 2
    share = bands // groups
    rows = 2 * share // CHUNKS
    cells = jnp.concatenate([cells[i : i + rows] for i in range(0, side, rows)], axis=1)
    tiles = waves // LANES
    in_tile = one_hot(rank & (LANES - 1), LANES)
    col = dot_nt(one_hot(rank >> 7, tiles) * slot_of.astype(BF16), in_tile)
    steps = lax.broadcasted_iota(jnp.int32, (8, side), 1).astype(F32).astype(BF16)
    place = [dot_nt(steps, jnp.minimum(dot_nt(ch, hot), 1.0).astype(BF16)) for hot in (xh, yh)]
    lines = [col, jnp.concatenate(place, axis=1)]
    spare = -(tiles + 8) % rows
    if spare:
        lines.append(jnp.zeros((spare, LANES), F32))
    lines = jnp.concatenate(lines, axis=0)
    lines = [lines[i : i + rows] for i in range(0, lines.shape[0], rows)]
    extra = jnp.concatenate([cells] + lines, axis=1).astype(BF16)
    low = one_hot(rank & 255, 256)
    for shift in range(groups):
        outs[shift * CHUNKS][:, waves:] = extra
    fetch.wait()
    parts = waves // 256
    step = 2 if parts % 2 == 0 else 1
    half = share // CHUNKS
    for first in range(0, parts, step):
        for part in range(first, first + step):
            mask = jnp.where((rank >> 8) == part, 1.0, 0.0).astype(BF16)
            wide[part * both : (part + 1) * both] = x_ref[...] * mask
        rows_now = slice(first * both, (first + step) * both)
        pieces[rows_now] = dot_nt(wide[rows_now], low)
        for part in range(first, first + step):
            here = slice(part * 256, (part + 1) * 256)
            re_ref[:, here] = pieces[part * both : part * both + bands].astype(BF16)
            im_ref[:, here] = pieces[part * both + bands : (part + 1) * both].astype(BF16)
            for shift in range(groups):
                begin = pl.multiple_of(part * both + (me_ref[0] ^ shift) * share, 8)
                re = pieces[pl.ds(begin, share)]
                im = pieces[pl.ds(begin + bands, share)]
                for c in range(CHUNKS):
                    mine = slice(c * half, (c + 1) * half)
                    outs[shift * CHUNKS + c][:, here] = jnp.concatenate(
                        [re[mine], im[mine]], axis=0
                    ).astype(BF16)


def field_kernel(side, chunks, pot_ref, field_ref):
    half = side // 2
    lane = lax.broadcasted_iota(jnp.int32, (side, LANES), 1)
    first = lane < side
    flipped = (lane & side) + ((side - (lane & (side - 1))) & (side - 1))

    def pair(row_a, row_b):
        p = jnp.where(first, row_a, pltpu.roll(row_b, side, 1))
        q = jnp.where(first, pltpu.roll(row_a, side, 1), row_b)
        return p, q

    def plane(y):
        return pot_ref[pl.ds(y, side, stride=side), :]

    def mirror(y):
        if y == 0 or y >= half:
            return jnp.zeros((side, LANES), F32)
        return jnp.take_along_axis(plane(side - y), flipped, axis=1)

    zero = jnp.zeros((side, LANES), F32)
    for k in range(chunks):
        ya, yb = 2 * k, 2 * k + 1
        here = slice(k * LANES, (k + 1) * LANES)
        values = pair(plane(ya), plane(yb) if yb <= half else zero) + pair(mirror(ya), mirror(yb))
        for i, value in enumerate(values):
            field_ref[i, :, here] = value.astype(BF16)


def select_kernel(order_ref, in_ref, out_ref, sems):
    copies = []
    for i in range(out_ref.shape[0]):
        copy = pltpu.make_async_copy(in_ref.at[order_ref[i]], out_ref.at[i], sems.at[i])
        copy.start()
        copies.append(copy)
    for copy in copies:
        copy.wait()


def choose(code, mask, sources, out_ref):
    for name, source in sources.items():

        @pl.when((code & mask) == name)
        def _(source=source):
            out_ref[...] = source[...]


def stack_kernel(re_ref, im_ref, xn_ref, yn_ref, out_ref):
    half = re_ref.shape[0]
    for k, ref in enumerate((re_ref, im_ref, xn_ref, yn_ref)):
        out_ref[k * half : (k + 1) * half] = ref[...]


def seen(own_re, own_im, xn, yn, other):
    half = own_re.shape[0]
    sib_re, sib_im, xns, yns = [other.at[k * half : (k + 1) * half] for k in range(4)]
    return {0: own_re, 1: sib_re, 2: xn, 3: xns}, {0: own_im, 1: sib_im, 4: yn, 5: yns}


def route_kernel(order_ref, i_ref, own_re, own_im, xn, yn, other, re_ref, im_ref):
    i = i_ref[0]
    near_re, near_im = seen(own_re, own_im, xn, yn, other)
    choose(order_ref[i ^ 4] ^ i, 3, near_re, re_ref)
    choose(order_ref[i ^ 2] ^ i, 5, near_im, im_ref)


def couple_routed_kernel(
    order_ref, i_ref, own_re, own_im, xn, yn, other, far_re, far_im, sorted_ref, g_ref, partner,
):
    i = i_ref[0]
    half = own_re.shape[0]
    code = order_ref[i] ^ i
    re_ref, im_ref = partner.at[:half], partner.at[half:]
    near_re, near_im = seen(own_re, own_im, xn, yn, other)
    choose(code, 7, {**near_re, **{4 + name: far_re for name in near_re}}, re_ref)
    choose(code, 7, {**near_im, **{2 + name: far_im for name in near_im}}, im_ref)
    couple_kernel(partner, sorted_ref, g_ref)


def build_tables(side, chunks, waves, x_refs, cs_ref, tab_ref, spot_ref, col_ref, start_ref, cyr_ref, syr_ref):
    rows = x_refs[0].shape[0]
    parts = side // rows
    tiles = waves // LANES
    cells_end = waves + parts * STICK_DEV
    tri = triangles(side)
    ahead = jnp.where(
        lax.broadcasted_iota(jnp.int32, (side, LANES), 0)
        < lax.broadcasted_iota(jnp.int32, (side, LANES), 1),
        1.0, 0.0,
    ).astype(BF16)
    left = lax.broadcasted_iota(jnp.int32, (tiles, LANES), 1) < STICK_DEV
    first = lax.broadcasted_iota(jnp.int32, (side, LANES), 1) < side
    for ref, begin in ((cyr_ref, 0), (syr_ref, LANES)):
        table = cs_ref[:, begin : begin + side].astype(F32)
        for k in range(chunks):
            ya, yb = (2 * k) % side, (2 * k + 1) % side
            ref[:, k * LANES : (k + 1) * LANES] = jnp.where(
                first, table[:, ya : ya + 1], table[:, yb : yb + 1]
            ).astype(BF16)
    at_x, at_y = [], []
    for d, x_ref in enumerate(x_refs):
        cells = jnp.concatenate(
            [x_ref[:, waves + i * STICK_DEV : waves + (i + 1) * STICK_DEV].astype(F32) for i in range(parts)],
            axis=0,
        )
        lines = jnp.concatenate(
            [
                x_ref[:, i : i + LANES].astype(F32)
                for i in range(cells_end, cells_end + -(-(tiles + 8) // rows) * LANES, LANES)
            ],
            axis=0,
        )
        place = lines[tiles : tiles + 1].astype(jnp.int32)
        at_x.append(one_hot(place[:, :side], side).astype(F32).T)
        at_y.append(one_hot(place[:, side:], side).astype(F32).T)
        ranks = prefix(cells.astype(BF16), tri)
        begins = jnp.minimum(jnp.floor(ranks[:, :1] * (1.0 / STICK_DEV)), waves // STICK_DEV - 1.0)
        spot = jnp.where(cells > 0.5, ranks - begins * STICK_DEV, -1.0)
        spot_ref[d] = jnp.concatenate([spot, spot], axis=1)
        level = dot_nt(jnp.ones((8, STICK_DEV), BF16), cells.astype(BF16))
        start_ref[d : d + 1, :] = dot(level.astype(BF16), ahead)[:1].astype(jnp.int32)
        col = lines[:tiles] + float((d % 2) * STICK_DEV)
        turned = pltpu.roll(col, STICK_DEV, 1)
        after = jnp.concatenate([turned[1:], turned[:1]], axis=0)
        col_ref[0, d] = col.astype(jnp.int32)
        col_ref[1, d] = jnp.where(left, turned, after).astype(jnp.int32)
    at_x = jnp.concatenate(at_x, axis=0).astype(BF16)
    at_y = jnp.concatenate(at_y, axis=0).astype(BF16)
    both = dot(at_x, cs_ref[...])
    cx, sx = both[:, :LANES], both[:, LANES:]
    for k in range(chunks):
        cy = dot(at_y, cyr_ref[:, k * LANES : (k + 1) * LANES])
        sy = dot(at_y, syr_ref[:, k * LANES : (k + 1) * LANES])
        base = 2 * k * LANES
        tab_ref[:, base : base + LANES] = (cy * cx - sy * sx).astype(BF16)
        tab_ref[:, base + LANES : base + 2 * LANES] = (cy * sx + sy * cx).astype(BF16)


def box_first_kernel(side, chunks, team, waves, groups, gates, *refs):
    x_refs, refs = refs[:groups], refs[groups:]
    (field_ref, cs_ref, wz_ref), refs = refs[:3], refs[3 + gates :]
    out_refs, refs = refs[:groups], refs[groups:]
    (tab_ref, spot_ref, col_ref, start_ref), refs = refs[:4], refs[4:]
    *scratch, cyr_ref, syr_ref, start_s, sem = refs
    build_tables(
        side, chunks, waves, x_refs, cs_ref, tab_ref, spot_ref, col_ref, start_ref, cyr_ref, syr_ref
    )
    to_scalars = pltpu.make_async_copy(start_ref, start_s, sem)
    to_scalars.start()
    to_scalars.wait()
    box_work(
        side, chunks, team, waves, x_refs, field_ref, wz_ref, tab_ref, spot_ref, col_ref, start_s,
        out_refs, *scratch,
    )


def box_next_kernel(side, chunks, team, waves, groups, *refs):
    x_refs, refs = refs[:groups], refs[groups:]
    (field_ref, wz_ref, tab_ref, spot_ref, col_ref, start_s), refs = refs[:6], refs[6:]
    out_refs, scratch = refs[:groups], refs[groups:]
    box_work(
        side, chunks, team, waves, x_refs, field_ref, wz_ref, tab_ref, spot_ref, col_ref, start_s,
        out_refs, *scratch,
    )


def box_work(
    side, chunks, team, waves, x_refs, field_ref, wz_ref, tab_ref, spot_ref, col_ref, start_s,
    out_refs, xf, grid, t_scr, l_scr, acc,
):
    groups = len(x_refs)
    rows = x_refs[0].shape[0]
    bands = rows // 2
    blocks = rows // 8
    span = 2 * side
    for d in range(groups):
        value = x_refs[d][:, :waves].astype(F32)
        xf[0, d] = value
        xf[1, d] = jnp.concatenate([value[:, STICK_DEV:], value[:, :STICK_DEV]], axis=1)
        acc[0, d] = jnp.zeros((rows, waves), F32)
        acc[1, d] = jnp.zeros((rows, waves), F32)
    lane = lax.broadcasted_iota(jnp.int32, (8, LANES), 1)
    left = lane < STICK_DEV

    def window(z, d):
        begin = jnp.minimum(start_s[d, z] >> 6, waves // STICK_DEV - 1)
        tile = begin >> 1
        return begin & 1, tile, pl.ds(pl.multiple_of(tile * LANES, LANES), LANES), begin * STICK_DEV

    def expand(z):
        for dp in range(groups // 2):
            spot = jnp.where(
                left,
                jnp.broadcast_to(spot_ref[2 * dp, pl.ds(z, 1), :], (8, LANES)),
                jnp.broadcast_to(spot_ref[2 * dp + 1, pl.ds(z, 1), :], (8, LANES)),
            )
            valid = spot >= 0.0
            at = jnp.maximum(spot, 0.0).astype(jnp.int32)
            odd_a, _, lanes_a, _ = window(z, 2 * dp)
            odd_b, _, lanes_b, _ = window(z, 2 * dp + 1)
            for block in range(blocks):
                part = slice(block * 8, (block + 1) * 8)
                a = jnp.take_along_axis(xf[odd_a, 2 * dp, part, lanes_a], at, axis=1)
                b = jnp.take_along_axis(xf[odd_b, 2 * dp + 1, part, lanes_b], at, axis=1)
                value = jnp.where(valid, jnp.where(left, a, b), 0.0)
                grid[dp, pl.ds(block * 8 * side + z, 8, stride=side), :] = value

    def collect(z):
        for dp in range(groups // 2):
            sources = [
                grid[dp, pl.ds(block * 8 * side + z, 8, stride=side), :] for block in range(blocks)
            ]
            for d in (2 * dp, 2 * dp + 1):
                odd, tile, lanes, base = window(z, d)
                at = jnp.broadcast_to(col_ref[odd, d, pl.ds(tile, 1), :], (8, LANES))
                mask = (lane >= start_s[d, z] - base) & (lane < start_s[d, z + 1] - base)
                for block in range(blocks):
                    part = slice(block * 8, (block + 1) * 8)
                    value = jnp.take_along_axis(sources[block], at, axis=1)
                    acc[odd, d, part, lanes] = jnp.where(mask, value, acc[odd, d, part, lanes])

    def levels(step):
        def body(i, carry):
            for j in range(UNROLL):
                step(i * UNROLL + j)
            return carry

        lax.fori_loop(0, side // UNROLL, body, 0)

    levels(expand)

    def depth_in(g, carry):
        for b in [g * team + i for i in range(team)]:
            both = jnp.concatenate(
                [
                    jnp.concatenate(
                        [
                            grid[n, pl.ds(b * side, side), :].astype(BF16),
                            grid[n, pl.ds((bands + b) * side, side), :].astype(BF16),
                        ],
                        axis=0,
                    )
                    for n in range(groups // 2)
                ],
                axis=1,
            )
            t_scr[pl.ds(b * span, span), :] = dot(wz_ref[0], both).astype(BF16)
        return carry

    lax.fori_loop(0, bands // team, depth_in, 0)

    def planes(g, carry):
        rows_g = pl.ds(g * team * span, team * span)
        sticks = t_scr[rows_g, :]
        for k in range(chunks):
            here = slice(k * LANES, (k + 1) * LANES)
            wide = slice(2 * k * LANES, 2 * (k + 1) * LANES)
            ab = dot(sticks, tab_ref[:, wide])
            p, q = field_ref[0, :, here], field_ref[1, :, here]
            p2, q2 = field_ref[2, :, here], field_ref[3, :, here]
            for b in range(team):
                u, x = ab[b * span : b * span + side, :LANES], ab[b * span : b * span + side, LANES:]
                w, v = ab[b * span + side : (b + 1) * span, :LANES], ab[b * span + side : (b + 1) * span, LANES:]
                pr, pi, mr, mi = [t.astype(BF16) for t in (u - v, w + x, u + v, w - x)]
                ar, ai = p * pr - q * pi, p * pi + q * pr
                br, bi = p2 * mr - q2 * mi, p2 * mi + q2 * mr
                even = jnp.concatenate([ar + br, ai + bi], axis=0)
                odd = jnp.concatenate([ai - bi, br - ar], axis=0)
                l_scr[b * span : (b + 1) * span, wide] = jnp.concatenate([even, odd], axis=1)
        back = dot_nt(l_scr[...], tab_ref[...]).astype(BF16)
        for b in range(team):
            done = dot(wz_ref[1], back[b * span : (b + 1) * span])
            for n in range(groups // 2):
                here = slice(n * LANES, (n + 1) * LANES)
                grid[n, pl.ds((g * team + b) * side, side), :] = done[:side, here]
                grid[n, pl.ds((bands + g * team + b) * side, side), :] = done[side:, here]
        return carry

    lax.fori_loop(0, bands // team, planes, 0)

    levels(collect)
    for d in range(groups):
        late = acc[1, d]
        late = jnp.concatenate([late[:, waves - STICK_DEV :], late[:, : waves - STICK_DEV]], axis=1)
        out_refs[d][...] = (acc[0, d] + late).astype(BF16)


def arrange_kernel(groups, me_ref, *refs):
    y_refs, (rows_ref,) = refs[:groups], refs[groups:]
    part = y_refs[0].shape[0] // 2
    half = groups * part
    me = me_ref[0]
    for j in range(groups // 2):
        one, other = y_refs[2 * j][...].astype(F32), y_refs[2 * j + 1][...].astype(F32)
        low = jnp.where((me & 1) == 0, one, other)
        high = jnp.where((me & 1) == 0, other, one)
        begin = pl.multiple_of(((me >> 1) ^ j) * (2 * part), 8)
        rows_ref[pl.ds(begin, 2 * part)] = jnp.concatenate([low[:part], high[:part]], axis=0)
        rows_ref[pl.ds(begin + half, 2 * part)] = jnp.concatenate([low[part:], high[part:]], axis=0)


def join_kernel(groups, me_ref, *refs):
    rows_refs, refs = refs[: CHUNKS - 1], refs[CHUNKS - 1 :]
    sorted_ref, rows_scr = refs[groups:]
    arrange_kernel(groups, me_ref, *refs[:groups], rows_scr)
    values = [ref[...] for ref in (*rows_refs, rows_scr)]
    part = values[0].shape[0] // (2 * groups)
    sorted_ref[...] = jnp.concatenate(
        [v[i * part : (i + 1) * part] for i in range(2 * groups) for v in values], axis=0
    ).astype(BF16)


def couple_kernel(partner_ref, sorted_ref, g_ref):
    products = dot_nt(partner_ref[...], sorted_ref[...])
    half = products.shape[0] // 2
    g_ref[0] = (products[:half, :half] + products[half:, half:]).astype(BF16)
    g_ref[1] = (products[:half, half:] - products[half:, :half]).astype(BF16)


def unsort_kernel(y_ref, rank_ref, out_ref):
    both, waves = y_ref.shape
    parts = waves // 256
    stacked = jnp.concatenate([y_ref[:, i * 256 : (i + 1) * 256] for i in range(parts)], axis=0)
    for tile in range(parts):
        here = slice(tile * 256, (tile + 1) * 256)
        rank = rank_ref[:, here]
        values = dot(stacked, one_hot(rank & 255, 256))
        total = None
        for part in range(parts):
            value = jnp.where((rank >> 8) == part, values[part * both : (part + 1) * both], 0.0)
            total = value if total is None else total + value
        out_ref[:, here] = total.astype(BF16)


def whole(memory=pltpu.VMEM):
    return pl.BlockSpec(memory_space=memory)


def params(limit=VMEM_LIMIT):
    return pltpu.CompilerParams(vmem_limit_bytes=limit)


def shards(orbitals, box_index, partner_pool, potential):
    fft_count = lax.axis_size("fft")
    side = potential.shape[0]
    bands = orbitals.shape[2]
    waves = orbitals.shape[3]
    share = bands // fft_count
    columns = STICK_DEV * fft_count
    chunks = (side // 2 + 1 + 1) // 2
    coeffs = orbitals.reshape(2 * bands, waves)

    cosine, sine = cos_sin(side)
    cs = jnp.asarray(np.concatenate([cosine, cosine, sine, sine], axis=1))
    inward = np.block([[cosine, -sine], [sine, cosine]])
    outward = np.block([[cosine, sine], [-sine, cosine]])
    wz = jnp.asarray(np.stack([inward, outward]))

    me = lax.axis_index("fft")
    me_row = me.reshape(1)
    pairs = [[(i, i ^ s) for i in range(fft_count)] for s in range(fft_count)]
    pool_count = lax.axis_size("pool")
    rows = 2 * share // CHUNKS
    tiles = waves // LANES
    packed = waves + side * STICK_DEV // rows + -(-(tiles + 8) // rows) * LANES
    scalars, blocks = whole(pltpu.SMEM), [whole()] * fft_count

    *ordered, own_re, own_im, rank = pl.pallas_call(
        functools.partial(sort_kernel, side, fft_count),
        out_shape=[
            jax.ShapeDtypeStruct((rows, waves if c else packed), BF16)
            for _ in range(fft_count)
            for c in range(CHUNKS)
        ]
        + [
            jax.ShapeDtypeStruct((bands, waves), BF16),
            jax.ShapeDtypeStruct((bands, waves), BF16),
            jax.ShapeDtypeStruct((1, waves), jnp.int32),
        ],
        in_specs=[scalars, whole(), whole(pltpu.HBM)],
        out_specs=blocks * CHUNKS + [whole()] * 3,
        scratch_shapes=[
            pltpu.VMEM((2 * bands, waves), BF16),
            pltpu.VMEM((waves // 256 * 2 * bands, waves), BF16),
            pltpu.VMEM((waves // 256 * 2 * bands, 256), F32),
            pltpu.SemaphoreType.DMA,
        ],
        compiler_params=params(SORT_LIMIT),
        name="sort_waves",
    )(me_row, box_index.reshape(1, waves), coeffs)
    moved = [
        [ordered[c]] + [lax.ppermute(ordered[s * CHUNKS + c], "fft", pairs[s]) for s in range(1, fft_count)]
        for c in range(CHUNKS)
    ]

    routed = pool_count == 8
    half_rows = jax.ShapeDtypeStruct((bands, waves), BF16)
    pool_row = lax.axis_index("pool").reshape(1)
    if routed:
        swaps = {m: [(i, i ^ m) for i in range(pool_count)] for m in (1, 2, 4)}
        xn = lax.ppermute(own_re, "pool", swaps[2])
        yn = lax.ppermute(own_im, "pool", swaps[4])
        stacked = pl.pallas_call(
            stack_kernel,
            out_shape=jax.ShapeDtypeStruct((4 * bands, waves), BF16),
            in_specs=[whole()] * 4,
            out_specs=whole(),
            compiler_params=params(),
            name="stack",
        )(own_re, own_im, xn, yn)
        other = lax.ppermute(stacked, "pool", swaps[1])
        near = [own_re, own_im, xn, yn, other]
    else:
        spread = lax.all_to_all(
            jnp.concatenate([own_re, own_im]).reshape(pool_count, 2 * bands // pool_count, waves),
            "pool", 0, 0, tiled=True,
        )
        near = []

    field = pl.pallas_call(
        functools.partial(field_kernel, side, chunks),
        out_shape=jax.ShapeDtypeStruct((4, side, chunks * LANES), BF16),
        in_specs=[whole()],
        out_specs=whole(),
        compiler_params=params(),
        cost_estimate=pl.CostEstimate(flops=10**9, bytes_accessed=10**6, transcendentals=0),
        name="field_pairs",
    )(potential.reshape(side * side, 2 * side))

    gates = [xn, yn] if routed else []
    team = min(8, rows // 2)
    scratch = [
        pltpu.VMEM((2, fft_count, rows, waves), F32),
        pltpu.VMEM((columns // LANES, rows * side, LANES), F32),
        pltpu.VMEM((rows * side, columns), BF16),
        pltpu.VMEM((team * 2 * side, 2 * chunks * LANES), BF16),
        pltpu.VMEM((2, fft_count, rows, waves), F32),
    ]
    cost = pl.CostEstimate(flops=BOX_COST, bytes_accessed=10**7, transcendentals=0)
    shapes = [jax.ShapeDtypeStruct((rows, waves), BF16)] * fft_count
    *back, tab, spot, col, start = pl.pallas_call(
        functools.partial(box_first_kernel, side, chunks, team, waves, fft_count, len(gates)),
        out_shape=shapes
        + [
            jax.ShapeDtypeStruct((columns, 2 * chunks * LANES), BF16),
            jax.ShapeDtypeStruct((fft_count, side, 2 * STICK_DEV), F32),
            jax.ShapeDtypeStruct((2, fft_count, tiles, LANES), jnp.int32),
            jax.ShapeDtypeStruct((fft_count, LANES), jnp.int32),
        ],
        in_specs=blocks + [whole()] * 3 + [whole(pl.ANY)] * len(gates),
        out_specs=blocks + [whole()] * 4,
        scratch_shapes=scratch
        + [pltpu.VMEM((side, chunks * LANES), BF16)] * 2
        + [pltpu.SMEM((fft_count, LANES), jnp.int32), pltpu.SemaphoreType.DMA],
        compiler_params=params(),
        cost_estimate=cost,
        name="box_first",
    )(*moved[0], field, cs, wz, *gates)
    returned = [[back[0]] + [lax.ppermute(back[s], "fft", pairs[s]) for s in range(1, fft_count)]]
    for c in range(1, CHUNKS):
        back = pl.pallas_call(
            functools.partial(box_next_kernel, side, chunks, team, waves, fft_count),
            out_shape=shapes,
            in_specs=blocks + [whole()] * 5 + [scalars],
            out_specs=blocks,
            scratch_shapes=scratch,
            compiler_params=params(),
            cost_estimate=cost,
            name="box_next",
        )(*moved[c], field, wz, tab, spot, col, start)
        returned.append(
            [back[0]] + [lax.ppermute(back[s], "fft", pairs[s]) for s in range(1, fft_count)]
        )

    if not routed:
        chosen = pl.pallas_call(
            select_kernel,
            out_shape=jax.ShapeDtypeStruct(spread.shape, BF16),
            in_specs=[scalars, whole(pl.ANY)],
            out_specs=whole(pl.ANY),
            scratch_shapes=[pltpu.SemaphoreType.DMA((pool_count,))],
            compiler_params=params(),
            name="select_partner",
        )(partner_pool, spread)
        partner = lax.all_to_all(chosen, "pool", 0, 0, tiled=True).reshape(2 * bands, waves)
    else:
        far_re, far_im = pl.pallas_call(
            route_kernel,
            out_shape=(half_rows, half_rows),
            in_specs=[scalars] * 2 + [whole()] * len(near),
            out_specs=(whole(), whole()),
            compiler_params=params(),
            name="route_partner",
        )(partner_pool, pool_row, *near)
        far_re = lax.ppermute(far_re, "pool", swaps[4])
        far_im = lax.ppermute(far_im, "pool", swaps[2])

    arranged = [
        pl.pallas_call(
            functools.partial(arrange_kernel, fft_count),
            out_shape=jax.ShapeDtypeStruct((rows * fft_count, waves), F32),
            in_specs=[scalars] + blocks,
            out_specs=whole(),
            compiler_params=params(),
            cost_estimate=pl.CostEstimate(
                flops=ARRANGE_COST, bytes_accessed=10**6, transcendentals=0
            ),
            name="arrange",
        )(me_row, *returned[c])
        for c in range(CHUNKS - 1)
    ]
    sorted_response = pl.pallas_call(
        functools.partial(join_kernel, fft_count),
        out_shape=jax.ShapeDtypeStruct((2 * bands, waves), BF16),
        in_specs=[scalars] + [whole()] * (CHUNKS - 1) + blocks,
        out_specs=whole(),
        scratch_shapes=[pltpu.VMEM((rows * fft_count, waves), F32)],
        compiler_params=params(),
        cost_estimate=pl.CostEstimate(flops=JOIN_COST, bytes_accessed=10**6, transcendentals=0),
        name="join",
    )(me_row, *arranged, *returned[-1])
    sums_shape = jax.ShapeDtypeStruct((2, bands, bands), BF16)
    if routed:
        sums = pl.pallas_call(
            couple_routed_kernel,
            out_shape=sums_shape,
            in_specs=[scalars] * 2 + [whole()] * (len(near) + 3),
            out_specs=whole(),
            scratch_shapes=[pltpu.VMEM((2 * bands, waves), BF16)],
            compiler_params=params(),
            name="couple",
        )(partner_pool, pool_row, *near, far_re, far_im, sorted_response)
    else:
        sums = pl.pallas_call(
            couple_kernel,
            out_shape=sums_shape,
            in_specs=[whole(), whole()],
            out_specs=whole(),
            compiler_params=params(),
            name="couple",
        )(partner, sorted_response)
    shares = [sums] + [lax.ppermute(sums, "fft", pairs[s]) for s in range(1, fft_count)]
    response = pl.pallas_call(
        unsort_kernel,
        out_shape=jax.ShapeDtypeStruct((2 * bands, waves), BF16),
        in_specs=[whole(), whole()],
        out_specs=whole(),
        compiler_params=params(),
        cost_estimate=pl.CostEstimate(flops=10**9, bytes_accessed=10**7, transcendentals=0),
        name="unsort",
    )(sorted_response, rank)
    summed = None
    for d in range(fft_count):
        offset = me ^ d
        term = shares[0]
        for s in range(1, fft_count):
            term = jnp.where(offset == s, shares[s], term)
        term = term.astype(F32)
        summed = term if summed is None else summed + term
    coupling = (summed / jnp.sqrt(jnp.float32(waves * fft_count)))[:, None]
    return response.reshape(2, 1, bands, waves), coupling


def solution(mesh):
    placed = (P(None, "pool", None, "fft"), P("fft"), P(), P())
    return jax.shard_map(
        shards,
        mesh=mesh,
        in_specs=placed,
        out_specs=(P(None, "pool", None, "fft"), P(None, "pool", None, None)),
        check_vma=False,
    )
```

```python
import functools

import jax
import jax.numpy as jnp
import ml_dtypes
import numpy as np
from jax import lax
from jax.experimental import pallas as pl
from jax.experimental.pallas import tpu as pltpu
from jax.sharding import PartitionSpec as P

STICK_DEV = 64
LANES = 128
UNROLL = 16
BF16 = jnp.bfloat16
F32 = jnp.float32
VMEM_LIMIT = 24 * 1024 * 1024
SORT_LIMIT = 24 * 1024 * 1024
JOIN_COST = 10**11
MARK_COST = 3*10**9
BOX_COST = 10**10


def cos_sin(side):
    points = np.arange(side)
    angles = (2.0 * np.pi / side) * (points[:, None] * points[None, :] % side)
    scaling = 1.0 / np.sqrt(side)
    cosine = (np.cos(angles) * scaling).astype(ml_dtypes.bfloat16)
    sine = (np.sin(angles) * scaling).astype(ml_dtypes.bfloat16)
    return cosine, sine


def dot(a, b):
    return jnp.dot(a, b, preferred_element_type=F32)


def dot_nt(a, b):
    return lax.dot_general(a, b, (((1,), (1,)), ((), ())), preferred_element_type=F32)


def one_hot(row, count):
    places = lax.broadcasted_iota(jnp.int32, (count, row.shape[1]), 0)
    return jnp.where(places == row, 1.0, 0.0).astype(BF16)


def triangles(side):
    rows = lax.broadcasted_iota(jnp.int32, (side, side), 0)
    cols = lax.broadcasted_iota(jnp.int32, (side, side), 1)
    upper = jnp.where(rows < cols, 1.0, 0.0).astype(BF16)
    lower = jnp.where(rows > cols, 1.0, 0.0).astype(BF16)
    return upper, lower, jnp.ones((side, side), BF16)


def prefix(occupied, tri):
    upper, lower, ones = tri
    in_rows = dot(occupied, ones).astype(BF16)
    return dot(occupied, upper) + dot(lower, in_rows)


def locate(idx, side):
    bits = side.bit_length() - 1
    tri = triangles(side)
    xh = one_hot(idx >> (2 * bits), side)
    yh = one_hot((idx >> bits) & (side - 1), side)
    zh = one_hot(idx & (side - 1), side)
    columns = jnp.minimum(dot_nt(xh, yh), 1.0).astype(BF16)
    slots = prefix(columns, tri).astype(BF16)
    slot = jnp.sum(xh.astype(F32) * dot(slots, yh), axis=0, keepdims=True)
    ch = one_hot(slot.astype(jnp.int32), STICK_DEV)
    cells = dot_nt(zh, ch)
    ranks = prefix(cells.astype(BF16), tri)
    high = jnp.floor(ranks * (1.0 / side))
    low = ranks - high * side
    looked = dot(high.astype(BF16), ch) * side + dot(low.astype(BF16), ch)
    rank = jnp.sum(zh.astype(F32) * looked, axis=0, keepdims=True)
    return xh, yh, ch, slot, cells, rank.astype(jnp.int32)


def sort_kernel(side, groups, me_ref, idx_ref, x_hbm, *refs):
    outs, (re_ref, im_ref, rank_ref, x_ref, wide, pieces, sem) = refs[:groups], refs[groups:]
    fetch = pltpu.make_async_copy(x_hbm, x_ref, sem)
    fetch.start()
    xh, yh, ch, slot_of, cells, rank = locate(idx_ref[...], side)
    rank_ref[...] = rank
    waves = rank.shape[1]
    both = x_ref.shape[0]
    bands = both // 2
    share = bands // groups
    rows = 2 * share
    cells = jnp.concatenate([cells[i : i + rows] for i in range(0, side, rows)], axis=1)
    tiles = waves // LANES
    in_tile = one_hot(rank & (LANES - 1), LANES)
    col = dot_nt(one_hot(rank >> 7, tiles) * slot_of.astype(BF16), in_tile)
    steps = lax.broadcasted_iota(jnp.int32, (8, side), 1).astype(F32).astype(BF16)
    place = [dot_nt(steps, jnp.minimum(dot_nt(ch, hot), 1.0).astype(BF16)) for hot in (xh, yh)]
    lines = [col, jnp.concatenate(place, axis=1)]
    spare = -(tiles + 8) % rows
    if spare:
        lines.append(jnp.zeros((spare, LANES), F32))
    lines = jnp.concatenate(lines, axis=0)
    lines = [lines[i : i + rows] for i in range(0, lines.shape[0], rows)]
    extra = jnp.concatenate([cells] + lines, axis=1).astype(BF16)
    low = one_hot(rank & 255, 256)
    for shift in range(groups):
        outs[shift][:, waves:] = extra
    fetch.wait()
    parts = waves // 256
    step = 2 if parts % 2 == 0 else 1
    for first in range(0, parts, step):
        for part in range(first, first + step):
            mask = jnp.where((rank >> 8) == part, 1.0, 0.0).astype(BF16)
            wide[part * both : (part + 1) * both] = x_ref[...] * mask
        rows_now = slice(first * both, (first + step) * both)
        pieces[rows_now] = dot_nt(wide[rows_now], low)
        for part in range(first, first + step):
            here = slice(part * 256, (part + 1) * 256)
            re_ref[:, here] = pieces[part * both : part * both + bands].astype(BF16)
            im_ref[:, here] = pieces[part * both + bands : (part + 1) * both].astype(BF16)
            for shift in range(groups):
                begin = pl.multiple_of(part * both + (me_ref[0] ^ shift) * share, 8)
                re = pieces[pl.ds(begin, share)]
                im = pieces[pl.ds(begin + bands, share)]
                outs[shift][:, here] = jnp.concatenate([re, im], axis=0).astype(BF16)


def field_kernel(side, chunks, pot_ref, field_ref):
    half = side // 2
    lane = lax.broadcasted_iota(jnp.int32, (side, LANES), 1)
    first = lane < side
    flipped = (lane & side) + ((side - (lane & (side - 1))) & (side - 1))

    def pair(row_a, row_b):
        p = jnp.where(first, row_a, pltpu.roll(row_b, side, 1))
        q = jnp.where(first, pltpu.roll(row_a, side, 1), row_b)
        return p, q

    def plane(y):
        return pot_ref[pl.ds(y, side, stride=side), :]

    def mirror(y):
        if y == 0 or y >= half:
            return jnp.zeros((side, LANES), F32)
        return jnp.take_along_axis(plane(side - y), flipped, axis=1)

    zero = jnp.zeros((side, LANES), F32)
    for k in range(chunks):
        ya, yb = 2 * k, 2 * k + 1
        here = slice(k * LANES, (k + 1) * LANES)
        values = pair(plane(ya), plane(yb) if yb <= half else zero) + pair(mirror(ya), mirror(yb))
        for i, value in enumerate(values):
            field_ref[i, :, here] = value.astype(BF16)


def select_kernel(order_ref, in_ref, out_ref, sems):
    copies = []
    for i in range(out_ref.shape[0]):
        copy = pltpu.make_async_copy(in_ref.at[order_ref[i]], out_ref.at[i], sems.at[i])
        copy.start()
        copies.append(copy)
    for copy in copies:
        copy.wait()


def mark_kernel(*refs):
    refs[-1][...] = jnp.zeros(refs[-1].shape, F32)


def choose(code, mask, sources, out_ref):
    for name, source in sources.items():

        @pl.when((code & mask) == name)
        def _(source=source):
            out_ref[...] = source[...]


def stack_kernel(re_ref, im_ref, xn_ref, yn_ref, out_ref):
    half = re_ref.shape[0]
    for k, ref in enumerate((re_ref, im_ref, xn_ref, yn_ref)):
        out_ref[k * half : (k + 1) * half] = ref[...]


def seen(own_re, own_im, xn, yn, other):
    half = own_re.shape[0]
    sib_re, sib_im, xns, yns = [other.at[k * half : (k + 1) * half] for k in range(4)]
    return {0: own_re, 1: sib_re, 2: xn, 3: xns}, {0: own_im, 1: sib_im, 4: yn, 5: yns}


def route_kernel(order_ref, i_ref, own_re, own_im, xn, yn, other, re_ref, im_ref):
    i = i_ref[0]
    near_re, near_im = seen(own_re, own_im, xn, yn, other)
    choose(order_ref[i ^ 4] ^ i, 3, near_re, re_ref)
    choose(order_ref[i ^ 2] ^ i, 5, near_im, im_ref)


def couple_routed_kernel(
    order_ref, i_ref, own_re, own_im, xn, yn, other, far_re, far_im, sorted_ref, g_ref, partner,
):
    i = i_ref[0]
    half = own_re.shape[0]
    code = order_ref[i] ^ i
    re_ref, im_ref = partner.at[:half], partner.at[half:]
    near_re, near_im = seen(own_re, own_im, xn, yn, other)
    choose(code, 7, {**near_re, **{4 + name: far_re for name in near_re}}, re_ref)
    choose(code, 7, {**near_im, **{2 + name: far_im for name in near_im}}, im_ref)
    couple_kernel(partner, sorted_ref, g_ref)


def build_tables(side, chunks, waves, x_refs, cs_ref, tab_ref, spot_ref, col_ref, start_ref, cyr_ref, syr_ref):
    rows = x_refs[0].shape[0]
    parts = side // rows
    tiles = waves // LANES
    cells_end = waves + parts * STICK_DEV
    tri = triangles(side)
    ahead = jnp.where(
        lax.broadcasted_iota(jnp.int32, (side, LANES), 0)
        < lax.broadcasted_iota(jnp.int32, (side, LANES), 1),
        1.0, 0.0,
    ).astype(BF16)
    left = lax.broadcasted_iota(jnp.int32, (tiles, LANES), 1) < STICK_DEV
    first = lax.broadcasted_iota(jnp.int32, (side, LANES), 1) < side
    for ref, begin in ((cyr_ref, 0), (syr_ref, LANES)):
        table = cs_ref[:, begin : begin + side].astype(F32)
        for k in range(chunks):
            ya, yb = (2 * k) % side, (2 * k + 1) % side
            ref[:, k * LANES : (k + 1) * LANES] = jnp.where(
                first, table[:, ya : ya + 1], table[:, yb : yb + 1]
            ).astype(BF16)
    at_x, at_y = [], []
    for d, x_ref in enumerate(x_refs):
        cells = jnp.concatenate(
            [x_ref[:, waves + i * STICK_DEV : waves + (i + 1) * STICK_DEV].astype(F32) for i in range(parts)],
            axis=0,
        )
        lines = jnp.concatenate(
            [
                x_ref[:, i : i + LANES].astype(F32)
                for i in range(cells_end, cells_end + -(-(tiles + 8) // rows) * LANES, LANES)
            ],
            axis=0,
        )
        place = lines[tiles : tiles + 1].astype(jnp.int32)
        at_x.append(one_hot(place[:, :side], side).astype(F32).T)
        at_y.append(one_hot(place[:, side:], side).astype(F32).T)
        ranks = prefix(cells.astype(BF16), tri)
        begins = jnp.minimum(jnp.floor(ranks[:, :1] * (1.0 / STICK_DEV)), waves // STICK_DEV - 1.0)
        spot = jnp.where(cells > 0.5, ranks - begins * STICK_DEV, -1.0)
        spot_ref[d] = jnp.concatenate([spot, spot], axis=1)
        level = dot_nt(jnp.ones((8, STICK_DEV), BF16), cells.astype(BF16))
        start_ref[d : d + 1, :] = dot(level.astype(BF16), ahead)[:1].astype(jnp.int32)
        col = lines[:tiles] + float((d % 2) * STICK_DEV)
        turned = pltpu.roll(col, STICK_DEV, 1)
        after = jnp.concatenate([turned[1:], turned[:1]], axis=0)
        col_ref[0, d] = col.astype(jnp.int32)
        col_ref[1, d] = jnp.where(left, turned, after).astype(jnp.int32)
    at_x = jnp.concatenate(at_x, axis=0).astype(BF16)
    at_y = jnp.concatenate(at_y, axis=0).astype(BF16)
    both = dot(at_x, cs_ref[...])
    cx, sx = both[:, :LANES], both[:, LANES:]
    for k in range(chunks):
        cy = dot(at_y, cyr_ref[:, k * LANES : (k + 1) * LANES])
        sy = dot(at_y, syr_ref[:, k * LANES : (k + 1) * LANES])
        base = 2 * k * LANES
        tab_ref[:, base : base + LANES] = (cy * cx - sy * sx).astype(BF16)
        tab_ref[:, base + LANES : base + 2 * LANES] = (cy * sx + sy * cx).astype(BF16)


def box_kernel(side, chunks, team, waves, groups, gates, *refs):
    x_refs, refs = refs[:groups][::-1], refs[groups:]
    (field_ref, cs_ref, wz_ref), refs = refs[:3], refs[3 + gates :]
    out_refs, refs = refs[:groups], refs[groups:]
    *scratch, tab_ref, spot_ref, col_ref, start_ref, cyr_ref, syr_ref, start_s, sem = refs
    build_tables(
        side, chunks, waves, x_refs, cs_ref, tab_ref, spot_ref, col_ref, start_ref, cyr_ref, syr_ref
    )
    to_scalars = pltpu.make_async_copy(start_ref, start_s, sem)
    to_scalars.start()
    to_scalars.wait()
    box_work(
        side, chunks, team, waves, x_refs, field_ref, wz_ref, tab_ref, spot_ref, col_ref, start_s,
        out_refs, *scratch,
    )


def box_work(
    side, chunks, team, waves, x_refs, field_ref, wz_ref, tab_ref, spot_ref, col_ref, start_s,
    out_refs, xf, grid, t_scr, l_scr, acc,
):
    groups = len(x_refs)
    rows = x_refs[0].shape[0]
    bands = rows // 2
    blocks = rows // 8
    span = 2 * side
    for d in range(groups):
        value = x_refs[d][:, :waves].astype(F32)
        xf[0, d] = value
        xf[1, d] = jnp.concatenate([value[:, STICK_DEV:], value[:, :STICK_DEV]], axis=1)
        acc[0, d] = jnp.zeros((rows, waves), F32)
        acc[1, d] = jnp.zeros((rows, waves), F32)
    lane = lax.broadcasted_iota(jnp.int32, (8, LANES), 1)
    left = lane < STICK_DEV

    def window(z, d):
        begin = jnp.minimum(start_s[d, z] >> 6, waves // STICK_DEV - 1)
        tile = begin >> 1
        return begin & 1, tile, pl.ds(pl.multiple_of(tile * LANES, LANES), LANES), begin * STICK_DEV

    def expand(z):
        for dp in range(groups // 2):
            spot = jnp.where(
                left,
                jnp.broadcast_to(spot_ref[2 * dp, pl.ds(z, 1), :], (8, LANES)),
                jnp.broadcast_to(spot_ref[2 * dp + 1, pl.ds(z, 1), :], (8, LANES)),
            )
            valid = spot >= 0.0
            at = jnp.maximum(spot, 0.0).astype(jnp.int32)
            odd_a, _, lanes_a, _ = window(z, 2 * dp)
            odd_b, _, lanes_b, _ = window(z, 2 * dp + 1)
            for block in range(blocks):
                part = slice(block * 8, (block + 1) * 8)
                a = jnp.take_along_axis(xf[odd_a, 2 * dp, part, lanes_a], at, axis=1)
                b = jnp.take_along_axis(xf[odd_b, 2 * dp + 1, part, lanes_b], at, axis=1)
                value = jnp.where(valid, jnp.where(left, a, b), 0.0)
                grid[dp, pl.ds(block * 8 * side + z, 8, stride=side), :] = value

    def collect(z):
        for dp in range(groups // 2):
            sources = [
                grid[dp, pl.ds(block * 8 * side + z, 8, stride=side), :] for block in range(blocks)
            ]
            for d in (2 * dp, 2 * dp + 1):
                odd, tile, lanes, base = window(z, d)
                at = jnp.broadcast_to(col_ref[odd, d, pl.ds(tile, 1), :], (8, LANES))
                mask = (lane >= start_s[d, z] - base) & (lane < start_s[d, z + 1] - base)
                for block in range(blocks):
                    part = slice(block * 8, (block + 1) * 8)
                    value = jnp.take_along_axis(sources[block], at, axis=1)
                    acc[odd, d, part, lanes] = jnp.where(mask, value, acc[odd, d, part, lanes])

    def levels(step):
        def body(i, carry):
            for j in range(UNROLL):
                step(i * UNROLL + j)
            return carry

        lax.fori_loop(0, side // UNROLL, body, 0)

    levels(expand)

    def depth_in(g, carry):
        for b in [g * team + i for i in range(team)]:
            both = jnp.concatenate(
                [
                    jnp.concatenate(
                        [
                            grid[n, pl.ds(b * side, side), :].astype(BF16),
                            grid[n, pl.ds((bands + b) * side, side), :].astype(BF16),
                        ],
                        axis=0,
                    )
                    for n in range(groups // 2)
                ],
                axis=1,
            )
            t_scr[pl.ds(b * span, span), :] = dot(wz_ref[0], both).astype(BF16)
        return carry

    lax.fori_loop(0, bands // team, depth_in, 0)

    def planes(g, carry):
        rows_g = pl.ds(g * team * span, team * span)
        sticks = t_scr[rows_g, :]
        for k in range(chunks):
            here = slice(k * LANES, (k + 1) * LANES)
            wide = slice(2 * k * LANES, 2 * (k + 1) * LANES)
            ab = dot(sticks, tab_ref[:, wide])
            p, q = field_ref[0, :, here], field_ref[1, :, here]
            p2, q2 = field_ref[2, :, here], field_ref[3, :, here]
            for b in range(team):
                u, x = ab[b * span : b * span + side, :LANES], ab[b * span : b * span + side, LANES:]
                w, v = ab[b * span + side : (b + 1) * span, :LANES], ab[b * span + side : (b + 1) * span, LANES:]
                pr, pi, mr, mi = [t.astype(BF16) for t in (u - v, w + x, u + v, w - x)]
                ar, ai = p * pr - q * pi, p * pi + q * pr
                br, bi = p2 * mr - q2 * mi, p2 * mi + q2 * mr
                even = jnp.concatenate([ar + br, ai + bi], axis=0)
                odd = jnp.concatenate([ai - bi, br - ar], axis=0)
                l_scr[b * span : (b + 1) * span, wide] = jnp.concatenate([even, odd], axis=1)
        back = dot_nt(l_scr[...], tab_ref[...]).astype(BF16)
        for b in range(team):
            done = dot(wz_ref[1], back[b * span : (b + 1) * span])
            for n in range(groups // 2):
                here = slice(n * LANES, (n + 1) * LANES)
                grid[n, pl.ds((g * team + b) * side, side), :] = done[:side, here]
                grid[n, pl.ds((bands + g * team + b) * side, side), :] = done[side:, here]
        return carry

    lax.fori_loop(0, bands // team, planes, 0)

    levels(collect)
    for d in range(groups):
        late = acc[1, d]
        late = jnp.concatenate([late[:, waves - STICK_DEV :], late[:, : waves - STICK_DEV]], axis=1)
        out_refs[d][...] = (acc[0, d] + late).astype(BF16)


def join_kernel(groups, me_ref, *refs):
    y_refs, (sorted_ref,) = refs[:groups][::-1], refs[groups:]
    part = y_refs[0].shape[0] // 2
    half = groups * part
    me = me_ref[0]
    even = (me & 1) == 0
    for j in range(groups // 2):
        one, other = y_refs[2 * j][...].astype(F32), y_refs[2 * j + 1][...].astype(F32)
        low = jnp.where(even, one, other)
        high = jnp.where(even, other, one)
        begin = pl.multiple_of(((me >> 1) ^ j) * (2 * part), 16)
        sorted_ref[pl.ds(begin, 2 * part)] = jnp.concatenate(
            [low[:part], high[:part]], axis=0
        ).astype(BF16)
        sorted_ref[pl.ds(begin + half, 2 * part)] = jnp.concatenate(
            [low[part:], high[part:]], axis=0
        ).astype(BF16)


def couple_kernel(partner_ref, sorted_ref, g_ref):
    products = dot_nt(partner_ref[...], sorted_ref[...])
    half = products.shape[0] // 2
    g_ref[0] = (products[:half, :half] + products[half:, half:]).astype(BF16)
    g_ref[1] = (products[:half, half:] - products[half:, :half]).astype(BF16)


def unsort_kernel(y_ref, rank_ref, out_ref):
    both, waves = y_ref.shape
    parts = waves // 256
    stacked = jnp.concatenate([y_ref[:, i * 256 : (i + 1) * 256] for i in range(parts)], axis=0)
    for tile in range(parts):
        here = slice(tile * 256, (tile + 1) * 256)
        rank = rank_ref[:, here]
        values = dot(stacked, one_hot(rank & 255, 256))
        total = None
        for part in range(parts):
            value = jnp.where((rank >> 8) == part, values[part * both : (part + 1) * both], 0.0)
            total = value if total is None else total + value
        out_ref[:, here] = total.astype(BF16)


def exchange(blocks, pairs):
    moved = list(blocks)
    for s in range(len(blocks) - 1, 0, -1):
        moved[s] = lax.ppermute(blocks[s], "fft", pairs[s])
    return moved


def whole(memory=pltpu.VMEM):
    return pl.BlockSpec(memory_space=memory)


def params(limit=VMEM_LIMIT):
    return pltpu.CompilerParams(vmem_limit_bytes=limit)


def shards(orbitals, box_index, partner_pool, potential):
    fft_count = lax.axis_size("fft")
    side = potential.shape[0]
    bands = orbitals.shape[2]
    waves = orbitals.shape[3]
    share = bands // fft_count
    columns = STICK_DEV * fft_count
    chunks = (side // 2 + 1 + 1) // 2
    coeffs = orbitals.reshape(2 * bands, waves)

    cosine, sine = cos_sin(side)
    cs = jnp.asarray(np.concatenate([cosine, cosine, sine, sine], axis=1))
    inward = np.block([[cosine, -sine], [sine, cosine]])
    outward = np.block([[cosine, sine], [-sine, cosine]])
    wz = jnp.asarray(np.stack([inward, outward]))

    me = lax.axis_index("fft")
    me_row = me.reshape(1)
    pairs = [[(i, i ^ s) for i in range(fft_count)] for s in range(fft_count)]
    pool_count = lax.axis_size("pool")
    rows = 2 * share
    tiles = waves // LANES
    packed = waves + side * STICK_DEV // rows + -(-(tiles + 8) // rows) * LANES
    scalars, blocks = whole(pltpu.SMEM), [whole()] * fft_count

    *ordered, own_re, own_im, rank = pl.pallas_call(
        functools.partial(sort_kernel, side, fft_count),
        out_shape=[
            jax.ShapeDtypeStruct((rows, packed), BF16)
            for _ in range(fft_count)
        ]
        + [
            jax.ShapeDtypeStruct((bands, waves), BF16),
            jax.ShapeDtypeStruct((bands, waves), BF16),
            jax.ShapeDtypeStruct((1, waves), jnp.int32),
        ],
        in_specs=[scalars, whole(), whole(pltpu.HBM)],
        out_specs=blocks + [whole()] * 3,
        scratch_shapes=[
            pltpu.VMEM((2 * bands, waves), BF16),
            pltpu.VMEM((waves // 256 * 2 * bands, waves), BF16),
            pltpu.VMEM((waves // 256 * 2 * bands, 256), F32),
            pltpu.SemaphoreType.DMA,
        ],
        compiler_params=params(SORT_LIMIT),
        name="sort_waves",
    )(me_row, box_index.reshape(1, waves), coeffs)
    moved = exchange(ordered, pairs)

    routed = pool_count == 8
    half_rows = jax.ShapeDtypeStruct((bands, waves), BF16)
    pool_row = lax.axis_index("pool").reshape(1)
    if routed:
        swaps = {m: [(i, i ^ m) for i in range(pool_count)] for m in (1, 2, 4)}
        xn = lax.ppermute(own_re, "pool", swaps[2])
        yn = lax.ppermute(own_im, "pool", swaps[4])
        stacked = pl.pallas_call(
            stack_kernel,
            out_shape=jax.ShapeDtypeStruct((4 * bands, waves), BF16),
            in_specs=[whole()] * 4,
            out_specs=whole(),
            compiler_params=params(),
            name="stack",
        )(own_re, own_im, xn, yn)
        other = lax.ppermute(stacked, "pool", swaps[1])
        near = [own_re, own_im, xn, yn, other]
    else:
        spread = lax.all_to_all(
            jnp.concatenate([own_re, own_im]).reshape(pool_count, 2 * bands // pool_count, waves),
            "pool", 0, 0, tiled=True,
        )
        near = []

    field = pl.pallas_call(
        functools.partial(field_kernel, side, chunks),
        out_shape=jax.ShapeDtypeStruct((4, side, chunks * LANES), BF16),
        in_specs=[whole()],
        out_specs=whole(),
        compiler_params=params(),
        cost_estimate=pl.CostEstimate(flops=10**9, bytes_accessed=10**6, transcendentals=0),
        name="field_pairs",
    )(potential.reshape(side * side, 2 * side))

    mark = pl.pallas_call(
        mark_kernel,
        out_shape=jax.ShapeDtypeStruct((8, LANES), F32),
        in_specs=[whole(pl.ANY)] * (fft_count - 1),
        out_specs=whole(),
        compiler_params=params(),
        cost_estimate=pl.CostEstimate(flops=MARK_COST, bytes_accessed=10**4, transcendentals=0),
        name="mark",
    )(*moved[:0:-1])
    gates = [mark, xn, yn] if routed else [mark]
    team = min(8, rows // 2)
    scratch = [
        pltpu.VMEM((2, fft_count, rows, waves), F32),
        pltpu.VMEM((columns // LANES, rows * side, LANES), F32),
        pltpu.VMEM((rows * side, columns), BF16),
        pltpu.VMEM((team * 2 * side, 2 * chunks * LANES), BF16),
        pltpu.VMEM((2, fft_count, rows, waves), F32),
    ]
    cost = pl.CostEstimate(flops=BOX_COST, bytes_accessed=10**7, transcendentals=0)
    back = pl.pallas_call(
        functools.partial(box_kernel, side, chunks, team, waves, fft_count, len(gates)),
        out_shape=[jax.ShapeDtypeStruct((rows, waves), BF16)] * fft_count,
        in_specs=blocks + [whole()] * 3 + [whole(pl.ANY)] * len(gates),
        out_specs=blocks,
        scratch_shapes=scratch
        + [
            pltpu.VMEM((columns, 2 * chunks * LANES), BF16),
            pltpu.VMEM((fft_count, side, 2 * STICK_DEV), F32),
            pltpu.VMEM((2, fft_count, tiles, LANES), jnp.int32),
            pltpu.VMEM((fft_count, LANES), jnp.int32),
            pltpu.VMEM((side, chunks * LANES), BF16),
            pltpu.VMEM((side, chunks * LANES), BF16),
            pltpu.SMEM((fft_count, LANES), jnp.int32),
            pltpu.SemaphoreType.DMA,
        ],
        compiler_params=params(),
        cost_estimate=cost,
        name="box_work",
    )(*moved[::-1], field, cs, wz, *gates)
    returned = exchange(back, pairs)

    if not routed:
        chosen = pl.pallas_call(
            select_kernel,
            out_shape=jax.ShapeDtypeStruct(spread.shape, BF16),
            in_specs=[scalars, whole(pl.ANY)],
            out_specs=whole(pl.ANY),
            scratch_shapes=[pltpu.SemaphoreType.DMA((pool_count,))],
            compiler_params=params(),
            name="select_partner",
        )(partner_pool, spread)
        partner = lax.all_to_all(chosen, "pool", 0, 0, tiled=True).reshape(2 * bands, waves)
    else:
        far_re, far_im = pl.pallas_call(
            route_kernel,
            out_shape=(half_rows, half_rows),
            in_specs=[scalars] * 2 + [whole()] * len(near),
            out_specs=(whole(), whole()),
            compiler_params=params(),
            name="route_partner",
        )(partner_pool, pool_row, *near)
        far_re = lax.ppermute(far_re, "pool", swaps[4])
        far_im = lax.ppermute(far_im, "pool", swaps[2])

    sorted_response = pl.pallas_call(
        functools.partial(join_kernel, fft_count),
        out_shape=jax.ShapeDtypeStruct((2 * bands, waves), BF16),
        in_specs=[scalars] + blocks,
        out_specs=whole(),
        compiler_params=params(),
        cost_estimate=pl.CostEstimate(flops=JOIN_COST, bytes_accessed=10**6, transcendentals=0),
        name="join",
    )(me_row, *returned[::-1])
    sums_shape = jax.ShapeDtypeStruct((2, bands, bands), BF16)
    if routed:
        sums = pl.pallas_call(
            couple_routed_kernel,
            out_shape=sums_shape,
            in_specs=[scalars] * 2 + [whole()] * (len(near) + 3),
            out_specs=whole(),
            scratch_shapes=[pltpu.VMEM((2 * bands, waves), BF16)],
            compiler_params=params(),
            name="couple",
        )(partner_pool, pool_row, *near, far_re, far_im, sorted_response)
    else:
        sums = pl.pallas_call(
            couple_kernel,
            out_shape=sums_shape,
            in_specs=[whole(), whole()],
            out_specs=whole(),
            compiler_params=params(),
            name="couple",
        )(partner, sorted_response)
    shares = [sums] + [lax.ppermute(sums, "fft", pairs[s]) for s in range(1, fft_count)]
    response = pl.pallas_call(
        unsort_kernel,
        out_shape=jax.ShapeDtypeStruct((2 * bands, waves), BF16),
        in_specs=[whole(), whole()],
        out_specs=whole(),
        compiler_params=params(),
        cost_estimate=pl.CostEstimate(flops=10**9, bytes_accessed=10**7, transcendentals=0),
        name="unsort",
    )(sorted_response, rank)
    summed = None
    for d in range(fft_count):
        offset = me ^ d
        term = shares[0]
        for s in range(1, fft_count):
            term = jnp.where(offset == s, shares[s], term)
        term = term.astype(F32)
        summed = term if summed is None else summed + term
    coupling = (summed / jnp.sqrt(jnp.float32(waves * fft_count)))[:, None]
    return response.reshape(2, 1, bands, waves), coupling


def solution(mesh):
    placed = (P(None, "pool", None, "fft"), P("fft"), P(), P())
    return jax.shard_map(
        shards,
        mesh=mesh,
        in_specs=placed,
        out_specs=(P(None, "pool", None, "fft"), P(None, "pool", None, None)),
        check_vma=False,
    )
```

```python
import functools

import jax
import jax.numpy as jnp
import ml_dtypes
import numpy as np
from jax import lax
from jax.experimental import pallas as pl
from jax.experimental.pallas import tpu as pltpu
from jax.sharding import PartitionSpec as P

STICK_DEV = 64
LANES = 128
UNROLL = 32
BF16 = jnp.bfloat16
F32 = jnp.float32
VMEM_LIMIT = 24 * 1024 * 1024
SMALL_LIMIT = 8 * 1024 * 1024
SORT_LIMIT = 24 * 1024 * 1024
JOIN_COST = 10**11
RANK_COST = 5 * 10**9
MARK_COST = 3*10**9
BOX_COST = 10**10


def cos_sin(side):
    points = np.arange(side)
    angles = (2.0 * np.pi / side) * (points[:, None] * points[None, :] % side)
    scaling = 1.0 / np.sqrt(side)
    cosine = (np.cos(angles) * scaling).astype(ml_dtypes.bfloat16)
    sine = (np.sin(angles) * scaling).astype(ml_dtypes.bfloat16)
    return cosine, sine


def dot(a, b):
    return jnp.dot(a, b, preferred_element_type=F32)


def dot_nt(a, b):
    return lax.dot_general(a, b, (((1,), (1,)), ((), ())), preferred_element_type=F32)


def one_hot(row, count):
    places = lax.broadcasted_iota(jnp.int32, (count, row.shape[1]), 0)
    return jnp.where(places == row, 1.0, 0.0).astype(BF16)


def triangles(side):
    rows = lax.broadcasted_iota(jnp.int32, (side, side), 0)
    cols = lax.broadcasted_iota(jnp.int32, (side, side), 1)
    upper = jnp.where(rows < cols, 1.0, 0.0).astype(BF16)
    lower = jnp.where(rows > cols, 1.0, 0.0).astype(BF16)
    return upper, lower, jnp.ones((side, side), BF16)


def prefix(occupied, tri):
    upper, lower, ones = tri
    in_rows = dot(occupied, ones).astype(BF16)
    return dot(occupied, upper) + dot(lower, in_rows)


def locate(idx, side):
    bits = side.bit_length() - 1
    tri = triangles(side)
    xh = one_hot(idx >> (2 * bits), side)
    yh = one_hot((idx >> bits) & (side - 1), side)
    zh = one_hot(idx & (side - 1), side)
    columns = jnp.minimum(dot_nt(xh, yh), 1.0).astype(BF16)
    slots = prefix(columns, tri).astype(BF16)
    slot = jnp.sum(xh.astype(F32) * dot(slots, yh), axis=0, keepdims=True)
    ch = one_hot(slot.astype(jnp.int32), STICK_DEV)
    cells = dot_nt(zh, ch)
    ranks = prefix(cells.astype(BF16), tri)
    high = jnp.floor(ranks * (1.0 / side))
    low = ranks - high * side
    looked = dot(high.astype(BF16), ch) * side + dot(low.astype(BF16), ch)
    rank = jnp.sum(zh.astype(F32) * looked, axis=0, keepdims=True)
    return xh, yh, ch, slot, cells, rank.astype(jnp.int32)


def rank_kernel(side, idx_ref, rank_ref, extra_ref):
    xh, yh, ch, slot_of, cells, rank = locate(idx_ref[...], side)
    rank_ref[...] = rank
    waves = rank.shape[1]
    rows = extra_ref.shape[0]
    cells = jnp.concatenate([cells[i : i + rows] for i in range(0, side, rows)], axis=1)
    tiles = waves // LANES
    in_tile = one_hot(rank & (LANES - 1), LANES)
    col = dot_nt(one_hot(rank >> 7, tiles) * slot_of.astype(BF16), in_tile)
    steps = lax.broadcasted_iota(jnp.int32, (8, side), 1).astype(F32).astype(BF16)
    place = [dot_nt(steps, jnp.minimum(dot_nt(ch, hot), 1.0).astype(BF16)) for hot in (xh, yh)]
    lines = [col, jnp.concatenate(place, axis=1)]
    spare = -(tiles + 8) % rows
    if spare:
        lines.append(jnp.zeros((spare, LANES), F32))
    lines = jnp.concatenate(lines, axis=0)
    lines = [lines[i : i + rows] for i in range(0, lines.shape[0], rows)]
    extra_ref[...] = jnp.concatenate([cells] + lines, axis=1).astype(BF16)


def sort_kernel(side, groups, me_ref, rank_ref, extra_ref, x_ref, *refs):
    outs, (re_ref, im_ref, wide, pieces) = refs[:groups], refs[groups:]
    rank = rank_ref[...]
    waves = rank.shape[1]
    both = x_ref.shape[0]
    bands = both // 2
    share = bands // groups
    low = one_hot(rank & 255, 256)
    for out in outs:
        out[:, waves:] = extra_ref[...]
    parts = waves // 256
    step = 2 if parts % 2 == 0 else 1
    for first in range(0, parts, step):
        for part in range(first, first + step):
            mask = jnp.where((rank >> 8) == part, 1.0, 0.0).astype(BF16)
            wide[part * both : (part + 1) * both] = x_ref[...] * mask
        rows_now = slice(first * both, (first + step) * both)
        pieces[rows_now] = dot_nt(wide[rows_now], low)
        for part in range(first, first + step):
            here = slice(part * 256, (part + 1) * 256)
            re_ref[:, here] = pieces[part * both : part * both + bands].astype(BF16)
            im_ref[:, here] = pieces[part * both + bands : (part + 1) * both].astype(BF16)
            for shift in range(groups):
                begin = pl.multiple_of(part * both + (me_ref[0] ^ shift) * share, 8)
                re = pieces[pl.ds(begin, share)]
                im = pieces[pl.ds(begin + bands, share)]
                outs[shift][:, here] = jnp.concatenate([re, im], axis=0).astype(BF16)


def field_kernel(side, chunks, pot_ref, cs_ref, wz_ref, field_ref, cs_out, wz_out):
    cs_out[...] = cs_ref[...]
    wz_out[...] = wz_ref[...]
    half = side // 2
    lane = lax.broadcasted_iota(jnp.int32, (side, LANES), 1)
    first = lane < side
    flipped = (lane & side) + ((side - (lane & (side - 1))) & (side - 1))

    def pair(row_a, row_b):
        p = jnp.where(first, row_a, pltpu.roll(row_b, side, 1))
        q = jnp.where(first, pltpu.roll(row_a, side, 1), row_b)
        return p, q

    def plane(y):
        return pot_ref[pl.ds(y, side, stride=side), :]

    def mirror(y):
        if y == 0 or y >= half:
            return jnp.zeros((side, LANES), F32)
        return jnp.take_along_axis(plane(side - y), flipped, axis=1)

    zero = jnp.zeros((side, LANES), F32)
    for k in range(chunks):
        ya, yb = 2 * k, 2 * k + 1
        here = slice(k * LANES, (k + 1) * LANES)
        values = pair(plane(ya), plane(yb) if yb <= half else zero) + pair(mirror(ya), mirror(yb))
        for i, value in enumerate(values):
            field_ref[i, :, here] = value.astype(BF16)


def select_kernel(order_ref, in_ref, out_ref, sems):
    copies = []
    for i in range(out_ref.shape[0]):
        copy = pltpu.make_async_copy(in_ref.at[order_ref[i]], out_ref.at[i], sems.at[i])
        copy.start()
        copies.append(copy)
    for copy in copies:
        copy.wait()


def mark_kernel(*refs):
    refs[-1][...] = jnp.zeros(refs[-1].shape, F32)


def choose(code, mask, sources, out_ref):
    for name, source in sources.items():

        @pl.when((code & mask) == name)
        def _(source=source):
            out_ref[...] = source[...]


def stack_kernel(re_ref, im_ref, xn_ref, yn_ref, out_ref):
    half = re_ref.shape[0]
    for k, ref in enumerate((re_ref, im_ref, xn_ref, yn_ref)):
        out_ref[k * half : (k + 1) * half] = ref[...]


def seen(own_re, own_im, xn, yn, other):
    half = own_re.shape[0]
    sib_re, sib_im, xns, yns = [other.at[k * half : (k + 1) * half] for k in range(4)]
    return {0: own_re, 1: sib_re, 2: xn, 3: xns}, {0: own_im, 1: sib_im, 4: yn, 5: yns}


def route_kernel(order_ref, i_ref, own_re, own_im, xn, yn, other, re_ref, im_ref):
    i = i_ref[0]
    near_re, near_im = seen(own_re, own_im, xn, yn, other)
    choose(order_ref[i ^ 4] ^ i, 3, near_re, re_ref)
    choose(order_ref[i ^ 2] ^ i, 5, near_im, im_ref)


def couple_routed_kernel(groups, me_ref, order_ref, i_ref, *refs):
    y_refs, refs = refs[:groups], refs[groups:]
    own_re, own_im, xn, yn, other, far_re, far_im, _, sorted_ref, g_ref, partner = refs
    join_kernel(groups, me_ref, *y_refs, sorted_ref)
    half = own_re.shape[0]
    code = order_ref[i_ref[0]] ^ i_ref[0]
    near_re, near_im = seen(own_re, own_im, xn, yn, other)
    re_ref, im_ref = partner.at[:half], partner.at[half:]
    choose(code, 7, near_re, re_ref)
    choose(code, 4, {4: far_re}, re_ref)
    choose(code, 7, near_im, im_ref)
    choose(code, 2, {2: far_im}, im_ref)
    couple_kernel(partner, sorted_ref, g_ref)


def build_tables(side, chunks, waves, x_refs, cs_ref, tab_ref, spot_ref, col_ref, start_ref, cyr_ref, syr_ref):
    rows = x_refs[0].shape[0]
    parts = side // rows
    tiles = waves // LANES
    cells_end = waves + parts * STICK_DEV
    tri = triangles(side)
    ahead = jnp.where(
        lax.broadcasted_iota(jnp.int32, (side, LANES), 0)
        < lax.broadcasted_iota(jnp.int32, (side, LANES), 1),
        1.0, 0.0,
    ).astype(BF16)
    left = lax.broadcasted_iota(jnp.int32, (tiles, LANES), 1) < STICK_DEV
    first = lax.broadcasted_iota(jnp.int32, (side, LANES), 1) < side
    for ref, begin in ((cyr_ref, 0), (syr_ref, LANES)):
        table = cs_ref[:, begin : begin + side].astype(F32)
        for k in range(chunks):
            ya, yb = (2 * k) % side, (2 * k + 1) % side
            ref[:, k * LANES : (k + 1) * LANES] = jnp.where(
                first, table[:, ya : ya + 1], table[:, yb : yb + 1]
            ).astype(BF16)
    at_x, at_y = [], []
    for d, x_ref in enumerate(x_refs):
        cells = jnp.concatenate(
            [x_ref[:, waves + i * STICK_DEV : waves + (i + 1) * STICK_DEV].astype(F32) for i in range(parts)],
            axis=0,
        )
        lines = jnp.concatenate(
            [
                x_ref[:, i : i + LANES].astype(F32)
                for i in range(cells_end, cells_end + -(-(tiles + 8) // rows) * LANES, LANES)
            ],
            axis=0,
        )
        place = lines[tiles : tiles + 1].astype(jnp.int32)
        at_x.append(one_hot(place[:, :side], side).astype(F32).T)
        at_y.append(one_hot(place[:, side:], side).astype(F32).T)
        ranks = prefix(cells.astype(BF16), tri)
        begins = jnp.minimum(jnp.floor(ranks[:, :1] * (1.0 / STICK_DEV)), waves // STICK_DEV - 1.0)
        spot = jnp.where(cells > 0.5, ranks - begins * STICK_DEV, -1.0)
        spot_ref[d] = jnp.concatenate([spot, spot], axis=1)
        level = dot_nt(jnp.ones((8, STICK_DEV), BF16), cells.astype(BF16))
        start_ref[d : d + 1, :] = dot(level.astype(BF16), ahead)[:1].astype(jnp.int32)
        col = lines[:tiles] + float((d % 2) * STICK_DEV)
        turned = pltpu.roll(col, STICK_DEV, 1)
        after = jnp.concatenate([turned[1:], turned[:1]], axis=0)
        col_ref[0, d] = col.astype(jnp.int32)
        col_ref[1, d] = jnp.where(left, turned, after).astype(jnp.int32)
    at_x = jnp.concatenate(at_x, axis=0).astype(BF16)
    at_y = jnp.concatenate(at_y, axis=0).astype(BF16)
    both = dot(at_x, cs_ref[...])
    cx, sx = both[:, :LANES], both[:, LANES:]
    for k in range(chunks):
        cy = dot(at_y, cyr_ref[:, k * LANES : (k + 1) * LANES])
        sy = dot(at_y, syr_ref[:, k * LANES : (k + 1) * LANES])
        base = 2 * k * LANES
        tab_ref[:, base : base + LANES] = (cy * cx - sy * sx).astype(BF16)
        tab_ref[:, base + LANES : base + 2 * LANES] = (cy * sx + sy * cx).astype(BF16)


def box_kernel(side, chunks, team, waves, groups, gates, *refs):
    x_refs, refs = refs[:groups][::-1], refs[groups:]
    (field_ref, cs_ref, wz_ref), refs = refs[:3], refs[3 + gates :]
    out_refs, refs = refs[:groups], refs[groups:]
    *scratch, tab_ref, spot_ref, col_ref, start_ref, cyr_ref, syr_ref, start_s, sem = refs
    build_tables(
        side, chunks, waves, x_refs, cs_ref, tab_ref, spot_ref, col_ref, start_ref, cyr_ref, syr_ref
    )
    to_scalars = pltpu.make_async_copy(start_ref, start_s, sem)
    to_scalars.start()
    to_scalars.wait()
    box_work(
        side, chunks, team, waves, x_refs, field_ref, wz_ref, tab_ref, spot_ref, col_ref, start_s,
        out_refs, *scratch,
    )


def box_work(
    side, chunks, team, waves, x_refs, field_ref, wz_ref, tab_ref, spot_ref, col_ref, start_s,
    out_refs, xf, grid, t_scr, l_scr, acc,
):
    groups = len(x_refs)
    rows = x_refs[0].shape[0]
    bands = rows // 2
    blocks = rows // 8
    span = 2 * side
    for d in range(groups):
        value = x_refs[d][:, :waves].astype(F32)
        xf[0, d] = value
        xf[1, d] = jnp.concatenate([value[:, STICK_DEV:], value[:, :STICK_DEV]], axis=1)
        acc[0, d] = jnp.zeros((rows, waves), F32)
        acc[1, d] = jnp.zeros((rows, waves), F32)
    lane = lax.broadcasted_iota(jnp.int32, (8, LANES), 1)
    left = lane < STICK_DEV

    def window(z, d):
        begin = jnp.minimum(start_s[d, z] >> 6, waves // STICK_DEV - 1)
        tile = begin >> 1
        return begin & 1, tile, pl.ds(pl.multiple_of(tile * LANES, LANES), LANES), begin * STICK_DEV

    def expand(z):
        for dp in range(groups // 2):
            spot = jnp.where(
                left,
                jnp.broadcast_to(spot_ref[2 * dp, pl.ds(z, 1), :], (8, LANES)),
                jnp.broadcast_to(spot_ref[2 * dp + 1, pl.ds(z, 1), :], (8, LANES)),
            )
            valid = spot >= 0.0
            at = jnp.maximum(spot, 0.0).astype(jnp.int32)
            odd_a, _, lanes_a, _ = window(z, 2 * dp)
            odd_b, _, lanes_b, _ = window(z, 2 * dp + 1)
            for block in range(blocks):
                part = slice(block * 8, (block + 1) * 8)
                a = jnp.take_along_axis(xf[odd_a, 2 * dp, part, lanes_a], at, axis=1)
                b = jnp.take_along_axis(xf[odd_b, 2 * dp + 1, part, lanes_b], at, axis=1)
                value = jnp.where(valid, jnp.where(left, a, b), 0.0)
                grid[dp, pl.ds(block * 8 * side + z, 8, stride=side), :] = value

    def collect(z):
        for dp in range(groups // 2):
            sources = [
                grid[dp, pl.ds(block * 8 * side + z, 8, stride=side), :] for block in range(blocks)
            ]
            for d in (2 * dp, 2 * dp + 1):
                odd, tile, lanes, base = window(z, d)
                at = jnp.broadcast_to(col_ref[odd, d, pl.ds(tile, 1), :], (8, LANES))
                mask = (lane >= start_s[d, z] - base) & (lane < start_s[d, z + 1] - base)
                for block in range(blocks):
                    part = slice(block * 8, (block + 1) * 8)
                    value = jnp.take_along_axis(sources[block], at, axis=1)
                    acc[odd, d, part, lanes] = jnp.where(mask, value, acc[odd, d, part, lanes])

    def levels(step):
        def body(i, carry):
            for j in range(UNROLL):
                step(i * UNROLL + j)
            return carry

        lax.fori_loop(0, side // UNROLL, body, 0)

    levels(expand)

    def depth_in(g, carry):
        for b in [g * team + i for i in range(team)]:
            both = jnp.concatenate(
                [
                    jnp.concatenate(
                        [
                            grid[n, pl.ds(b * side, side), :].astype(BF16),
                            grid[n, pl.ds((bands + b) * side, side), :].astype(BF16),
                        ],
                        axis=0,
                    )
                    for n in range(groups // 2)
                ],
                axis=1,
            )
            t_scr[pl.ds(b * span, span), :] = dot(wz_ref[0], both).astype(BF16)
        return carry

    lax.fori_loop(0, bands // team, depth_in, 0)

    def planes(g, carry):
        rows_g = pl.ds(g * team * span, team * span)
        sticks = t_scr[rows_g, :]
        for k in range(chunks):
            here = slice(k * LANES, (k + 1) * LANES)
            wide = slice(2 * k * LANES, 2 * (k + 1) * LANES)
            ab = dot(sticks, tab_ref[:, wide])
            p, q = field_ref[0, :, here], field_ref[1, :, here]
            p2, q2 = field_ref[2, :, here], field_ref[3, :, here]
            for b in range(team):
                u, x = ab[b * span : b * span + side, :LANES], ab[b * span : b * span + side, LANES:]
                w, v = ab[b * span + side : (b + 1) * span, :LANES], ab[b * span + side : (b + 1) * span, LANES:]
                pr, pi, mr, mi = [t.astype(BF16) for t in (u - v, w + x, u + v, w - x)]
                ar, ai = p * pr - q * pi, p * pi + q * pr
                br, bi = p2 * mr - q2 * mi, p2 * mi + q2 * mr
                even = jnp.concatenate([ar + br, ai + bi], axis=0)
                odd = jnp.concatenate([ai - bi, br - ar], axis=0)
                l_scr[b * span : (b + 1) * span, wide] = jnp.concatenate([even, odd], axis=1)
        back = dot_nt(l_scr[...], tab_ref[...]).astype(BF16)
        for b in range(team):
            done = dot(wz_ref[1], back[b * span : (b + 1) * span])
            for n in range(groups // 2):
                here = slice(n * LANES, (n + 1) * LANES)
                grid[n, pl.ds((g * team + b) * side, side), :] = done[:side, here]
                grid[n, pl.ds((bands + g * team + b) * side, side), :] = done[side:, here]
        return carry

    lax.fori_loop(0, bands // team, planes, 0)

    levels(collect)
    for d in range(groups):
        late = acc[1, d]
        late = jnp.concatenate([late[:, waves - STICK_DEV :], late[:, : waves - STICK_DEV]], axis=1)
        out_refs[d][...] = (acc[0, d] + late).astype(BF16)


def join_kernel(groups, me_ref, *refs):
    y_refs, (sorted_ref,) = refs[:groups][::-1], refs[groups:]
    part = y_refs[0].shape[0] // 2
    half = groups * part
    me = me_ref[0]
    even = (me & 1) == 0
    for j in range(groups // 2):
        one, other = y_refs[2 * j][...].astype(F32), y_refs[2 * j + 1][...].astype(F32)
        low = jnp.where(even, one, other)
        high = jnp.where(even, other, one)
        begin = pl.multiple_of(((me >> 1) ^ j) * (2 * part), 16)
        sorted_ref[pl.ds(begin, 2 * part)] = jnp.concatenate(
            [low[:part], high[:part]], axis=0
        ).astype(BF16)
        sorted_ref[pl.ds(begin + half, 2 * part)] = jnp.concatenate(
            [low[part:], high[part:]], axis=0
        ).astype(BF16)


def couple_kernel(partner_ref, sorted_ref, g_ref):
    products = dot_nt(partner_ref[...], sorted_ref[...])
    half = products.shape[0] // 2
    g_ref[0] = (products[:half, :half] + products[half:, half:]).astype(BF16)
    g_ref[1] = (products[:half, half:] - products[half:, :half]).astype(BF16)


def unsort_kernel(y_ref, rank_ref, out_ref):
    both, waves = y_ref.shape
    parts = waves // 256
    stacked = jnp.concatenate([y_ref[:, i * 256 : (i + 1) * 256] for i in range(parts)], axis=0)
    for tile in range(parts):
        here = slice(tile * 256, (tile + 1) * 256)
        rank = rank_ref[:, here]
        values = dot(stacked, one_hot(rank & 255, 256))
        total = None
        for part in range(parts):
            value = jnp.where((rank >> 8) == part, values[part * both : (part + 1) * both], 0.0)
            total = value if total is None else total + value
        out_ref[:, here] = total.astype(BF16)


def exchange(blocks, pairs):
    moved = list(blocks)
    for s in range(len(blocks) - 1, 0, -1):
        moved[s] = lax.ppermute(blocks[s], "fft", pairs[s])
    return moved


def whole(memory=pltpu.VMEM):
    return pl.BlockSpec(memory_space=memory)


def params(limit=VMEM_LIMIT):
    return pltpu.CompilerParams(vmem_limit_bytes=limit)


def shards(orbitals, box_index, partner_pool, potential):
    fft_count = lax.axis_size("fft")
    side = potential.shape[0]
    bands = orbitals.shape[2]
    waves = orbitals.shape[3]
    share = bands // fft_count
    columns = STICK_DEV * fft_count
    chunks = (side // 2 + 1 + 1) // 2
    coeffs = orbitals.reshape(2 * bands, waves)

    cosine, sine = cos_sin(side)
    cs = jnp.asarray(np.concatenate([cosine, cosine, sine, sine], axis=1))
    inward = np.block([[cosine, -sine], [sine, cosine]])
    outward = np.block([[cosine, sine], [-sine, cosine]])
    wz = jnp.asarray(np.stack([inward, outward]))

    me = lax.axis_index("fft")
    me_row = me.reshape(1)
    pairs = [[(i, i ^ s) for i in range(fft_count)] for s in range(fft_count)]
    pool_count = lax.axis_size("pool")
    rows = 2 * share
    tiles = waves // LANES
    packed = waves + side * STICK_DEV // rows + -(-(tiles + 8) // rows) * LANES
    scalars, blocks = whole(pltpu.SMEM), [whole()] * fft_count

    rank, extra = pl.pallas_call(
        functools.partial(rank_kernel, side),
        out_shape=(
            jax.ShapeDtypeStruct((1, waves), jnp.int32),
            jax.ShapeDtypeStruct((rows, packed - waves), BF16),
        ),
        in_specs=[whole()],
        out_specs=(whole(), whole()),
        compiler_params=params(SORT_LIMIT),
        cost_estimate=pl.CostEstimate(flops=RANK_COST, bytes_accessed=10**4, transcendentals=0),
        name="rank_waves",
    )(box_index.reshape(1, waves))
    *ordered, own_re, own_im = pl.pallas_call(
        functools.partial(sort_kernel, side, fft_count),
        out_shape=[jax.ShapeDtypeStruct((rows, packed), BF16)] * fft_count
        + [jax.ShapeDtypeStruct((bands, waves), BF16)] * 2,
        in_specs=[scalars, whole(), whole(), whole()],
        out_specs=blocks + [whole()] * 2,
        scratch_shapes=[
            pltpu.VMEM((waves // 256 * 2 * bands, waves), BF16),
            pltpu.VMEM((waves // 256 * 2 * bands, 256), F32),
        ],
        compiler_params=params(SORT_LIMIT),
        name="sort_waves",
    )(me_row, rank, extra, coeffs)
    moved = exchange(ordered, pairs)

    routed = pool_count == 8
    half_rows = jax.ShapeDtypeStruct((bands, waves), BF16)
    pool_row = lax.axis_index("pool").reshape(1)
    if routed:
        swaps = {m: [(i, i ^ m) for i in range(pool_count)] for m in (1, 2, 4)}
        xn = lax.ppermute(own_re, "pool", swaps[2])
        yn = lax.ppermute(own_im, "pool", swaps[4])
        stacked = pl.pallas_call(
            stack_kernel,
            out_shape=jax.ShapeDtypeStruct((4 * bands, waves), BF16),
            in_specs=[whole()] * 4,
            out_specs=whole(),
            compiler_params=params(SMALL_LIMIT),
            name="stack",
        )(own_re, own_im, xn, yn)
        other = lax.ppermute(stacked, "pool", swaps[1])
        near = [own_re, own_im, xn, yn, other]
    else:
        spread = lax.all_to_all(
            jnp.concatenate([own_re, own_im]).reshape(pool_count, 2 * bands // pool_count, waves),
            "pool", 0, 0, tiled=True,
        )
        near = []

    field, cs, wz = pl.pallas_call(
        functools.partial(field_kernel, side, chunks),
        out_shape=(
            jax.ShapeDtypeStruct((4, side, chunks * LANES), BF16),
            jax.ShapeDtypeStruct(cs.shape, BF16),
            jax.ShapeDtypeStruct(wz.shape, BF16),
        ),
        in_specs=[whole()] * 3,
        out_specs=(whole(),) * 3,
        compiler_params=params(),
        cost_estimate=pl.CostEstimate(flops=10**9, bytes_accessed=10**6, transcendentals=0),
        name="field_pairs",
    )(potential.reshape(side * side, 2 * side), cs, wz)

    mark = pl.pallas_call(
        mark_kernel,
        out_shape=jax.ShapeDtypeStruct((8, LANES), F32),
        in_specs=[whole(pl.ANY)] * (fft_count - 1),
        out_specs=whole(),
        compiler_params=params(SMALL_LIMIT),
        cost_estimate=pl.CostEstimate(flops=MARK_COST, bytes_accessed=10**4, transcendentals=0),
        name="mark",
    )(*moved[:0:-1])
    gates = [mark, xn, yn] if routed else [mark]
    team = min(8, rows // 2)
    scratch = [
        pltpu.VMEM((2, fft_count, rows, waves), F32),
        pltpu.VMEM((columns // LANES, rows * side, LANES), F32),
        pltpu.VMEM((rows * side, columns), BF16),
        pltpu.VMEM((team * 2 * side, 2 * chunks * LANES), BF16),
        pltpu.VMEM((2, fft_count, rows, waves), F32),
    ]
    cost = pl.CostEstimate(flops=BOX_COST, bytes_accessed=10**7, transcendentals=0)
    back = pl.pallas_call(
        functools.partial(box_kernel, side, chunks, team, waves, fft_count, len(gates)),
        out_shape=[jax.ShapeDtypeStruct((rows, waves), BF16)] * fft_count,
        in_specs=blocks + [whole()] * 3 + [whole(pl.ANY)] * len(gates),
        out_specs=blocks,
        scratch_shapes=scratch
        + [
            pltpu.VMEM((columns, 2 * chunks * LANES), BF16),
            pltpu.VMEM((fft_count, side, 2 * STICK_DEV), F32),
            pltpu.VMEM((2, fft_count, tiles, LANES), jnp.int32),
            pltpu.VMEM((fft_count, LANES), jnp.int32),
            pltpu.VMEM((side, chunks * LANES), BF16),
            pltpu.VMEM((side, chunks * LANES), BF16),
            pltpu.SMEM((fft_count, LANES), jnp.int32),
            pltpu.SemaphoreType.DMA,
        ],
        compiler_params=params(),
        cost_estimate=cost,
        name="box_work",
    )(*moved[::-1], field, cs, wz, *gates)
    returned = exchange(back, pairs)

    if not routed:
        chosen = pl.pallas_call(
            select_kernel,
            out_shape=jax.ShapeDtypeStruct(spread.shape, BF16),
            in_specs=[scalars, whole(pl.ANY)],
            out_specs=whole(pl.ANY),
            scratch_shapes=[pltpu.SemaphoreType.DMA((pool_count,))],
            compiler_params=params(),
            name="select_partner",
        )(partner_pool, spread)
        partner = lax.all_to_all(chosen, "pool", 0, 0, tiled=True).reshape(2 * bands, waves)
    else:
        far_re, far_im = pl.pallas_call(
            route_kernel,
            out_shape=(half_rows, half_rows),
            in_specs=[scalars] * 2 + [whole()] * len(near),
            out_specs=(whole(), whole()),
            compiler_params=params(SMALL_LIMIT),
            name="route_partner",
        )(partner_pool, pool_row, *near)
        far_re = lax.ppermute(far_re, "pool", swaps[4])
        far_im = lax.ppermute(far_im, "pool", swaps[2])

    sums_shape = jax.ShapeDtypeStruct((2, bands, bands), BF16)
    sorted_shape = jax.ShapeDtypeStruct((2 * bands, waves), BF16)
    blocks_home = [returned[s] for s in range(fft_count - 1, -1, -1)]
    if routed:
        home = pl.pallas_call(
            mark_kernel,
            out_shape=jax.ShapeDtypeStruct((8, LANES), F32),
            in_specs=[whole(pl.ANY)] * (fft_count - 1),
            out_specs=whole(),
            compiler_params=params(SMALL_LIMIT),
            cost_estimate=pl.CostEstimate(flops=JOIN_COST, bytes_accessed=10**4, transcendentals=0),
            name="mark_home",
        )(*blocks_home[:-1])
        sorted_response, sums = pl.pallas_call(
            functools.partial(couple_routed_kernel, fft_count),
            out_shape=(sorted_shape, sums_shape),
            in_specs=[scalars] * 3 + blocks + [whole()] * (len(near) + 2) + [whole(pl.ANY)],
            out_specs=(whole(), whole()),
            scratch_shapes=[pltpu.VMEM((2 * bands, waves), BF16)],
            compiler_params=params(SMALL_LIMIT),
            name="couple",
        )(me_row, partner_pool, pool_row, *blocks_home, *near, far_re, far_im, home)
    else:
        sorted_response = pl.pallas_call(
            functools.partial(join_kernel, fft_count),
            out_shape=sorted_shape,
            in_specs=[scalars] + blocks,
            out_specs=whole(),
            compiler_params=params(SMALL_LIMIT),
            name="join",
        )(me_row, *blocks_home)
        sums = pl.pallas_call(
            couple_kernel,
            out_shape=sums_shape,
            in_specs=[whole(), whole()],
            out_specs=whole(),
            compiler_params=params(SMALL_LIMIT),
            name="couple",
        )(partner, sorted_response)
    shares = [sums] + [lax.ppermute(sums, "fft", pairs[s]) for s in range(1, fft_count)]
    response = pl.pallas_call(
        unsort_kernel,
        out_shape=jax.ShapeDtypeStruct((2 * bands, waves), BF16),
        in_specs=[whole(), whole()],
        out_specs=whole(),
        compiler_params=params(),
        cost_estimate=pl.CostEstimate(flops=10**9, bytes_accessed=10**7, transcendentals=0),
        name="unsort",
    )(sorted_response, rank)
    summed = None
    for d in range(fft_count):
        offset = me ^ d
        term = shares[0]
        for s in range(1, fft_count):
            term = jnp.where(offset == s, shares[s], term)
        term = term.astype(F32)
        summed = term if summed is None else summed + term
    coupling = (summed / jnp.sqrt(jnp.float32(waves * fft_count)))[:, None]
    return response.reshape(2, 1, bands, waves), coupling


def solution(mesh):
    placed = (P(None, "pool", None, "fft"), P("fft"), P(), P())
    return jax.shard_map(
        shards,
        mesh=mesh,
        in_specs=placed,
        out_specs=(P(None, "pool", None, "fft"), P(None, "pool", None, None)),
        check_vma=False,
    )
```
